256 devices in a mesh: comp: 2 (over core), gx: 16 (over x, y), gy: 8 (over z).
Axes of the slice: x: 4, y: 4, z: 8, core: 2. Of those that a mesh axis runs over, the one named last changes fastest.
Arguments:
- state: float32 [2, 8, 384, 3072], P('comp', None, 'gx', 'gy'), may hold values from -6 to 6
- response: float32 [2, 8, 3072], P('comp'), may hold values from -0.95 to 0
- diffusion: float32 [2, 384, 3072], P('comp', 'gx', 'gy'), may hold values from 0.02 to 0.24
- land_mask: int32 [384, 3072], P('gx', 'gy'), may hold values 0 or 1
- couple_src: int32 [2, 16, 8, 128, 128], P('comp', 'gx', 'gy'), may hold values from 0 to 9215
- couple_dst: int32 [2, 16, 8, 128, 128], P('comp', 'gx', 'gy'), may hold values from 0 to 9215
- couple_weight: float32 [2, 16, 8, 128, 128], P('comp', 'gx', 'gy'), may hold values from 0.1 to 1
- couple_count: int32 [2, 16, 8, 128], P('comp', 'gx', 'gy'), may hold values from 0 to 128, as said below
Outputs:
- final_state: float32 [2, 8, 384, 3072], P('comp', None, 'gx', 'gy')
The draws below stay inside these ranges and needn't reach their ends.
Inputs may be any that keep to these rules, and one draw needn't show every extreme that they name: `couple_count`: at most 128 live slots per ordered device pair; every sending device has one pair with exactly 128.
All inputs are finite; a program needn't handle non-finite values. No bound on the sum of `land_mask` on one device may be relied on, other than what follows from the above.
Results may differ from the reference program's by a relative error of at most 0.0095.
Values may be sent and summed in bfloat16 or wider, within the bound.
No kernel may reach another device: no remote copies, remote signals or barrier semaphores. Data moves between devices by JAX's collectives and lax.ppermute only.
A program may use at most 128 MiB of HBM per device.

```python
import math
import jax
import jax.numpy as jnp
from jax import lax

LEV = 8
FC = 4
STEPS = 1
RD = 24
COLS = 3072
CAP = 128
CD = 384
ROWS = 384
NPEER = 128
N_GX = 16
N_GY = 8


def draw_couple_count(key, part):
    key_a = jax.random.fold_in(key, 11)
    key_b = jax.random.fold_in(key, 12)
    key_c = jax.random.fold_in(key, 13)
    first = jax.random.randint(key_a, (2, N_GX, N_GY, NPEER), 0, CAP + 1)
    second = jax.random.randint(key_b, (2, N_GX, N_GY, NPEER), 0, CAP + 1)
    counts = jnp.maximum(first, second)
    chosen = jax.random.randint(key_c, (2, N_GX, N_GY, 1), 0, NPEER)
    peers = jnp.arange(NPEER, dtype=jnp.int32)[None, None, None, :]
    return jnp.where(peers == chosen, CAP, counts).astype(jnp.int32)


def place_ends(drawn, own_key, smallest, largest):
    longest = drawn.shape.index(max(drawn.shape))
    spots = []
    for shift in (0, 1):
        where = [jax.random.randint(jax.random.fold_in(own_key, axis), (), 0, length) for axis, length in enumerate(drawn.shape)]
        where[longest] = (where[longest] + shift) % drawn.shape[longest]
        spots.append(tuple(where))
    return drawn.at[spots[0]].set(smallest).at[spots[1]].set(largest)


def levels(own_key, dims, cuts, low, largest):
    gain, own = 1.0, jax.random.fold_in(own_key, 6)
    for axis_at, blocks in cuts:
        heights = jnp.exp(jax.random.uniform(jax.random.fold_in(own, axis_at), (blocks,), jnp.float32, low / len(cuts), largest / len(cuts)))
        gain = gain * jnp.repeat(heights, dims[axis_at] // blocks).reshape([-1 if axis == axis_at else 1 for axis in range(len(dims))])
    return gain


def centred(rng, extent, width, limit, split=(), held_as=jnp.bfloat16):
    level = levels(rng, extent, split, -0.22, 0.18) if split else 1.0
    drawn = jax.random.normal(rng, extent, jnp.float32) * width * level
    return jnp.minimum(jnp.maximum(drawn, -limit), limit).astype(held_as)


def setup_inputs(seed: int = 0) -> dict:
    keys = jax.random.split(jax.random.key(seed), 9)
    return {
        "state": centred(keys[0], (2, LEV, ROWS, COLS), 1.0, 6.0, ((0, 2), (2, 16), (3, 8)), jnp.float32),
        "response": jnp.clip(-0.95 + 0.95 * jax.random.uniform(keys[1], (2, LEV, COLS), jnp.float32) ** levels(keys[1], (2, LEV, COLS), ((0, 2),), -0.2, 0.2), -0.95, 0.0),
        "diffusion": jnp.clip(jnp.exp(math.log(0.24) - 2.4849066 * jax.random.uniform(keys[2], (2, ROWS, COLS), jnp.float32) ** levels(keys[2], (2, ROWS, COLS), ((0, 2), (1, 16), (2, 8)), -0.2, 0.2)), 0.02, 0.24),
        "land_mask": place_ends((jax.random.randint(keys[3], (ROWS, COLS), 0, 4) < 3).astype(jnp.int32), jax.random.fold_in(keys[3], 1), 0, 1),
        "couple_src": place_ends(jax.random.randint(keys[4], (2, N_GX, N_GY, NPEER, CAP), 0, RD * CD), jax.random.fold_in(keys[4], 1), 0, (RD * CD) - 1).astype(jnp.int32),
        "couple_dst": place_ends(jax.random.randint(keys[5], (2, N_GX, N_GY, NPEER, CAP), 0, RD * CD), jax.random.fold_in(keys[5], 1), 0, (RD * CD) - 1).astype(jnp.int32),
        "couple_weight": jnp.clip(0.1 + 0.9 * jax.random.uniform(keys[6], (2, N_GX, N_GY, NPEER, CAP), jnp.float32) ** levels(keys[6], (2, N_GX, N_GY, NPEER, CAP), ((0, 2), (1, 16), (2, 8)), -0.2, 0.2), 0.1, 1.0),
        "couple_count": draw_couple_count(jax.random.fold_in(keys[8], 71), 0),
    }


def make_table(cols):
    rows_idx = jnp.arange(cols, dtype=jnp.int32)[:, None]
    wave_idx = jnp.arange(cols // 2, dtype=jnp.int32)[None, :]
    phase = (rows_idx * wave_idx) % cols
    angle = phase.astype(jnp.float32) * (2.0 * math.pi / cols)
    return jnp.concatenate([jnp.cos(angle), jnp.sin(angle)], axis=1).astype(jnp.bfloat16)


def reference(state, response, diffusion, land_mask, couple_src, couple_dst, couple_weight, couple_count):
    cells = RD * CD
    table = make_table(COLS)
    slot_idx = jnp.arange(CAP, dtype=jnp.int32)
    live = slot_idx[None, None, None, None, :] < couple_count[..., None]
    weights = jnp.where(live, couple_weight, jnp.float32(0.0)).reshape(2, NPEER, NPEER, CAP)
    src_idx = couple_src.reshape(2, NPEER, NPEER * CAP)
    dst_idx = couple_dst.reshape(2, NPEER, NPEER * CAP)
    keep = jnp.stack([jnp.ones((ROWS, COLS), jnp.float32), land_mask.astype(jnp.float32)])
    lead = jnp.arange(2 * FC * NPEER, dtype=jnp.int32).reshape(2, FC, NPEER, 1)
    global_idx = (lead * cells + dst_idx[:, None, :, :]).reshape(-1)
    for step in range(STEPS):
        surface = state[:, :FC].reshape(2, FC, N_GX, RD, N_GY, CD)
        blocks = surface.transpose(0, 1, 2, 4, 3, 5).reshape(2, FC, NPEER, cells)
        values = jnp.take_along_axis(blocks, jnp.broadcast_to(src_idx[:, None], (2, FC, NPEER, NPEER * CAP)), axis=3)
        values = values.reshape(2, FC, NPEER, NPEER, CAP) * weights[:, None]
        arrived = values[::-1].transpose(0, 1, 3, 2, 4).reshape(-1)
        updated = blocks.reshape(-1).at[global_idx].add(arrived)
        updated = updated.reshape(2, FC, N_GX, N_GY, RD, CD).transpose(0, 1, 2, 4, 3, 5).reshape(2, FC, ROWS, COLS)
        state = jnp.concatenate([updated, state[:, FC:]], axis=1)
        grid_bf = state.astype(jnp.bfloat16).reshape(-1, COLS)
        spec = jnp.dot(grid_bf, table, preferred_element_type=jnp.float32).reshape(2, LEV, ROWS, COLS)
        filtered = (spec * response[:, :, None, :]).astype(jnp.bfloat16).reshape(-1, COLS)
        incr = lax.dot_general(filtered, table, (((1,), (1,)), ((), ())), preferred_element_type=jnp.float32)
        incr = (incr * (2.0 / COLS)).astype(jnp.bfloat16).reshape(2, LEV, ROWS, COLS)
        state = state + incr.astype(jnp.float32)
        padded = jnp.pad(state, ((0, 0), (0, 0), (1, 1), (0, 0)))
        state = state + diffusion[:, None] * (padded[:, :, 2:] + padded[:, :, :-2] - 2.0 * state)
        state = state * keep[:, None]
    return state
```

```python
import functools
import math

import jax
import jax.numpy as jnp
import numpy as np
from jax import lax
from jax.experimental import pallas as pl
from jax.experimental.pallas import tpu as pltpu
from jax.sharding import PartitionSpec as P

FC = 4
LANES = 128
BF = jnp.bfloat16
F32 = jnp.float32
VMEM = pl.BlockSpec(memory_space=pltpu.VMEM)
SMEM = pl.BlockSpec(memory_space=pltpu.SMEM)
PARAMS = pltpu.CompilerParams(vmem_limit_bytes=32 * 2**20)


def one_hot(rows, index):
    spot = lax.broadcasted_iota(jnp.int32, (rows, index.shape[1]), 0)
    return spot == index


def split_cell(idx, cols):
    row = (idx.astype(F32) * (1.0 / cols) + 0.5 / cols).astype(jnp.int32)
    return row, idx - row * cols


def gather_kernel(group, count_ref, surf_ref, src_ref, weight_ref, out_ref):
    _, _, rows, cols = surf_ref.shape
    peers, slots = src_ref.shape
    fc = out_ref.shape[1]
    surface = surf_ref[0, :fc].reshape(fc * rows, cols).astype(BF)
    lane = lax.broadcasted_iota(jnp.int32, (1, slots), 1)

    def step(g, carry):
        base = pl.multiple_of(g * group, group)
        row, col = split_cell(src_ref[pl.ds(base, group), :], cols)
        for i in range(0, group, 2):
            pick = jnp.concatenate([one_hot(cols, col[i : i + 1]), one_hot(cols, col[i + 1 : i + 2])], axis=1)
            lines = jnp.dot(surface, jnp.where(pick, 1.0, 0.0).astype(BF), preferred_element_type=F32)
            rowpick = jnp.concatenate([one_hot(rows, row[i : i + 1]), one_hot(rows, row[i + 1 : i + 2])], axis=1)
            value = jnp.sum(jnp.where(rowpick[None], lines.reshape(fc, rows, 2 * slots), 0.0), axis=1)
            for j in range(2):
                w = jnp.where(lane < count_ref[base + i + j], weight_ref[pl.ds(base + i + j, 1), :], 0.0)
                out_ref[base + i + j] = (value[:, j * slots : (j + 1) * slots] * w).astype(BF)
        return carry

    lax.fori_loop(0, peers // group, step, 0)


def scatter_kernel(group, state_ref, arrived_ref, dst_ref, surf_ref, grid_ref):
    _, levels, rows, cols = state_ref.shape
    peers, fc, slots = arrived_ref.shape
    surf_ref[...] = state_ref[0, :fc]

    def step(g, carry):
        base = pl.multiple_of(g * group, group)
        row, col = split_cell(dst_ref[pl.ds(base, group), :], cols)
        spread, pick = [], []
        for i in range(group):
            value = arrived_ref[base + i].astype(F32)
            rowpick = one_hot(rows, row[i : i + 1])
            spread.append(jnp.where(rowpick[None], value[:, None, :], 0.0).reshape(fc * rows, slots).astype(BF))
            pick.append(jnp.where(one_hot(cols, col[i : i + 1]), 1.0, 0.0).astype(BF))
        part = lax.dot_general(
            jnp.concatenate(spread, axis=1),
            jnp.concatenate(pick, axis=1),
            (((1,), (1,)), ((), ())),
            preferred_element_type=F32,
        )
        surf_ref[...] += part.reshape(fc, rows, cols)
        return carry

    lax.fori_loop(0, peers // group, step, 0)
    grid_ref[:fc] = surf_ref[...].astype(BF)
    grid_ref[fc:] = state_ref[0, fc:].astype(BF)


def zonal_tables(blocks, cols, waves):
    total = blocks * cols
    b = np.arange(cols)
    n = np.arange(total // 2 // blocks)
    angle = 2.0 * np.pi * ((b[:, None] * n[None, :]) % cols) / cols
    pad = ((0, 0), (0, waves - len(n)))
    cos, sin = np.pad(np.cos(angle), pad), np.pad(np.sin(angle), pad)
    ahead = np.concatenate([cos, sin], axis=1)
    back = np.concatenate([cos.T, sin.T], axis=1)
    turn = 2.0 * np.pi * np.arange(blocks)[:, None] * b[None, :] / total
    twiddle = np.stack([np.cos(turn), np.sin(turn)])
    return jnp.asarray(ahead, BF), jnp.asarray(back, BF), jnp.asarray(twiddle, F32)


def zonal_kernel(scale, x_ref, resp_ref, ahead_ref, back_ref, twiddle_ref, out_ref):
    blocks, rows, cols = x_ref.shape
    waves = ahead_ref.shape[1] // 2
    half = math.sqrt(0.5)
    x = [x_ref[h].astype(F32) for h in range(blocks)]
    a = [x[i] + x[i + 4] for i in range(4)]
    b = [x[i] - x[i + 4] for i in range(4)]
    b13, d13 = half * (b[1] + b[3]), half * (b[1] - b[3])
    a02, a13 = a[0] + a[2], a[1] + a[3]
    z1 = (b[0] + d13, -(b[2] + b13))
    z2 = (a[0] - a[2], a[3] - a[1])
    z3 = (b[0] - d13, b[2] - b13)
    z = [(a02 + a13, None), z1, z2, z3, (a02 - a13, None)]
    z += [(re, -im) for re, im in (z3, z2, z1)]
    real, imag = [], []
    for r in range(blocks):
        re, im = z[r]
        ct, st = twiddle_ref[0, r : r + 1, :], twiddle_ref[1, r : r + 1, :]
        if r == 0:
            real.append(re)
        elif im is None:
            real.append(re * ct)
            imag.append(-re * st)
        else:
            real.append(re * ct + im * st)
            imag.append(im * ct - re * st)
    spec = jnp.dot(jnp.concatenate(real + imag, axis=0).astype(BF), ahead_ref[...], preferred_element_type=F32)
    cosine, sine = [], []
    for r in range(blocks):
        own = spec[r * rows : (r + 1) * rows]
        c, s = own[:, :waves], own[:, waves:]
        if r > 0:
            other = spec[(blocks + r - 1) * rows : (blocks + r) * rows]
            c, s = c + other[:, waves:], s - other[:, :waves]
        cosine.append(c * resp_ref[0, r : r + 1, :])
        sine.append(s * resp_ref[1, r : r + 1, :])
    full = jnp.dot(jnp.concatenate(cosine + sine, axis=0).astype(BF), back_ref[...], preferred_element_type=F32)
    u = []
    for r in range(blocks):
        fc = full[r * rows : (r + 1) * rows]
        fs = full[(blocks + r) * rows : (blocks + r + 1) * rows]
        re, im = fc[:, :cols] + fs[:, cols:], fc[:, cols:] - fs[:, :cols]
        ct, st = twiddle_ref[0, r : r + 1, :], twiddle_ref[1, r : r + 1, :]
        u.append((re, None) if r == 0 else (re * ct - im * st, re * st + im * ct))
    even, odd = u[0][0] + u[4][0], u[0][0] - u[4][0]
    p1, q1 = u[1][0] + u[7][0], u[1][1] - u[7][1]
    p2, q2 = u[2][0] + u[6][0], u[2][1] - u[6][1]
    p3, q3 = u[3][0] + u[5][0], u[3][1] - u[5][1]
    m1, n1 = half * (p1 - q1), half * (p1 + q1)
    m3, n3 = half * (p3 - q3), half * (p3 + q3)
    incr = [
        even + p1 + p2 + p3,
        odd + m1 - q2 - n3,
        even - q1 - p2 + q3,
        odd - n1 + q2 + m3,
        even - p1 + p2 - p3,
        odd - m1 - q2 + n3,
        even + q1 - p2 - q3,
        odd + n1 + q2 - m3,
    ]
    for h in range(blocks):
        out_ref[h] = (incr[h] * scale).astype(BF)


def halo(top, bottom):
    count = lax.axis_size("gx")
    odd = lax.axis_index("gx") % 2 == 1
    first = [(i, i ^ 1) for i in range(count)]
    second = []
    for i in range(1, count - 1, 2):
        second += [(i, i + 1), (i + 1, i)]
    got_a = lax.ppermute(jnp.where(odd, top, bottom), "gx", first)
    got_b = lax.ppermute(jnp.where(odd, bottom, top), "gx", second)
    return jnp.where(odd, got_a, got_b), jnp.where(odd, got_b, got_a)


def local(
    state, response, diffusion, land_mask, couple_src, couple_dst, couple_weight, couple_count
):
    levels, rows_dev, cols_dev = (state.shape[1], state.shape[2], state.shape[3])
    groups_x = lax.axis_size("gx")
    groups_y = lax.axis_size("gy")
    peers = groups_x * groups_y
    slots = couple_src.shape[4]
    cols_all = cols_dev * groups_y
    section = lax.axis_index("comp")
    src_idx = couple_src.reshape(peers, slots)
    dst_idx = couple_dst.reshape(peers, slots)
    weight = couple_weight.reshape(peers, slots)
    count = couple_count.reshape(peers)

    outgoing = pl.pallas_call(
        functools.partial(gather_kernel, 8),
        out_shape=jax.ShapeDtypeStruct((peers, FC, slots), BF),
        in_specs=[SMEM, VMEM, VMEM, VMEM],
        out_specs=VMEM,
        compiler_params=PARAMS,
        name="couple_gather",
    )(count, state, src_idx, weight)
    crossed = lax.ppermute(outgoing, "comp", [(0, 1), (1, 0)])
    arrived = lax.all_to_all(crossed, ("gx", "gy"), split_axis=0, concat_axis=0, tiled=True)

    surface, grid_bf = pl.pallas_call(
        functools.partial(scatter_kernel, 8),
        out_shape=(
            jax.ShapeDtypeStruct((FC, rows_dev, cols_dev), F32),
            jax.ShapeDtypeStruct((levels, rows_dev, cols_dev), BF),
        ),
        in_specs=[VMEM, VMEM, VMEM],
        out_specs=(VMEM, VMEM),
        compiler_params=PARAMS,
        name="couple_scatter",
    )(state, arrived, dst_idx)

    circles = lax.all_to_all(grid_bf, "gy", split_axis=0, concat_axis=0, tiled=True)
    waves = 256
    ahead, back, twiddle = zonal_tables(groups_y, cols_dev, waves)
    own = lax.dynamic_slice_in_dim(response[0], lax.axis_index("gy"), 1, 0)
    half = cols_all // 2 // groups_y
    resp = own.reshape(2, half, groups_y).transpose(0, 2, 1)
    resp = jnp.pad(resp, ((0, 0), (0, 0), (0, waves - half)))
    incr = pl.pallas_call(
        functools.partial(zonal_kernel, 2.0 / cols_all),
        out_shape=jax.ShapeDtypeStruct((groups_y, rows_dev, cols_dev), BF),
        in_specs=[VMEM] * 5,
        out_specs=VMEM,
        compiler_params=PARAMS,
        name="zonal_filter",
    )(circles, resp, ahead, back, twiddle)
    incr = lax.all_to_all(incr, "gy", split_axis=0, concat_axis=0, tiled=True)

    fields = jnp.concatenate([surface, state[0, FC:]], axis=0) + incr.astype(F32)
    low, high = halo(fields[:, 0].astype(BF), fields[:, -1].astype(BF))
    padded = jnp.concatenate([low[:, None].astype(F32), fields, high[:, None].astype(F32)], axis=1)
    keep = jnp.where(section == 1, land_mask.astype(F32), jnp.float32(1.0))
    rate = diffusion[0][None]
    fields = fields + rate * (padded[:, 2:] + padded[:, :-2] - 2.0 * fields)
    return (fields * keep[None])[None]


def solution(mesh):
    return jax.shard_map(
        local,
        mesh=mesh,
        in_specs=(
            P("comp", None, "gx", "gy"),
            P("comp", None, None),
            P("comp", "gx", "gy"),
            P("gx", "gy"),
            P("comp", "gx", "gy", None, None),
            P("comp", "gx", "gy", None, None),
            P("comp", "gx", "gy", None, None),
            P("comp", "gx", "gy", None),
        ),
        out_specs=P("comp", None, "gx", "gy"),
        check_vma=False,
    )
```

```python
import functools
import math

import jax
import jax.numpy as jnp
import numpy as np
from jax import lax
from jax.experimental import pallas as pl
from jax.experimental.pallas import tpu as pltpu
from jax.sharding import PartitionSpec as P

FC = 4
LANES = 128
BF = jnp.bfloat16
F32 = jnp.float32
VMEM = pl.BlockSpec(memory_space=pltpu.VMEM)
SMEM = pl.BlockSpec(memory_space=pltpu.SMEM)
PARAMS = pltpu.CompilerParams(vmem_limit_bytes=32 * 2**20)


def one_hot(rows, index):
    spot = lax.broadcasted_iota(jnp.int32, (rows, index.shape[1]), 0)
    return jnp.where(spot == index, 1.0, 0.0)


def split_cell(idx, cols):
    row = (idx.astype(F32) * (1.0 / cols) + 0.5 / cols).astype(jnp.int32)
    return row, idx - row * cols


def tiles(block):
    return jnp.concatenate([block[:, t : t + LANES] for t in range(0, block.shape[1], LANES)], axis=0)


def untile(block, rows):
    return jnp.concatenate([block[t : t + rows] for t in range(0, block.shape[0], rows)], axis=1)


def pack_kernel(split, state_ref, dst_ref, out_ref):
    _, levels, rows, cols = state_ref.shape
    peers, slots = dst_ref.shape
    groups = peers // levels
    for h in range(levels):
        idx = dst_ref[pl.ds(h, groups, stride=levels), :]
        row, col = split_cell(idx, cols)
        tile = col // LANES
        line = (tile * rows + row).astype(F32).astype(BF)
        lane = (col - tile * LANES).astype(F32).astype(BF)
        u, other = h // split, h % split
        for v in range(split):
            piece = u * split + v
            out_ref[piece, pl.ds(other * groups, groups), :] = line
            out_ref[piece, pl.ds((split + other) * groups, groups), :] = lane
        out_ref[h, pl.ds(2 * split * groups, rows * cols // LANES), :] = tiles(state_ref[0, h]).astype(BF)


def gather_kernel(split, blocks, count_ref, surf_ref, src_ref, weight_ref, pick_ref, out_ref):
    _, _, rows, cols = surf_ref.shape
    peers, slots = src_ref.shape
    fc = split * out_ref.shape[1] // blocks
    each = fc // split * blocks
    surface = surf_ref[0, :fc].reshape(fc * rows, cols).astype(BF)
    lane = lax.broadcasted_iota(jnp.int32, (blocks, slots), 1)
    sub = lax.broadcasted_iota(jnp.int32, (blocks, slots), 0)

    def step(g, carry):
        base = pl.multiple_of(g * blocks, blocks)
        row, col = split_cell(src_ref[pl.ds(base, blocks), :], cols)
        found = []
        for i in range(0, blocks, 2):
            pick = jnp.concatenate([one_hot(cols, col[j : j + 1]) for j in (i, i + 1)], axis=1)
            lines = jnp.dot(surface, pick.astype(BF), preferred_element_type=F32)
            for j in range(2):
                mask = one_hot(rows, row[i + j : i + j + 1])
                own = lines[:, j * slots : (j + 1) * slots].reshape(fc, rows, slots)
                found.append((own * mask[None]).reshape(fc * rows, slots))
        value = jnp.dot(pick_ref[...], jnp.concatenate(found, axis=0).astype(BF), preferred_element_type=F32)
        limit = jnp.zeros((blocks, slots), jnp.int32)
        for i in range(blocks):
            limit = jnp.where(sub == i, count_ref[base + i], limit)
        weight = jnp.where(lane < limit, weight_ref[pl.ds(base, blocks), :], 0.0)
        value = value * jnp.concatenate([weight] * fc, axis=0)
        for v in range(split):
            out_ref[g * split + v] = value[v * each : (v + 1) * each].astype(BF)
        return carry

    lax.fori_loop(0, peers // blocks, step, 0)


def band_kernel(
    split, scale, arrived_ref, early_ref, resp_ref, ahead_ref, back_ref, twiddle_ref, out_ref, value_ref, line_ref, lane_ref, acc_ref
):
    senders, each, slots = arrived_ref.shape
    blocks = early_ref.shape[0]
    fields = each // blocks
    groups = senders // split
    rows, cols = out_ref.shape[2], out_ref.shape[3]
    cell_rows = rows * cols // LANES
    for s in range(senders):
        value_ref[s] = arrived_ref[s].astype(F32)
    for h in range(blocks):
        line_ref[h] = early_ref[h, :senders].astype(F32).astype(jnp.int32)
        lane_ref[h] = early_ref[h, senders : 2 * senders].astype(F32).astype(jnp.int32)
    acc_ref[...] = jnp.zeros_like(acc_ref)

    def step(g, carry):
        for h in range(blocks):
            spread, pick = [], []
            for v in range(split):
                at = v * groups + g
                mask = lax.broadcasted_iota(jnp.int32, (cell_rows, slots), 0) == line_ref[h, pl.ds(at, 1), :]
                vals = [
                    jnp.where(mask, value_ref[g * split + v, c * blocks + h : c * blocks + h + 1, :], 0.0)
                    for c in range(fields)
                ]
                spread.append(jnp.concatenate(vals, axis=0).astype(BF))
                pick.append(one_hot(LANES, lane_ref[h, pl.ds(at, 1), :]).astype(BF))
            acc_ref[h] += lax.dot_general(
                jnp.concatenate(spread, axis=1),
                jnp.concatenate(pick, axis=1),
                (((1,), (1,)), ((), ())),
                preferred_element_type=F32,
            )
        return carry

    lax.fori_loop(0, groups, step, 0)
    for c in range(fields + 1):
        if c < fields:
            x = [untile(acc_ref[h, c * cell_rows : (c + 1) * cell_rows], rows) for h in range(blocks)]
        else:
            x = [untile(early_ref[h, 2 * senders :].astype(F32), rows) for h in range(blocks)]
        incr = zonal_rows(x, resp_ref.at[c], ahead_ref, back_ref, twiddle_ref)
        for h in range(blocks):
            total = incr[h] * scale
            if c < fields:
                total = total + untile(acc_ref[h, c * cell_rows : (c + 1) * cell_rows], rows)
            out_ref[h, c] = total.astype(BF)


def sum_kernel(split, odd_ref, state_ref, back_ref, fields_ref, first_ref, second_ref):
    _, levels, rows, _ = state_ref.shape
    each = back_ref.shape[1] - 1
    tops, bottoms = [], []
    for c in range(levels):
        total = state_ref[0, c] + back_ref[c, each].astype(F32)
        if c < split * each:
            for u in range(levels // split):
                total = total + back_ref[u * split + c // each, c % each].astype(F32)
        fields_ref[c] = total
        tops.append(total[:1])
        bottoms.append(total[rows - 1 :])
    top, bottom = jnp.concatenate(tops, axis=0), jnp.concatenate(bottoms, axis=0)
    odd = odd_ref[0] == 1
    first_ref[...] = jnp.where(odd, top, bottom).astype(BF)
    second_ref[...] = jnp.where(odd, bottom, top).astype(BF)


def diffuse_kernel(flag_ref, fields_ref, first_ref, second_ref, rate_ref, land_ref, out_ref):
    levels, rows, cols = fields_ref.shape
    odd = flag_ref[0] == 1
    first, second = first_ref[...].astype(F32), second_ref[...].astype(F32)
    low, high = jnp.where(odd, first, second), jnp.where(odd, second, first)
    keep = jnp.where(flag_ref[1] == 1, land_ref[...].astype(F32), 1.0)
    rate = rate_ref[0] * keep
    for c in range(levels):
        own = fields_ref[c]
        above = jnp.concatenate([low[c : c + 1], own[: rows - 1]], axis=0)
        below = jnp.concatenate([own[1:], high[c : c + 1]], axis=0)
        out_ref[0, c] = own * keep + rate * (above + below - 2.0 * own)


def zonal_tables(blocks, cols, waves):
    total = blocks * cols
    b = np.arange(cols)
    n = np.arange(total // 2 // blocks)
    angle = 2.0 * np.pi * ((b[:, None] * n[None, :]) % cols) / cols
    pad = ((0, 0), (0, waves - len(n)))
    cos, sin = np.pad(np.cos(angle), pad), np.pad(np.sin(angle), pad)
    ahead = np.concatenate([cos, sin], axis=1)
    back = np.concatenate([cos.T, sin.T], axis=1)
    turn = 2.0 * np.pi * np.arange(blocks)[:, None] * b[None, :] / total
    twiddle = np.stack([np.cos(turn), np.sin(turn)])
    return jnp.asarray(ahead, BF), jnp.asarray(back, BF), jnp.asarray(twiddle, F32)


def zonal_rows(x, resp, ahead_ref, back_ref, twiddle_ref):
    blocks = len(x)
    rows, cols = x[0].shape
    waves = ahead_ref.shape[1] // 2
    half = math.sqrt(0.5)
    a = [x[i] + x[i + 4] for i in range(4)]
    b = [x[i] - x[i + 4] for i in range(4)]
    b13, d13 = half * (b[1] + b[3]), half * (b[1] - b[3])
    a02, a13 = a[0] + a[2], a[1] + a[3]
    z1 = (b[0] + d13, -(b[2] + b13))
    z2 = (a[0] - a[2], a[3] - a[1])
    z3 = (b[0] - d13, b[2] - b13)
    z = [(a02 + a13, None), z1, z2, z3, (a02 - a13, None)]
    z += [(re, -im) for re, im in (z3, z2, z1)]
    real, imag = [], []
    for r in range(blocks):
        re, im = z[r]
        ct, st = twiddle_ref[0, r : r + 1, :], twiddle_ref[1, r : r + 1, :]
        if r == 0:
            real.append(re)
        elif im is None:
            real.append(re * ct)
            imag.append(-re * st)
        else:
            real.append(re * ct + im * st)
            imag.append(im * ct - re * st)
    spec = jnp.dot(jnp.concatenate(real + imag, axis=0).astype(BF), ahead_ref[...], preferred_element_type=F32)
    cosine, sine = [], []
    for r in range(blocks):
        own = spec[r * rows : (r + 1) * rows]
        c, s = own[:, :waves], own[:, waves:]
        if r > 0:
            other = spec[(blocks + r - 1) * rows : (blocks + r) * rows]
            c, s = c + other[:, waves:], s - other[:, :waves]
        cosine.append(c * resp[0, r : r + 1, :])
        sine.append(s * resp[1, r : r + 1, :])
    full = jnp.dot(jnp.concatenate(cosine + sine, axis=0).astype(BF), back_ref[...], preferred_element_type=F32)
    u = []
    for r in range(blocks):
        fc = full[r * rows : (r + 1) * rows]
        fs = full[(blocks + r) * rows : (blocks + r + 1) * rows]
        re, im = fc[:, :cols] + fs[:, cols:], fc[:, cols:] - fs[:, :cols]
        ct, st = twiddle_ref[0, r : r + 1, :], twiddle_ref[1, r : r + 1, :]
        u.append((re, None) if r == 0 else (re * ct - im * st, re * st + im * ct))
    even, odd = u[0][0] + u[4][0], u[0][0] - u[4][0]
    p1, q1 = u[1][0] + u[7][0], u[1][1] - u[7][1]
    p2, q2 = u[2][0] + u[6][0], u[2][1] - u[6][1]
    p3, q3 = u[3][0] + u[5][0], u[3][1] - u[5][1]
    m1, n1 = half * (p1 - q1), half * (p1 + q1)
    m3, n3 = half * (p3 - q3), half * (p3 + q3)
    return [
        even + p1 + p2 + p3,
        odd + m1 - q2 - n3,
        even - q1 - p2 + q3,
        odd - n1 + q2 + m3,
        even - p1 + p2 - p3,
        odd - m1 - q2 + n3,
        even + q1 - p2 - q3,
        odd + n1 + q2 - m3,
    ]


def local(
    state, response, diffusion, land_mask, couple_src, couple_dst, couple_weight, couple_count
):
    levels, rows, cols = (state.shape[1], state.shape[2], state.shape[3])
    groups_x, split = lax.axis_size("gx"), lax.axis_size("gv")
    blocks = lax.axis_size("gu") * split
    peers = groups_x * blocks
    slots = couple_src.shape[4]
    cols_all = cols * blocks
    senders = groups_x * split
    each = FC // split
    cell_rows = rows * cols // LANES
    waves = 256
    gv = lax.axis_index("gv")
    own = lax.axis_index("gu") * split + gv
    src_idx = couple_src.reshape(peers, slots)
    dst_idx = couple_dst.reshape(peers, slots)
    weight = couple_weight.reshape(peers, slots)
    count = couple_count.reshape(peers)

    early = pl.pallas_call(
        functools.partial(pack_kernel, split),
        out_shape=jax.ShapeDtypeStruct((blocks, 2 * senders + cell_rows, LANES), BF),
        in_specs=[VMEM, VMEM],
        out_specs=VMEM,
        compiler_params=PARAMS,
        name="early_pack",
    )(state, dst_idx)
    early = lax.all_to_all(early, ("gu", "gv"), split_axis=0, concat_axis=0, tiled=True)

    spot = np.zeros((FC, blocks, blocks, FC, rows), np.float32)
    for c in range(FC):
        for h in range(blocks):
            spot[c, h, h, c] = 1.0
    outgoing = pl.pallas_call(
        functools.partial(gather_kernel, split, blocks),
        out_shape=jax.ShapeDtypeStruct((senders, each * blocks, slots), BF),
        in_specs=[SMEM, VMEM, VMEM, VMEM, VMEM],
        out_specs=VMEM,
        compiler_params=PARAMS,
        cost_estimate=pl.CostEstimate(flops=4 * 10**9, bytes_accessed=16 * 10**6, transcendentals=0),
        name="couple_gather",
    )(count, state, src_idx, weight, jnp.asarray(spot.reshape(FC * blocks, -1), BF))
    outgoing, early = lax.optimization_barrier((outgoing, early))
    crossed = lax.ppermute(outgoing, "comp", [(0, 1), (1, 0)])
    arrived = lax.all_to_all(crossed, ("gx", "gv"), split_axis=0, concat_axis=0, tiled=True)

    ahead, back, twiddle = zonal_tables(blocks, cols, waves)
    half = cols_all // 2 // blocks
    resp = jnp.concatenate(
        [lax.dynamic_slice_in_dim(response[0], gv * each, each, 0), lax.dynamic_slice_in_dim(response[0], own, 1, 0)], axis=0
    )
    resp = resp.reshape(each + 1, 2, half, blocks).transpose(0, 1, 3, 2)
    resp = jnp.pad(resp, ((0, 0), (0, 0), (0, 0), (0, waves - half)))
    incr = pl.pallas_call(
        functools.partial(band_kernel, split, 2.0 / cols_all),
        out_shape=jax.ShapeDtypeStruct((blocks, each + 1, rows, cols), BF),
        in_specs=[VMEM] * 6,
        out_specs=VMEM,
        scratch_shapes=[
            pltpu.VMEM((senders, each * blocks, slots), F32),
            pltpu.VMEM((blocks, senders, slots), jnp.int32),
            pltpu.VMEM((blocks, senders, slots), jnp.int32),
            pltpu.VMEM((blocks, each * cell_rows, LANES), F32),
        ],
        compiler_params=PARAMS,
        name="band_filter",
    )(arrived, early, resp, ahead, back, twiddle)
    incr = lax.all_to_all(incr, ("gu", "gv"), split_axis=0, concat_axis=0, tiled=True)

    odd = lax.axis_index("gx") % 2
    flag = jnp.stack([odd, lax.axis_index("comp")])
    edge = jax.ShapeDtypeStruct((levels, cols), BF)
    fields, first, second = pl.pallas_call(
        functools.partial(sum_kernel, split),
        out_shape=(jax.ShapeDtypeStruct((levels, rows, cols), F32), edge, edge),
        in_specs=[SMEM, VMEM, VMEM],
        out_specs=(VMEM, VMEM, VMEM),
        compiler_params=PARAMS,
        name="partial_sum",
    )(flag, state, incr)
    pairs = [(i, i ^ 1) for i in range(groups_x)]
    cross = [pair for i in range(1, groups_x - 1, 2) for pair in ((i, i + 1), (i + 1, i))]
    first = lax.ppermute(first, "gx", pairs)
    second = lax.ppermute(second, "gx", cross)
    return pl.pallas_call(
        diffuse_kernel,
        out_shape=jax.ShapeDtypeStruct((1, levels, rows, cols), F32),
        in_specs=[SMEM] + [VMEM] * 5,
        out_specs=VMEM,
        compiler_params=PARAMS,
        name="diffuse",
    )(flag, fields, first, second, diffusion, land_mask)


def solution(mesh):
    shape = mesh.devices.shape
    mesh = jax.sharding.Mesh(mesh.devices.reshape(shape[0], shape[1], shape[2] // 2, 2), ("comp", "gx", "gu", "gv"))
    gy = ("gu", "gv")
    return jax.shard_map(
        local,
        mesh=mesh,
        in_specs=(
            P("comp", None, "gx", gy),
            P("comp", None, None),
            P("comp", "gx", gy),
            P("gx", gy),
            P("comp", "gx", gy, None, None),
            P("comp", "gx", gy, None, None),
            P("comp", "gx", gy, None, None),
            P("comp", "gx", gy, None),
        ),
        out_specs=P("comp", None, "gx", gy),
        check_vma=False,
    )
```

```python
import functools
import math

import jax
import jax.numpy as jnp
import numpy as np
from jax import lax
from jax.experimental import pallas as pl
from jax.experimental.pallas import tpu as pltpu
from jax.sharding import PartitionSpec as P

FC = 4
LANES = 128
BF = jnp.bfloat16
F32 = jnp.float32
VMEM = pl.BlockSpec(memory_space=pltpu.VMEM)
SMEM = pl.BlockSpec(memory_space=pltpu.SMEM)
PARAMS = pltpu.CompilerParams(vmem_limit_bytes=32 * 2**20)


def one_hot(rows, index):
    spot = lax.broadcasted_iota(jnp.int32, (rows, index.shape[1]), 0)
    return jnp.where(spot == index, 1.0, 0.0)


def split_cell(idx, cols):
    row = (idx.astype(F32) * (1.0 / cols) + 0.5 / cols).astype(jnp.int32)
    return row, idx - row * cols


def split_lines(idx, rows, cols):
    row, col = split_cell(idx, cols)
    tile = col // LANES
    return tile * rows + row, col - tile * LANES


def tiles(block):
    return jnp.concatenate([block[:, t : t + LANES] for t in range(0, block.shape[1], LANES)], axis=0)


def untile(block, rows):
    return jnp.concatenate([block[t : t + rows] for t in range(0, block.shape[0], rows)], axis=1)


def pack_kernel(split, state_ref, dst_ref, out_ref):
    _, levels, rows, cols = state_ref.shape
    peers, slots = dst_ref.shape
    groups = peers // levels
    for h in range(levels):
        idx = dst_ref[pl.ds(h, groups, stride=levels), :]
        line, lane = split_lines(idx, rows, cols)
        line, lane = line.astype(F32).astype(BF), lane.astype(F32).astype(BF)
        u, other = h // split, h % split
        for v in range(split):
            piece = u * split + v
            out_ref[piece, pl.ds(other * groups, groups), :] = line
            out_ref[piece, pl.ds((split + other) * groups, groups), :] = lane
        out_ref[h, pl.ds(2 * split * groups, rows * cols // LANES), :] = tiles(state_ref[0, h]).astype(BF)


def gather_kernel(split, blocks, count_ref, surf_ref, src_ref, weight_ref, pick_ref, out_ref):
    _, _, rows, cols = surf_ref.shape
    peers, slots = src_ref.shape
    fc = split * out_ref.shape[1] // blocks
    each = fc // split * blocks
    lines = rows * cols // LANES
    half = -(-lines // 16) * 8
    shift = lines - half
    surface = [tiles(surf_ref[0, c]) for c in range(fc)]
    surface = jnp.concatenate([jnp.concatenate([x[:half], x[shift:]], axis=1) for x in surface], axis=0).astype(BF)
    lane = lax.broadcasted_iota(jnp.int32, (blocks, slots), 1)
    sub = lax.broadcasted_iota(jnp.int32, (blocks, slots), 0)
    spot = lax.broadcasted_iota(jnp.int32, (half, slots), 0)

    def step(g, carry):
        base = pl.multiple_of(g * blocks, blocks)
        line, col = split_lines(src_ref[pl.ds(base, blocks), :], rows, cols)
        upper = line >= half
        line = line - jnp.where(upper, shift, 0)
        col = col + jnp.where(upper, LANES, 0)
        found = []
        for i in range(0, blocks, 2):
            pick = jnp.concatenate([one_hot(2 * LANES, col[j : j + 1]) for j in (i, i + 1)], axis=1)
            values = jnp.dot(surface, pick.astype(BF), preferred_element_type=F32)
            for j in range(2):
                own = values[:, j * slots : (j + 1) * slots].reshape(fc, half, slots)
                own = jnp.where((spot == line[i + j : i + j + 1])[None], own, 0.0)
                found.append(jnp.sum(own.reshape(fc, half // 8, 8, slots), axis=1).reshape(fc * 8, slots))
        value = jnp.dot(pick_ref[...], jnp.concatenate(found, axis=0).astype(BF), preferred_element_type=F32)
        limit = jnp.zeros((blocks, slots), jnp.int32)
        for i in range(blocks):
            limit = jnp.where(sub == i, count_ref[base + i], limit)
        weight = jnp.where(lane < limit, weight_ref[pl.ds(base, blocks), :], 0.0)
        value = value * jnp.concatenate([weight] * fc, axis=0)
        for v in range(split):
            out_ref[g * split + v] = value[v * each : (v + 1) * each].astype(BF)
        return carry

    lax.fori_loop(0, peers // blocks, step, 0, unroll=16)


def circle_kernel(scale, early_ref, resp_ref, ahead_ref, back_ref, twiddle_ref, out_ref):
    blocks, rows, cols = out_ref.shape
    start = early_ref.shape[1] - rows * cols // LANES
    x = [untile(early_ref[h, start:].astype(F32), rows) for h in range(blocks)]
    incr = zonal_rows(x, resp_ref[0], resp_ref[1], ahead_ref, back_ref, twiddle_ref)
    for h in range(blocks):
        out_ref[h] = (incr[h] * scale).astype(BF)


def scatter_kernel(
    split, flag_ref, arrived_ref, early_ref, part_ref, first_ref, second_ref, value_ref, line_ref, lane_ref, acc_ref
):
    senders, each, slots = arrived_ref.shape
    blocks = early_ref.shape[0]
    fields, _, rows, cols = part_ref.shape
    groups = senders // split
    lines = rows * cols // LANES
    for s in range(senders):
        value_ref[s] = arrived_ref[s].astype(F32)
    for h in range(blocks):
        line_ref[h] = early_ref[h, :senders].astype(F32).astype(jnp.int32)
        lane_ref[h] = early_ref[h, senders : 2 * senders].astype(F32).astype(jnp.int32)
    acc_ref[...] = jnp.zeros_like(acc_ref)
    spot = lax.broadcasted_iota(jnp.int32, (lines, slots), 0)

    def step(g, carry):
        for h in range(blocks):
            spread, pick = [], []
            for v in range(split):
                at = v * groups + g
                mask = spot == line_ref[h, pl.ds(at, 1), :]
                vals = [
                    jnp.where(mask, value_ref[g * split + v, c * blocks + h : c * blocks + h + 1, :], 0.0)
                    for c in range(fields)
                ]
                spread.append(jnp.concatenate(vals, axis=0).astype(BF))
                pick.append(one_hot(LANES, lane_ref[h, pl.ds(at, 1), :]).astype(BF))
            acc_ref[h] += lax.dot_general(
                jnp.concatenate(spread, axis=1),
                jnp.concatenate(pick, axis=1),
                (((1,), (1,)), ((), ())),
                preferred_element_type=F32,
            )
        return carry

    lax.fori_loop(0, groups, step, 0, unroll=4)
    tops, bottoms = [], []
    for c in range(fields + 1):
        for h in range(blocks):
            if c < fields:
                x = untile(acc_ref[h, c * lines : (c + 1) * lines], rows)
                part_ref[c, h] = x
            else:
                x = untile(early_ref[h, 2 * senders :].astype(F32), rows)
            tops.append(x[:1])
            bottoms.append(x[rows - 1 :])
    top, bottom = jnp.concatenate(tops, axis=0), jnp.concatenate(bottoms, axis=0)
    odd = flag_ref[0] == 1
    first_ref[...] = jnp.where(odd, top, bottom).astype(BF)
    second_ref[...] = jnp.where(odd, bottom, top).astype(BF)


def part_kernel(scale, part_ref, resp_ref, ahead_ref, back_ref, twiddle_ref, out_ref):
    blocks, fields, rows, cols = out_ref.shape
    for c in range(fields):
        x = [part_ref[c, h] for h in range(blocks)]
        incr = zonal_rows(x, resp_ref[c, 0], resp_ref[c, 1], ahead_ref, back_ref, twiddle_ref)
        for h in range(blocks):
            out_ref[h, c] = (incr[h] * scale + x[h]).astype(BF)


def edge_kernel(
    scale, flag_ref, first_ref, second_ref, part_ref, circle_ref, resp_ref, ahead_ref, back_ref, twiddle_ref, out_ref
):
    blocks, fields, rows, cols = part_ref.shape
    sets = fields + 1
    odd = flag_ref[0] == 1
    first, second = first_ref[...].astype(F32), second_ref[...].astype(F32)
    low, high = jnp.where(odd, first, second), jnp.where(odd, second, first)
    x = []
    blank = jnp.zeros((8 - 2 * sets, cols), F32)
    for h in range(blocks):
        lines = [side[c * blocks + h : c * blocks + h + 1] for c in range(sets) for side in (low, high)]
        x.append(jnp.concatenate(lines + [blank], axis=0))
    zero = jnp.zeros((8 - 2 * sets, resp_ref.shape[3]), F32)
    resp = [
        [
            jnp.concatenate([resp_ref[c, k, r : r + 1, :] for c in range(sets) for _ in range(2)] + [zero], axis=0)
            for r in range(blocks)
        ]
        for k in range(2)
    ]
    incr = zonal_rows(x, resp[0], resp[1], ahead_ref, back_ref, twiddle_ref)
    for h in range(blocks):
        for c in range(fields):
            out_ref[h, c * rows : (c + 1) * rows] = part_ref[h, c]
        out_ref[h, fields * rows : sets * rows] = circle_ref[h]
        out_ref[h, sets * rows :] = (incr[h] * scale + x[h]).astype(BF)


def final_kernel(split, flag_ref, state_ref, back_ref, rate_ref, land_ref, out_ref):
    _, levels, rows, cols = state_ref.shape
    sets = (back_ref.shape[1] - 8) // rows
    fields = sets - 1
    keep = jnp.where(flag_ref[1] == 1, land_ref[...].astype(F32), 1.0)
    rate = rate_ref[0] * keep
    edges = [back_ref[z, sets * rows :].astype(F32) for z in range(levels)]
    for c in range(levels):
        own = state_ref[0, c] + back_ref[c, fields * rows : sets * rows].astype(F32)
        low, high = edges[c][2 * fields : 2 * fields + 1], edges[c][2 * fields + 1 : 2 * fields + 2]
        if c < split * fields:
            at = c % fields
            for u in range(levels // split):
                z = u * split + c // fields
                own = own + back_ref[z, at * rows : (at + 1) * rows].astype(F32)
                low = low + edges[z][2 * at : 2 * at + 1]
                high = high + edges[z][2 * at + 1 : 2 * at + 2]
        above = jnp.concatenate([low, own[: rows - 1]], axis=0)
        below = jnp.concatenate([own[1:], high], axis=0)
        out_ref[0, c] = own * keep + rate * (above + below - 2.0 * own)


def zonal_tables(blocks, cols, waves):
    total = blocks * cols
    b = np.arange(cols)
    n = np.arange(total // 2 // blocks)
    angle = 2.0 * np.pi * ((b[:, None] * n[None, :]) % cols) / cols
    pad = ((0, 0), (0, waves - len(n)))
    cos, sin = np.pad(np.cos(angle), pad), np.pad(np.sin(angle), pad)
    ahead = np.concatenate([cos, sin], axis=1)
    back = np.concatenate([cos.T, sin.T], axis=1)
    turn = 2.0 * np.pi * np.arange(blocks)[:, None] * b[None, :] / total
    twiddle = np.stack([np.cos(turn), np.sin(turn)])
    return jnp.asarray(ahead, BF), jnp.asarray(back, BF), jnp.asarray(twiddle, F32)


def response_row(resp, r):
    return resp[r] if isinstance(resp, list) else resp[r : r + 1, :]


def zonal_rows(x, resp_cos, resp_sin, ahead_ref, back_ref, twiddle_ref):
    blocks = len(x)
    rows, cols = x[0].shape
    waves = ahead_ref.shape[1] // 2
    half = math.sqrt(0.5)
    a = [x[i] + x[i + 4] for i in range(4)]
    b = [x[i] - x[i + 4] for i in range(4)]
    b13, d13 = half * (b[1] + b[3]), half * (b[1] - b[3])
    a02, a13 = a[0] + a[2], a[1] + a[3]
    z1 = (b[0] + d13, -(b[2] + b13))
    z2 = (a[0] - a[2], a[3] - a[1])
    z3 = (b[0] - d13, b[2] - b13)
    z = [(a02 + a13, None), z1, z2, z3, (a02 - a13, None)]
    z += [(re, -im) for re, im in (z3, z2, z1)]
    real, imag = [], []
    for r in range(blocks):
        re, im = z[r]
        ct, st = twiddle_ref[0, r : r + 1, :], twiddle_ref[1, r : r + 1, :]
        if r == 0:
            real.append(re)
        elif im is None:
            real.append(re * ct)
            imag.append(-re * st)
        else:
            real.append(re * ct + im * st)
            imag.append(im * ct - re * st)
    spec = jnp.dot(jnp.concatenate(real + imag, axis=0).astype(BF), ahead_ref[...], preferred_element_type=F32)
    cosine, sine = [], []
    for r in range(blocks):
        own = spec[r * rows : (r + 1) * rows]
        c, s = own[:, :waves], own[:, waves:]
        if r > 0:
            other = spec[(blocks + r - 1) * rows : (blocks + r) * rows]
            c, s = c + other[:, waves:], s - other[:, :waves]
        cosine.append(c * response_row(resp_cos, r))
        sine.append(s * response_row(resp_sin, r))
    full = jnp.dot(jnp.concatenate(cosine + sine, axis=0).astype(BF), back_ref[...], preferred_element_type=F32)
    u = []
    for r in range(blocks):
        fc = full[r * rows : (r + 1) * rows]
        fs = full[(blocks + r) * rows : (blocks + r + 1) * rows]
        re, im = fc[:, :cols] + fs[:, cols:], fc[:, cols:] - fs[:, :cols]
        ct, st = twiddle_ref[0, r : r + 1, :], twiddle_ref[1, r : r + 1, :]
        u.append((re, None) if r == 0 else (re * ct - im * st, re * st + im * ct))
    even, odd = u[0][0] + u[4][0], u[0][0] - u[4][0]
    p1, q1 = u[1][0] + u[7][0], u[1][1] - u[7][1]
    p2, q2 = u[2][0] + u[6][0], u[2][1] - u[6][1]
    p3, q3 = u[3][0] + u[5][0], u[3][1] - u[5][1]
    m1, n1 = half * (p1 - q1), half * (p1 + q1)
    m3, n3 = half * (p3 - q3), half * (p3 + q3)
    return [
        even + p1 + p2 + p3,
        odd + m1 - q2 - n3,
        even - q1 - p2 + q3,
        odd - n1 + q2 + m3,
        even - p1 + p2 - p3,
        odd - m1 - q2 + n3,
        even + q1 - p2 - q3,
        odd + n1 + q2 - m3,
    ]


def cost(micros):
    return pl.CostEstimate(flops=micros * 10**9, bytes_accessed=micros * 3 * 10**6, transcendentals=0)


def local(
    state, response, diffusion, land_mask, couple_src, couple_dst, couple_weight, couple_count
):
    levels, rows, cols = (state.shape[1], state.shape[2], state.shape[3])
    groups_x, split = lax.axis_size("gx"), lax.axis_size("gv")
    blocks = lax.axis_size("gu") * split
    peers = groups_x * blocks
    slots = couple_src.shape[4]
    cols_all = cols * blocks
    senders = groups_x * split
    each = FC // split
    cell_rows = rows * cols // LANES
    waves = 256
    gv = lax.axis_index("gv")
    own = lax.axis_index("gu") * split + gv
    src_idx = couple_src.reshape(peers, slots)
    dst_idx = couple_dst.reshape(peers, slots)
    weight = couple_weight.reshape(peers, slots)
    count = couple_count.reshape(peers)

    early = pl.pallas_call(
        functools.partial(pack_kernel, split),
        out_shape=jax.ShapeDtypeStruct((blocks, 2 * senders + cell_rows, LANES), BF),
        in_specs=[VMEM, VMEM],
        out_specs=VMEM,
        compiler_params=PARAMS,
        name="early_pack",
    )(state, dst_idx)
    early = lax.all_to_all(early, ("gu", "gv"), split_axis=0, concat_axis=0, tiled=True)

    spot = np.zeros((FC, blocks, blocks, FC, 8), np.float32)
    for c in range(FC):
        for h in range(blocks):
            spot[c, h, h, c] = 1.0
    outgoing = pl.pallas_call(
        functools.partial(gather_kernel, split, blocks),
        out_shape=jax.ShapeDtypeStruct((senders, each * blocks, slots), BF),
        in_specs=[SMEM, VMEM, VMEM, VMEM, VMEM],
        out_specs=VMEM,
        compiler_params=PARAMS,
        cost_estimate=cost(4),
        name="couple_gather",
    )(count, state, src_idx, weight, jnp.asarray(spot.reshape(FC * blocks, -1), BF))
    outgoing, early = lax.optimization_barrier((outgoing, early))
    crossed = lax.ppermute(outgoing, "comp", [(0, 1), (1, 0)])
    crossed, early = lax.optimization_barrier((crossed, early))
    arrived = lax.all_to_all(crossed, ("gx", "gv"), split_axis=0, concat_axis=0, tiled=True)

    ahead, back, twiddle = zonal_tables(blocks, cols, waves)
    half = cols_all // 2 // blocks
    resp = jnp.concatenate(
        [lax.dynamic_slice_in_dim(response[0], gv * each, each, 0), lax.dynamic_slice_in_dim(response[0], own, 1, 0)], axis=0
    )
    resp = resp.reshape(each + 1, 2, half, blocks).transpose(0, 1, 3, 2)
    resp = jnp.pad(resp, ((0, 0), (0, 0), (0, 0), (0, waves - half)))
    scale = 2.0 / cols_all
    flag = jnp.stack([lax.axis_index("gx") % 2, lax.axis_index("comp")])

    circle = pl.pallas_call(
        functools.partial(circle_kernel, scale),
        out_shape=jax.ShapeDtypeStruct((blocks, rows, cols), BF),
        in_specs=[VMEM] * 5,
        out_specs=VMEM,
        compiler_params=PARAMS,
        cost_estimate=cost(2),
        name="circle_filter",
    )(early, resp[each], ahead, back, twiddle)
    edge = jax.ShapeDtypeStruct(((each + 1) * blocks, cols), BF)
    part, first, second = pl.pallas_call(
        functools.partial(scatter_kernel, split),
        out_shape=(jax.ShapeDtypeStruct((each, blocks, rows, cols), F32), edge, edge),
        in_specs=[SMEM, VMEM, VMEM],
        out_specs=(VMEM, VMEM, VMEM),
        scratch_shapes=[
            pltpu.VMEM((senders, each * blocks, slots), F32),
            pltpu.VMEM((blocks, senders, slots), jnp.int32),
            pltpu.VMEM((blocks, senders, slots), jnp.int32),
            pltpu.VMEM((blocks, each * cell_rows, LANES), F32),
        ],
        compiler_params=PARAMS,
        cost_estimate=cost(4),
        name="couple_scatter",
    )(flag, arrived, early)
    pairs = [(i, i ^ 1) for i in range(groups_x)]
    cross = [pair for i in range(1, groups_x - 1, 2) for pair in ((i, i + 1), (i + 1, i))]
    first = lax.ppermute(first, "gx", pairs)
    second = lax.ppermute(second, "gx", cross)
    part = pl.pallas_call(
        functools.partial(part_kernel, scale),
        out_shape=jax.ShapeDtypeStruct((blocks, each, rows, cols), BF),
        in_specs=[VMEM] * 5,
        out_specs=VMEM,
        compiler_params=PARAMS,
        cost_estimate=cost(3),
        name="part_filter",
    )(part, resp, ahead, back, twiddle)
    incr = pl.pallas_call(
        functools.partial(edge_kernel, scale),
        out_shape=jax.ShapeDtypeStruct((blocks, (each + 1) * rows + 8, cols), BF),
        in_specs=[SMEM] + [VMEM] * 8,
        out_specs=VMEM,
        compiler_params=PARAMS,
        cost_estimate=cost(1),
        name="edge_filter",
    )(flag, first, second, part, circle, resp, ahead, back, twiddle)
    incr = lax.all_to_all(incr, ("gu", "gv"), split_axis=0, concat_axis=0, tiled=True)
    return pl.pallas_call(
        functools.partial(final_kernel, split),
        out_shape=jax.ShapeDtypeStruct((1, levels, rows, cols), F32),
        in_specs=[SMEM] + [VMEM] * 4,
        out_specs=VMEM,
        compiler_params=PARAMS,
        cost_estimate=cost(1),
        name="final_step",
    )(flag, state, incr, diffusion, land_mask)


def solution(mesh):
    shape = mesh.devices.shape
    mesh = jax.sharding.Mesh(mesh.devices.reshape(shape[0], shape[1], shape[2] // 2, 2), ("comp", "gx", "gu", "gv"))
    gy = ("gu", "gv")
    return jax.shard_map(
        local,
        mesh=mesh,
        in_specs=(
            P("comp", None, "gx", gy),
            P("comp", None, None),
            P("comp", "gx", gy),
            P("gx", gy),
            P("comp", "gx", gy, None, None),
            P("comp", "gx", gy, None, None),
            P("comp", "gx", gy, None, None),
            P("comp", "gx", gy, None),
        ),
        out_specs=P("comp", None, "gx", gy),
        check_vma=False,
    )
```

```python
import functools
import math

import jax
import jax.numpy as jnp
import numpy as np
from jax import lax
from jax.experimental import pallas as pl
from jax.experimental.pallas import tpu as pltpu
from jax.sharding import PartitionSpec as P

FC = 4
LANES = 128
BF = jnp.bfloat16
F32 = jnp.float32
VMEM = pl.BlockSpec(memory_space=pltpu.VMEM)
SMEM = pl.BlockSpec(memory_space=pltpu.SMEM)
HBM = pl.BlockSpec(memory_space=pltpu.HBM)
LARGE = pltpu.CompilerParams(vmem_limit_bytes=60 * 2**20)
PARAMS = pltpu.CompilerParams(vmem_limit_bytes=32 * 2**20)


def one_hot(rows, index):
    spot = lax.broadcasted_iota(jnp.int16, (rows, index.shape[1]), 0)
    return jnp.where(spot == index.astype(jnp.int16), jnp.asarray(1, BF), jnp.asarray(0, BF))


def split_cell(idx, cols):
    row = (idx.astype(F32) * (1.0 / cols) + 0.5 / cols).astype(jnp.int32)
    return row, idx - row * cols


def split_lines(idx, rows, cols):
    row, col = split_cell(idx, cols)
    tile = col // LANES
    return tile * rows + row, col - tile * LANES


def tiles(block):
    return jnp.concatenate([block[:, t : t + LANES] for t in range(0, block.shape[1], LANES)], axis=0)


def untile(block, rows):
    return jnp.concatenate([block[t : t + rows] for t in range(0, block.shape[0], rows)], axis=1)


def give_kernel(count_ref, state_hbm, src_hbm, weight_hbm, give_ref, state_ref, src_ref, weight_ref, sems):
    copies = [
        pltpu.make_async_copy(state_hbm.at[0, :FC], state_ref, sems.at[0]),
        pltpu.make_async_copy(src_hbm, src_ref, sems.at[1]),
        pltpu.make_async_copy(weight_hbm, weight_ref, sems.at[2]),
    ]
    for copy in copies:
        copy.start()
    for copy in copies:
        copy.wait()
    _, rows, cols = state_ref.shape
    peers, slots = src_ref.shape
    start = FC * rows * cols // LANES
    give_ref[:start] = jnp.concatenate([tiles(state_ref[c]) for c in range(FC)], axis=0).astype(BF)
    line, lane = split_lines(src_ref[...], rows, cols)
    give_ref[start : start + peers] = line.astype(F32).astype(BF)
    give_ref[start + peers : start + 2 * peers] = lane.astype(F32).astype(BF)
    slot = lax.broadcasted_iota(jnp.int32, (8, slots), 1)
    sub = lax.broadcasted_iota(jnp.int32, (8, slots), 0)
    weights = []
    for base in range(0, peers, 8):
        limit = jnp.zeros((8, slots), jnp.int32)
        for i in range(8):
            limit = jnp.where(sub == i, count_ref[base + i], limit)
        weights.append(jnp.where(slot < limit, weight_ref[base : base + 8, :], 0.0))
    give_ref[start + 2 * peers :] = jnp.concatenate(weights, axis=0).astype(BF)


def pack_kernel(split, state_hbm, dst_hbm, early_ref, state_ref, dst_ref, sems):
    copies = [
        pltpu.make_async_copy(dst_hbm, dst_ref, sems.at[0]),
        pltpu.make_async_copy(state_hbm, state_ref, sems.at[1]),
    ]
    for copy in copies:
        copy.start()
    for copy in copies:
        copy.wait()
    _, levels, rows, cols = state_ref.shape
    groups, blocks, slots = dst_ref.shape
    for h in range(blocks):
        line, lane = split_lines(dst_ref[:, h, :], rows, cols)
        line, lane = line.astype(F32).astype(BF), lane.astype(F32).astype(BF)
        u, other = h // split, h % split
        for v in range(split):
            piece = u * split + v
            early_ref[piece, other * groups : (other + 1) * groups, :] = line
            early_ref[piece, (split + other) * groups : (split + other + 1) * groups, :] = lane
        early_ref[h, 2 * split * groups :, :] = tiles(state_ref[0, h]).astype(BF)


def gather_kernel(split, blocks, lines, got_ref, pick_ref, out_ref, line_ref, lane_ref, weight_ref):
    peers, slots = line_ref.shape
    fc = split * out_ref.shape[1] // blocks
    each = fc // split * blocks
    start = fc * lines
    half = -(-lines // 16) * 8
    shift = lines - half
    surface = got_ref[:start].astype(F32)
    surface = [surface[c * lines : (c + 1) * lines] for c in range(fc)]
    surface = jnp.concatenate([jnp.concatenate([x[:half], x[shift:]], axis=1) for x in surface], axis=0).astype(BF)
    line = got_ref[start : start + peers].astype(F32).astype(jnp.int32)
    lane = got_ref[start + peers : start + 2 * peers].astype(F32).astype(jnp.int32)
    upper = line >= half
    line_ref[...] = line - jnp.where(upper, shift, 0)
    lane_ref[...] = lane + jnp.where(upper, LANES, 0)
    weight_ref[...] = got_ref[start + 2 * peers :].astype(F32)
    spot = lax.broadcasted_iota(jnp.int32, (half, slots), 0)

    def step(g, carry):
        base = pl.multiple_of(g * blocks, blocks)
        line = line_ref[pl.ds(base, blocks), :]
        lane = lane_ref[pl.ds(base, blocks), :]
        found = []
        for i in range(0, blocks, 2):
            pick = jnp.concatenate([one_hot(2 * LANES, lane[j : j + 1]) for j in (i, i + 1)], axis=1)
            values = jnp.dot(surface, pick, preferred_element_type=F32)
            for j in range(2):
                own = values[:, j * slots : (j + 1) * slots].reshape(fc, half, slots)
                own = jnp.where((spot == line[i + j : i + j + 1])[None], own, 0.0)
                found.append(jnp.sum(own.reshape(fc, half // 8, 8, slots), axis=1).reshape(fc * 8, slots))
        value = jnp.dot(pick_ref[...], jnp.concatenate(found, axis=0).astype(BF), preferred_element_type=F32)
        value = value * jnp.concatenate([weight_ref[pl.ds(base, blocks), :]] * fc, axis=0)
        for v in range(split):
            out_ref[g * split + v] = value[v * each : (v + 1) * each].astype(BF)
        return carry

    lax.fori_loop(0, peers // blocks, step, 0, unroll=16)


def circle_kernel(scale, early_ref, resp_ref, ahead_ref, back_ref, twiddle_ref, out_ref):
    blocks, rows, cols = out_ref.shape
    start = early_ref.shape[1] - rows * cols // LANES
    x = [untile(early_ref[h, start:].astype(F32), rows) for h in range(blocks)]
    incr = zonal_rows(x, resp_ref[0], resp_ref[1], ahead_ref, back_ref, twiddle_ref)
    for h in range(blocks):
        out_ref[h] = (incr[h] * scale).astype(BF)


def scatter_kernel(
    split, flag_ref, arrived_ref, early_ref, part_ref, first_ref, second_ref, value_ref, line_ref, lane_ref, acc_ref
):
    senders, each, slots = arrived_ref.shape
    blocks = early_ref.shape[0]
    fields, _, rows, cols = part_ref.shape
    groups = senders // split
    lines = rows * cols // LANES
    for s in range(senders):
        value_ref[s] = arrived_ref[s].astype(F32)
    for h in range(blocks):
        line_ref[h] = early_ref[h, :senders].astype(F32).astype(jnp.int32)
        lane_ref[h] = early_ref[h, senders : 2 * senders].astype(F32).astype(jnp.int32)
    acc_ref[...] = jnp.zeros_like(acc_ref)
    spot = lax.broadcasted_iota(jnp.int32, (lines, slots), 0)

    def step(pair, carry):
        for h in range(blocks):
            spread, pick = [], []
            for g in (2 * pair, 2 * pair + 1):
                for v in range(split):
                    at = v * groups + g
                    mask = spot == line_ref[h, pl.ds(at, 1), :]
                    vals = [
                        jnp.where(mask, value_ref[g * split + v, c * blocks + h : c * blocks + h + 1, :], 0.0)
                        for c in range(fields)
                    ]
                    spread.append(jnp.concatenate(vals, axis=0).astype(BF))
                    pick.append(one_hot(LANES, lane_ref[h, pl.ds(at, 1), :]))
            acc_ref[h] += lax.dot_general(
                jnp.concatenate(spread, axis=1),
                jnp.concatenate(pick, axis=1),
                (((1,), (1,)), ((), ())),
                preferred_element_type=F32,
            )
        return carry

    lax.fori_loop(0, groups // 2, step, 0, unroll=4)
    tops, bottoms = [], []
    for c in range(fields + 1):
        for h in range(blocks):
            if c < fields:
                x = untile(acc_ref[h, c * lines : (c + 1) * lines], rows)
                part_ref[c, h] = x
            else:
                x = untile(early_ref[h, 2 * senders :].astype(F32), rows)
            tops.append(x[:1])
            bottoms.append(x[rows - 1 :])
    top, bottom = jnp.concatenate(tops, axis=0), jnp.concatenate(bottoms, axis=0)
    odd = flag_ref[0] == 1
    first_ref[...] = jnp.where(odd, top, bottom).astype(BF)
    second_ref[...] = jnp.where(odd, bottom, top).astype(BF)


def part_kernel(scale, part_ref, resp_ref, ahead_ref, back_ref, twiddle_ref, out_ref):
    blocks, fields, rows, cols = out_ref.shape
    for c in range(fields):
        x = [part_ref[c, h] for h in range(blocks)]
        incr = zonal_rows(x, resp_ref[c, 0], resp_ref[c, 1], ahead_ref, back_ref, twiddle_ref)
        for h in range(blocks):
            out_ref[h, c] = (incr[h] * scale + x[h]).astype(BF)


def edge_kernel(
    scale, flag_ref, first_ref, second_ref, part_ref, circle_ref, resp_ref, ahead_ref, back_ref, twiddle_ref, out_ref
):
    blocks, fields, rows, cols = part_ref.shape
    sets = fields + 1
    odd = flag_ref[0] == 1
    first, second = first_ref[...].astype(F32), second_ref[...].astype(F32)
    low, high = jnp.where(odd, first, second), jnp.where(odd, second, first)
    x = []
    blank = jnp.zeros((8 - 2 * sets, cols), F32)
    for h in range(blocks):
        lines = [side[c * blocks + h : c * blocks + h + 1] for c in range(sets) for side in (low, high)]
        x.append(jnp.concatenate(lines + [blank], axis=0))
    zero = jnp.zeros((8 - 2 * sets, resp_ref.shape[3]), F32)
    resp = [
        [
            jnp.concatenate([resp_ref[c, k, r : r + 1, :] for c in range(sets) for _ in range(2)] + [zero], axis=0)
            for r in range(blocks)
        ]
        for k in range(2)
    ]
    incr = zonal_rows(x, resp[0], resp[1], ahead_ref, back_ref, twiddle_ref)
    for h in range(blocks):
        for c in range(fields):
            out_ref[h, c * rows : (c + 1) * rows] = part_ref[h, c]
        out_ref[h, fields * rows : sets * rows] = circle_ref[h]
        out_ref[h, sets * rows :] = (incr[h] * scale + x[h]).astype(BF)


def final_kernel(split, flag_ref, state_ref, back_ref, rate_ref, land_ref, out_ref):
    _, levels, rows, cols = state_ref.shape
    sets = (back_ref.shape[1] - 8) // rows
    fields = sets - 1
    keep = jnp.where(flag_ref[1] == 1, land_ref[...].astype(F32), 1.0)
    rate = rate_ref[0] * keep
    edges = [back_ref[z, sets * rows :].astype(F32) for z in range(levels)]
    for c in range(levels):
        own = state_ref[0, c] + back_ref[c, fields * rows : sets * rows].astype(F32)
        low, high = edges[c][2 * fields : 2 * fields + 1], edges[c][2 * fields + 1 : 2 * fields + 2]
        if c < split * fields:
            at = c % fields
            for u in range(levels // split):
                z = u * split + c // fields
                own = own + back_ref[z, at * rows : (at + 1) * rows].astype(F32)
                low = low + edges[z][2 * at : 2 * at + 1]
                high = high + edges[z][2 * at + 1 : 2 * at + 2]
        above = jnp.concatenate([low, own[: rows - 1]], axis=0)
        below = jnp.concatenate([own[1:], high], axis=0)
        out_ref[0, c] = own * keep + rate * (above + below - 2.0 * own)


def zonal_tables(blocks, cols, waves):
    total = blocks * cols
    b = np.arange(cols)
    n = np.arange(total // 2 // blocks)
    angle = 2.0 * np.pi * ((b[:, None] * n[None, :]) % cols) / cols
    pad = ((0, 0), (0, waves - len(n)))
    cos, sin = np.pad(np.cos(angle), pad), np.pad(np.sin(angle), pad)
    ahead = np.concatenate([cos, sin], axis=1)
    back = np.concatenate([cos.T, sin.T], axis=1)
    turn = 2.0 * np.pi * np.arange(blocks)[:, None] * b[None, :] / total
    twiddle = np.stack([np.cos(turn), np.sin(turn)])
    return jnp.asarray(ahead, BF), jnp.asarray(back, BF), jnp.asarray(twiddle, F32)


def response_row(resp, r):
    return resp[r] if isinstance(resp, list) else resp[r : r + 1, :]


def zonal_rows(x, resp_cos, resp_sin, ahead_ref, back_ref, twiddle_ref):
    blocks = len(x)
    rows, cols = x[0].shape
    waves = ahead_ref.shape[1] // 2
    half = math.sqrt(0.5)
    a = [x[i] + x[i + 4] for i in range(4)]
    b = [x[i] - x[i + 4] for i in range(4)]
    b13, d13 = half * (b[1] + b[3]), half * (b[1] - b[3])
    a02, a13 = a[0] + a[2], a[1] + a[3]
    z1 = (b[0] + d13, -(b[2] + b13))
    z2 = (a[0] - a[2], a[3] - a[1])
    z3 = (b[0] - d13, b[2] - b13)
    z = [(a02 + a13, None), z1, z2, z3, (a02 - a13, None)]
    z += [(re, -im) for re, im in (z3, z2, z1)]
    real, imag = [], []
    for r in range(blocks):
        re, im = z[r]
        ct, st = twiddle_ref[0, r : r + 1, :], twiddle_ref[1, r : r + 1, :]
        if r == 0:
            real.append(re)
        elif im is None:
            real.append(re * ct)
            imag.append(-re * st)
        else:
            real.append(re * ct + im * st)
            imag.append(im * ct - re * st)
    spec = jnp.dot(jnp.concatenate(real + imag, axis=0).astype(BF), ahead_ref[...], preferred_element_type=F32)
    cosine, sine = [], []
    for r in range(blocks):
        own = spec[r * rows : (r + 1) * rows]
        c, s = own[:, :waves], own[:, waves:]
        if r > 0:
            other = spec[(blocks + r - 1) * rows : (blocks + r) * rows]
            c, s = c + other[:, waves:], s - other[:, :waves]
        cosine.append(c * response_row(resp_cos, r))
        sine.append(s * response_row(resp_sin, r))
    full = jnp.dot(jnp.concatenate(cosine + sine, axis=0).astype(BF), back_ref[...], preferred_element_type=F32)
    u = []
    for r in range(blocks):
        fc = full[r * rows : (r + 1) * rows]
        fs = full[(blocks + r) * rows : (blocks + r + 1) * rows]
        re, im = fc[:, :cols] + fs[:, cols:], fc[:, cols:] - fs[:, :cols]
        ct, st = twiddle_ref[0, r : r + 1, :], twiddle_ref[1, r : r + 1, :]
        u.append((re, None) if r == 0 else (re * ct - im * st, re * st + im * ct))
    even, odd = u[0][0] + u[4][0], u[0][0] - u[4][0]
    p1, q1 = u[1][0] + u[7][0], u[1][1] - u[7][1]
    p2, q2 = u[2][0] + u[6][0], u[2][1] - u[6][1]
    p3, q3 = u[3][0] + u[5][0], u[3][1] - u[5][1]
    m1, n1 = half * (p1 - q1), half * (p1 + q1)
    m3, n3 = half * (p3 - q3), half * (p3 + q3)
    return [
        even + p1 + p2 + p3,
        odd + m1 - q2 - n3,
        even - q1 - p2 + q3,
        odd - n1 + q2 + m3,
        even - p1 + p2 - p3,
        odd - m1 - q2 + n3,
        even + q1 - p2 - q3,
        odd + n1 + q2 - m3,
    ]


def cost(micros):
    return pl.CostEstimate(flops=micros * 10**9, bytes_accessed=micros * 3 * 10**6, transcendentals=0)


def local(
    state, response, diffusion, land_mask, couple_src, couple_dst, couple_weight, couple_count
):
    levels, rows, cols = (state.shape[1], state.shape[2], state.shape[3])
    groups_x, split = lax.axis_size("gx"), lax.axis_size("gv")
    blocks = lax.axis_size("gu") * split
    peers = groups_x * blocks
    slots = couple_src.shape[4]
    cols_all = cols * blocks
    senders = groups_x * split
    each = FC // split
    cell_rows = rows * cols // LANES
    waves = 256
    gv = lax.axis_index("gv")
    own = lax.axis_index("gu") * split + gv
    src_idx = couple_src.reshape(peers, slots)
    weight = couple_weight.reshape(peers, slots)
    count = couple_count.reshape(peers)

    give = pl.pallas_call(
        give_kernel,
        out_shape=jax.ShapeDtypeStruct((FC * cell_rows + 3 * peers, LANES), BF),
        in_specs=[SMEM] + [HBM] * 3,
        out_specs=VMEM,
        scratch_shapes=[
            pltpu.VMEM((FC, rows, cols), F32),
            pltpu.VMEM((peers, slots), jnp.int32),
            pltpu.VMEM((peers, slots), F32),
            pltpu.SemaphoreType.DMA((3,)),
        ],
        compiler_params=LARGE,
        cost_estimate=cost(1),
        name="give_pack",
    )(count, state, src_idx, weight)
    got = lax.ppermute(give, "comp", [(0, 1), (1, 0)])
    early = pl.pallas_call(
        functools.partial(pack_kernel, split),
        out_shape=jax.ShapeDtypeStruct((blocks, 2 * senders + cell_rows, LANES), BF),
        in_specs=[HBM] * 2,
        out_specs=VMEM,
        scratch_shapes=[
            pltpu.VMEM(state.shape, F32),
            pltpu.VMEM((groups_x, blocks, slots), jnp.int32),
            pltpu.SemaphoreType.DMA((2,)),
        ],
        compiler_params=LARGE,
        cost_estimate=cost(1),
        name="early_pack",
    )(state, couple_dst.reshape(groups_x, blocks, slots))
    early = lax.all_to_all(early, ("gu", "gv"), split_axis=0, concat_axis=0, tiled=True)

    spot = np.zeros((FC, blocks, blocks, FC, 8), np.float32)
    for c in range(FC):
        for h in range(blocks):
            spot[c, h, h, c] = 1.0
    outgoing = pl.pallas_call(
        functools.partial(gather_kernel, split, blocks, cell_rows),
        out_shape=jax.ShapeDtypeStruct((senders, each * blocks, slots), BF),
        in_specs=[VMEM, VMEM],
        out_specs=VMEM,
        scratch_shapes=[
            pltpu.VMEM((peers, slots), jnp.int32),
            pltpu.VMEM((peers, slots), jnp.int32),
            pltpu.VMEM((peers, slots), F32),
        ],
        compiler_params=PARAMS,
        cost_estimate=cost(4),
        name="couple_gather",
    )(got, jnp.asarray(spot.reshape(FC * blocks, -1), BF))
    outgoing, early = lax.optimization_barrier((outgoing, early))
    arrived = lax.all_to_all(outgoing, ("gx", "gv"), split_axis=0, concat_axis=0, tiled=True)

    ahead, back, twiddle = zonal_tables(blocks, cols, waves)
    half = cols_all // 2 // blocks
    resp = jnp.concatenate(
        [lax.dynamic_slice_in_dim(response[0], gv * each, each, 0), lax.dynamic_slice_in_dim(response[0], own, 1, 0)], axis=0
    )
    resp = resp.reshape(each + 1, 2, half, blocks).transpose(0, 1, 3, 2)
    resp = jnp.pad(resp, ((0, 0), (0, 0), (0, 0), (0, waves - half)))
    scale = 2.0 / cols_all
    flag = jnp.stack([lax.axis_index("gx") % 2, lax.axis_index("comp")])

    circle = pl.pallas_call(
        functools.partial(circle_kernel, scale),
        out_shape=jax.ShapeDtypeStruct((blocks, rows, cols), BF),
        in_specs=[VMEM] * 5,
        out_specs=VMEM,
        compiler_params=PARAMS,
        cost_estimate=cost(2),
        name="circle_filter",
    )(early, resp[each], ahead, back, twiddle)
    edge = jax.ShapeDtypeStruct(((each + 1) * blocks, cols), BF)
    part, first, second = pl.pallas_call(
        functools.partial(scatter_kernel, split),
        out_shape=(jax.ShapeDtypeStruct((each, blocks, rows, cols), F32), edge, edge),
        in_specs=[SMEM, VMEM, VMEM],
        out_specs=(VMEM, VMEM, VMEM),
        scratch_shapes=[
            pltpu.VMEM((senders, each * blocks, slots), F32),
            pltpu.VMEM((blocks, senders, slots), jnp.int32),
            pltpu.VMEM((blocks, senders, slots), jnp.int32),
            pltpu.VMEM((blocks, each * cell_rows, LANES), F32),
        ],
        compiler_params=PARAMS,
        cost_estimate=cost(4),
        name="couple_scatter",
    )(flag, arrived, early)
    pairs = [(i, i ^ 1) for i in range(groups_x)]
    cross = [pair for i in range(1, groups_x - 1, 2) for pair in ((i, i + 1), (i + 1, i))]
    first = lax.ppermute(first, "gx", pairs)
    part = pl.pallas_call(
        functools.partial(part_kernel, scale),
        out_shape=jax.ShapeDtypeStruct((blocks, each, rows, cols), BF),
        in_specs=[VMEM] * 5,
        out_specs=VMEM,
        compiler_params=PARAMS,
        cost_estimate=cost(3),
        name="part_filter",
    )(part, resp, ahead, back, twiddle)
    second, part = lax.optimization_barrier((second, part))
    second = lax.ppermute(second, "gx", cross)
    incr = pl.pallas_call(
        functools.partial(edge_kernel, scale),
        out_shape=jax.ShapeDtypeStruct((blocks, (each + 1) * rows + 8, cols), BF),
        in_specs=[SMEM] + [VMEM] * 8,
        out_specs=VMEM,
        compiler_params=PARAMS,
        cost_estimate=cost(1),
        name="edge_filter",
    )(flag, first, second, part, circle, resp, ahead, back, twiddle)
    incr = lax.all_to_all(incr, ("gu", "gv"), split_axis=0, concat_axis=0, tiled=True)
    return pl.pallas_call(
        functools.partial(final_kernel, split),
        out_shape=jax.ShapeDtypeStruct((1, levels, rows, cols), F32),
        in_specs=[SMEM] + [VMEM] * 4,
        out_specs=VMEM,
        compiler_params=PARAMS,
        cost_estimate=cost(1),
        name="final_step",
    )(flag, state, incr, diffusion, land_mask)


def solution(mesh):
    shape = mesh.devices.shape
    mesh = jax.sharding.Mesh(mesh.devices.reshape(shape[0], shape[1], shape[2] // 2, 2), ("comp", "gx", "gu", "gv"))
    gy = ("gu", "gv")
    return jax.shard_map(
        local,
        mesh=mesh,
        in_specs=(
            P("comp", None, "gx", gy),
            P("comp", None, None),
            P("comp", "gx", gy),
            P("gx", gy),
            P("comp", "gx", gy, None, None),
            P("comp", "gx", gy, None, None),
            P("comp", "gx", gy, None, None),
            P("comp", "gx", gy, None),
        ),
        out_specs=P("comp", None, "gx", gy),
        check_vma=False,
    )
```

```python
import functools
import math

import jax
import jax.numpy as jnp
import numpy as np
from jax import lax
from jax.experimental import pallas as pl
from jax.experimental.pallas import tpu as pltpu
from jax.sharding import PartitionSpec as P

FC = 4
LANES = 128
BF = jnp.bfloat16
F32 = jnp.float32
VMEM = pl.BlockSpec(memory_space=pltpu.VMEM)
SMEM = pl.BlockSpec(memory_space=pltpu.SMEM)
HBM = pl.BlockSpec(memory_space=pltpu.HBM)
LARGE = pltpu.CompilerParams(vmem_limit_bytes=60 * 2**20)
PARAMS = pltpu.CompilerParams(vmem_limit_bytes=32 * 2**20)


def one_hot(rows, index):
    spot = lax.broadcasted_iota(jnp.int16, (rows, index.shape[1]), 0)
    return jnp.where(spot == index.astype(jnp.int16), jnp.asarray(1, BF), jnp.asarray(0, BF))


def split_cell(idx, cols):
    row = (idx.astype(F32) * (1.0 / cols) + 0.5 / cols).astype(jnp.int32)
    return row, idx - row * cols


def split_lines(idx, rows, cols):
    row, col = split_cell(idx, cols)
    tile = col // LANES
    return tile * rows + row, col - tile * LANES


def encode_cell(idx, rows, cols):
    line, lane = split_lines(idx, rows, cols)
    return (lane + LANES).astype(F32) * jnp.exp2((line - 36).astype(F32))


def decode_cell(code):
    top = jnp.floor(jnp.log2(code) + 0.003)
    lane = code * jnp.exp2(-top) * LANES - LANES + 0.5
    return (top + 29.0).astype(jnp.int32), lane.astype(jnp.int32)


def tiles(block):
    return jnp.concatenate([block[:, t : t + LANES] for t in range(0, block.shape[1], LANES)], axis=0)


def untile(block, rows):
    return jnp.concatenate([block[t : t + rows] for t in range(0, block.shape[0], rows)], axis=1)


def pack_kernel(split, state_hbm, dst_hbm, early_ref, state_ref, dst_ref, sems):
    copies = [
        pltpu.make_async_copy(dst_hbm, dst_ref, sems.at[0]),
        pltpu.make_async_copy(state_hbm, state_ref, sems.at[1]),
    ]
    for copy in copies:
        copy.start()
    copies[0].wait()
    _, levels, rows, cols = state_ref.shape
    groups, blocks, slots = dst_ref.shape
    for h in range(blocks):
        code = encode_cell(dst_ref[:, h, :], rows, cols).astype(BF)
        u, other = h // split, h % split
        for v in range(split):
            early_ref[u * split + v, other * groups : (other + 1) * groups, :] = code
    copies[1].wait()
    for h in range(blocks):
        early_ref[h, split * groups :, :] = tiles(state_ref[0, h]).astype(BF)


def gather_kernel(split, blocks, count_ref, surf_ref, src_ref, weight_ref, pick_ref, out_ref):
    _, _, rows, cols = surf_ref.shape
    peers, slots = src_ref.shape
    fc = split * out_ref.shape[1] // blocks
    each = fc // split * blocks
    lines = rows * cols // LANES
    half = -(-lines // 16) * 8
    shift = lines - half
    surface = [tiles(surf_ref[0, c]) for c in range(fc)]
    surface = jnp.concatenate([jnp.concatenate([x[:half], x[shift:]], axis=1) for x in surface], axis=0).astype(BF)
    lane = lax.broadcasted_iota(jnp.int32, (blocks, slots), 1)
    sub = lax.broadcasted_iota(jnp.int32, (blocks, slots), 0)
    spot = lax.broadcasted_iota(jnp.int32, (half, slots), 0)

    def step(g, carry):
        base = pl.multiple_of(g * blocks, blocks)
        line, col = split_lines(src_ref[pl.ds(base, blocks), :], rows, cols)
        upper = line >= half
        line = line - jnp.where(upper, shift, 0)
        col = col + jnp.where(upper, LANES, 0)
        found = []
        for i in range(0, blocks, 2):
            pick = jnp.concatenate([one_hot(2 * LANES, col[j : j + 1]) for j in (i, i + 1)], axis=1)
            values = jnp.dot(surface, pick, preferred_element_type=F32)
            for j in range(2):
                own = values[:, j * slots : (j + 1) * slots].reshape(fc, half, slots)
                own = jnp.where((spot == line[i + j : i + j + 1])[None], own, 0.0)
                found.append(jnp.sum(own.reshape(fc, half // 8, 8, slots), axis=1).reshape(fc * 8, slots))
        value = jnp.dot(pick_ref[...], jnp.concatenate(found, axis=0).astype(BF), preferred_element_type=F32)
        limit = jnp.zeros((blocks, slots), jnp.int32)
        for i in range(blocks):
            limit = jnp.where(sub == i, count_ref[base + i], limit)
        weight = jnp.where(lane < limit, weight_ref[pl.ds(base, blocks), :], 0.0)
        value = value * jnp.concatenate([weight] * fc, axis=0)
        for v in range(split):
            out_ref[g * split + v] = value[v * each : (v + 1) * each].astype(BF)
        return carry

    lax.fori_loop(0, peers // blocks, step, 0, unroll=16)


def circle_kernel(scale, early_ref, resp_ref, ahead_ref, back_ref, twiddle_ref, out_ref, line_ref, lane_ref):
    blocks, rows, cols = out_ref.shape
    start = early_ref.shape[1] - rows * cols // LANES
    for h in range(blocks):
        line_ref[h], lane_ref[h] = decode_cell(early_ref[h, :start].astype(F32))
    x = [untile(early_ref[h, start:].astype(F32), rows) for h in range(blocks)]
    incr = zonal_rows(x, resp_ref[0], resp_ref[1], ahead_ref, back_ref, twiddle_ref)
    for h in range(blocks):
        out_ref[h] = (incr[h] * scale).astype(BF)


def scatter_kernel(
    split, flag_ref, arrived_ref, early_ref, line_ref, lane_ref, part_ref, first_ref, second_ref, value_ref, acc_ref
):
    senders, each, slots = arrived_ref.shape
    blocks = early_ref.shape[0]
    fields, _, rows, cols = part_ref.shape
    groups = senders // split
    lines = rows * cols // LANES
    for s in range(senders):
        value_ref[s] = arrived_ref[s].astype(F32)
    acc_ref[...] = jnp.zeros_like(acc_ref)
    spot = lax.broadcasted_iota(jnp.int32, (lines, slots), 0)

    def step(pair, carry):
        for h in range(blocks):
            spread, pick = [], []
            for g in (2 * pair, 2 * pair + 1):
                for v in range(split):
                    at = v * groups + g
                    mask = spot == line_ref[h, pl.ds(at, 1), :]
                    vals = [
                        jnp.where(mask, value_ref[g * split + v, c * blocks + h : c * blocks + h + 1, :], 0.0)
                        for c in range(fields)
                    ]
                    spread.append(jnp.concatenate(vals, axis=0).astype(BF))
                    pick.append(one_hot(LANES, lane_ref[h, pl.ds(at, 1), :]))
            acc_ref[h] += lax.dot_general(
                jnp.concatenate(spread, axis=1),
                jnp.concatenate(pick, axis=1),
                (((1,), (1,)), ((), ())),
                preferred_element_type=F32,
            )
        return carry

    lax.fori_loop(0, groups // 2, step, 0, unroll=4)
    tops, bottoms = [], []
    for c in range(fields + 1):
        for h in range(blocks):
            if c < fields:
                x = untile(acc_ref[h, c * lines : (c + 1) * lines], rows)
                part_ref[c, h] = x
            else:
                x = untile(early_ref[h, senders:].astype(F32), rows)
            tops.append(x[:1])
            bottoms.append(x[rows - 1 :])
    top, bottom = jnp.concatenate(tops, axis=0), jnp.concatenate(bottoms, axis=0)
    odd = flag_ref[0] == 1
    first_ref[...] = jnp.where(odd, top, bottom).astype(BF)
    second_ref[...] = jnp.where(odd, bottom, top).astype(BF)


def part_kernel(scale, part_ref, resp_ref, ahead_ref, back_ref, twiddle_ref, out_ref):
    blocks, fields, rows, cols = out_ref.shape
    for c in range(fields):
        x = [part_ref[c, h] for h in range(blocks)]
        incr = zonal_rows(x, resp_ref[c, 0], resp_ref[c, 1], ahead_ref, back_ref, twiddle_ref)
        for h in range(blocks):
            out_ref[h, c] = (incr[h] * scale + x[h]).astype(BF)


def edge_kernel(
    scale, flag_ref, first_ref, second_ref, part_ref, circle_ref, resp_ref, ahead_ref, back_ref, twiddle_ref, out_ref
):
    blocks, fields, rows, cols = part_ref.shape
    sets = fields + 1
    odd = flag_ref[0] == 1
    first, second = first_ref[...].astype(F32), second_ref[...].astype(F32)
    low, high = jnp.where(odd, first, second), jnp.where(odd, second, first)
    x = []
    blank = jnp.zeros((8 - 2 * sets, cols), F32)
    for h in range(blocks):
        lines = [side[c * blocks + h : c * blocks + h + 1] for c in range(sets) for side in (low, high)]
        x.append(jnp.concatenate(lines + [blank], axis=0))
    zero = jnp.zeros((8 - 2 * sets, resp_ref.shape[3]), F32)
    resp = [
        [
            jnp.concatenate([resp_ref[c, k, r : r + 1, :] for c in range(sets) for _ in range(2)] + [zero], axis=0)
            for r in range(blocks)
        ]
        for k in range(2)
    ]
    incr = zonal_rows(x, resp[0], resp[1], ahead_ref, back_ref, twiddle_ref)
    for h in range(blocks):
        for c in range(fields):
            out_ref[h, c * rows : (c + 1) * rows] = part_ref[h, c]
        out_ref[h, fields * rows : sets * rows] = circle_ref[h]
        out_ref[h, sets * rows :] = (incr[h] * scale + x[h]).astype(BF)


def final_kernel(split, flag_ref, state_ref, back_ref, rate_ref, land_ref, out_ref):
    _, levels, rows, cols = state_ref.shape
    sets = (back_ref.shape[1] - 8) // rows
    fields = sets - 1
    keep = jnp.where(flag_ref[1] == 1, land_ref[...].astype(F32), 1.0)
    rate = rate_ref[0] * keep
    edges = [back_ref[z, sets * rows :].astype(F32) for z in range(levels)]
    for c in range(levels):
        own = state_ref[0, c] + back_ref[c, fields * rows : sets * rows].astype(F32)
        low, high = edges[c][2 * fields : 2 * fields + 1], edges[c][2 * fields + 1 : 2 * fields + 2]
        if c < split * fields:
            at = c % fields
            for u in range(levels // split):
                z = u * split + c // fields
                own = own + back_ref[z, at * rows : (at + 1) * rows].astype(F32)
                low = low + edges[z][2 * at : 2 * at + 1]
                high = high + edges[z][2 * at + 1 : 2 * at + 2]
        above = jnp.concatenate([low, own[: rows - 1]], axis=0)
        below = jnp.concatenate([own[1:], high], axis=0)
        out_ref[0, c] = own * keep + rate * (above + below - 2.0 * own)


def zonal_tables(blocks, cols, waves):
    total = blocks * cols
    b = np.arange(cols)
    n = np.arange(total // 2 // blocks)
    angle = 2.0 * np.pi * ((b[:, None] * n[None, :]) % cols) / cols
    pad = ((0, 0), (0, waves - len(n)))
    cos, sin = np.pad(np.cos(angle), pad), np.pad(np.sin(angle), pad)
    ahead = np.concatenate([cos, sin], axis=1)
    back = np.concatenate([cos.T, sin.T], axis=1)
    turn = 2.0 * np.pi * np.arange(blocks)[:, None] * b[None, :] / total
    twiddle = np.stack([np.cos(turn), np.sin(turn)])
    return jnp.asarray(ahead, BF), jnp.asarray(back, BF), jnp.asarray(twiddle, F32)


def response_row(resp, r):
    return resp[r] if isinstance(resp, list) else resp[r : r + 1, :]


def zonal_rows(x, resp_cos, resp_sin, ahead_ref, back_ref, twiddle_ref):
    blocks = len(x)
    rows, cols = x[0].shape
    waves = ahead_ref.shape[1] // 2
    half = math.sqrt(0.5)
    a = [x[i] + x[i + 4] for i in range(4)]
    b = [x[i] - x[i + 4] for i in range(4)]
    b13, d13 = half * (b[1] + b[3]), half * (b[1] - b[3])
    a02, a13 = a[0] + a[2], a[1] + a[3]
    z1 = (b[0] + d13, -(b[2] + b13))
    z2 = (a[0] - a[2], a[3] - a[1])
    z3 = (b[0] - d13, b[2] - b13)
    z = [(a02 + a13, None), z1, z2, z3, (a02 - a13, None)]
    z += [(re, -im) for re, im in (z3, z2, z1)]
    real, imag = [], []
    for r in range(blocks):
        re, im = z[r]
        ct, st = twiddle_ref[0, r : r + 1, :], twiddle_ref[1, r : r + 1, :]
        if r == 0:
            real.append(re)
        elif im is None:
            real.append(re * ct)
            imag.append(-re * st)
        else:
            real.append(re * ct + im * st)
            imag.append(im * ct - re * st)
    spec = jnp.dot(jnp.concatenate(real + imag, axis=0).astype(BF), ahead_ref[...], preferred_element_type=F32)
    cosine, sine = [], []
    for r in range(blocks):
        own = spec[r * rows : (r + 1) * rows]
        c, s = own[:, :waves], own[:, waves:]
        if r > 0:
            other = spec[(blocks + r - 1) * rows : (blocks + r) * rows]
            c, s = c + other[:, waves:], s - other[:, :waves]
        cosine.append(c * response_row(resp_cos, r))
        sine.append(s * response_row(resp_sin, r))
    full = jnp.dot(jnp.concatenate(cosine + sine, axis=0).astype(BF), back_ref[...], preferred_element_type=F32)
    u = []
    for r in range(blocks):
        fc = full[r * rows : (r + 1) * rows]
        fs = full[(blocks + r) * rows : (blocks + r + 1) * rows]
        re, im = fc[:, :cols] + fs[:, cols:], fc[:, cols:] - fs[:, :cols]
        ct, st = twiddle_ref[0, r : r + 1, :], twiddle_ref[1, r : r + 1, :]
        u.append((re, None) if r == 0 else (re * ct - im * st, re * st + im * ct))
    even, odd = u[0][0] + u[4][0], u[0][0] - u[4][0]
    p1, q1 = u[1][0] + u[7][0], u[1][1] - u[7][1]
    p2, q2 = u[2][0] + u[6][0], u[2][1] - u[6][1]
    p3, q3 = u[3][0] + u[5][0], u[3][1] - u[5][1]
    m1, n1 = half * (p1 - q1), half * (p1 + q1)
    m3, n3 = half * (p3 - q3), half * (p3 + q3)
    return [
        even + p1 + p2 + p3,
        odd + m1 - q2 - n3,
        even - q1 - p2 + q3,
        odd - n1 + q2 + m3,
        even - p1 + p2 - p3,
        odd - m1 - q2 + n3,
        even + q1 - p2 - q3,
        odd + n1 + q2 - m3,
    ]


def cost(micros):
    return pl.CostEstimate(flops=micros * 10**9, bytes_accessed=micros * 3 * 10**6, transcendentals=0)


def local(
    state, response, diffusion, land_mask, couple_src, couple_dst, couple_weight, couple_count
):
    levels, rows, cols = (state.shape[1], state.shape[2], state.shape[3])
    groups_x, split = lax.axis_size("gx"), lax.axis_size("gv")
    blocks = lax.axis_size("gu") * split
    peers = groups_x * blocks
    slots = couple_src.shape[4]
    cols_all = cols * blocks
    senders = groups_x * split
    each = FC // split
    cell_rows = rows * cols // LANES
    waves = 256
    gv = lax.axis_index("gv")
    own = lax.axis_index("gu") * split + gv
    src_idx = couple_src.reshape(peers, slots)
    weight = couple_weight.reshape(peers, slots)
    count = couple_count.reshape(peers)

    early = pl.pallas_call(
        functools.partial(pack_kernel, split),
        out_shape=jax.ShapeDtypeStruct((blocks, senders + cell_rows, LANES), BF),
        in_specs=[HBM] * 2,
        out_specs=VMEM,
        scratch_shapes=[
            pltpu.VMEM(state.shape, F32),
            pltpu.VMEM((groups_x, blocks, slots), jnp.int32),
            pltpu.SemaphoreType.DMA((2,)),
        ],
        compiler_params=LARGE,
        cost_estimate=cost(1),
        name="early_pack",
    )(state, couple_dst.reshape(groups_x, blocks, slots))
    src_idx, early = lax.optimization_barrier((src_idx, early))
    early = lax.all_to_all(early, ("gu", "gv"), split_axis=0, concat_axis=0, tiled=True)

    spot = np.zeros((FC, blocks, blocks, FC, 8), np.float32)
    for c in range(FC):
        for h in range(blocks):
            spot[c, h, h, c] = 1.0
    outgoing = pl.pallas_call(
        functools.partial(gather_kernel, split, blocks),
        out_shape=jax.ShapeDtypeStruct((senders, each * blocks, slots), BF),
        in_specs=[SMEM, VMEM, VMEM, VMEM, VMEM],
        out_specs=VMEM,
        compiler_params=PARAMS,
        cost_estimate=cost(4),
        name="couple_gather",
    )(count, state, src_idx, weight, jnp.asarray(spot.reshape(FC * blocks, -1), BF))
    crossed = lax.ppermute(outgoing, "comp", [(0, 1), (1, 0)])
    crossed, early = lax.optimization_barrier((crossed, early))
    arrived = lax.all_to_all(crossed, ("gx", "gv"), split_axis=0, concat_axis=0, tiled=True)

    ahead, back, twiddle = zonal_tables(blocks, cols, waves)
    half = cols_all // 2 // blocks
    resp = jnp.concatenate(
        [lax.dynamic_slice_in_dim(response[0], gv * each, each, 0), lax.dynamic_slice_in_dim(response[0], own, 1, 0)], axis=0
    )
    resp = resp.reshape(each + 1, 2, half, blocks).transpose(0, 1, 3, 2)
    resp = jnp.pad(resp, ((0, 0), (0, 0), (0, 0), (0, waves - half)))
    scale = 2.0 / cols_all
    flag = jnp.stack([lax.axis_index("gx") % 2, lax.axis_index("comp")])

    index = jax.ShapeDtypeStruct((blocks, senders, slots), jnp.int32)
    circle, line, lane = pl.pallas_call(
        functools.partial(circle_kernel, scale),
        out_shape=(jax.ShapeDtypeStruct((blocks, rows, cols), BF), index, index),
        in_specs=[VMEM] * 5,
        out_specs=(VMEM, VMEM, VMEM),
        compiler_params=PARAMS,
        cost_estimate=cost(2),
        name="circle_filter",
    )(early, resp[each], ahead, back, twiddle)
    edge = jax.ShapeDtypeStruct(((each + 1) * blocks, cols), BF)
    part, first, second = pl.pallas_call(
        functools.partial(scatter_kernel, split),
        out_shape=(jax.ShapeDtypeStruct((each, blocks, rows, cols), F32), edge, edge),
        in_specs=[SMEM] + [VMEM] * 4,
        out_specs=(VMEM, VMEM, VMEM),
        scratch_shapes=[
            pltpu.VMEM((senders, each * blocks, slots), F32),
            pltpu.VMEM((blocks, each * cell_rows, LANES), F32),
        ],
        compiler_params=PARAMS,
        cost_estimate=cost(4),
        name="couple_scatter",
    )(flag, arrived, early, line, lane)
    pairs = [(i, i ^ 1) for i in range(groups_x)]
    cross = [pair for i in range(1, groups_x - 1, 2) for pair in ((i, i + 1), (i + 1, i))]
    first = lax.ppermute(first, "gx", pairs)
    second = lax.ppermute(second, "gx", cross)
    part = pl.pallas_call(
        functools.partial(part_kernel, scale),
        out_shape=jax.ShapeDtypeStruct((blocks, each, rows, cols), BF),
        in_specs=[VMEM] * 5,
        out_specs=VMEM,
        compiler_params=PARAMS,
        cost_estimate=cost(3),
        name="part_filter",
    )(part, resp, ahead, back, twiddle)
    incr = pl.pallas_call(
        functools.partial(edge_kernel, scale),
        out_shape=jax.ShapeDtypeStruct((blocks, (each + 1) * rows + 8, cols), BF),
        in_specs=[SMEM] + [VMEM] * 8,
        out_specs=VMEM,
        compiler_params=PARAMS,
        cost_estimate=cost(1),
        name="edge_filter",
    )(flag, first, second, part, circle, resp, ahead, back, twiddle)
    incr = lax.all_to_all(incr, ("gu", "gv"), split_axis=0, concat_axis=0, tiled=True)
    return pl.pallas_call(
        functools.partial(final_kernel, split),
        out_shape=jax.ShapeDtypeStruct((1, levels, rows, cols), F32),
        in_specs=[SMEM] + [VMEM] * 4,
        out_specs=VMEM,
        compiler_params=PARAMS,
        cost_estimate=cost(1),
        name="final_step",
    )(flag, state, incr, diffusion, land_mask)


def solution(mesh):
    shape = mesh.devices.shape
    mesh = jax.sharding.Mesh(mesh.devices.reshape(shape[0], shape[1], shape[2] // 2, 2), ("comp", "gx", "gu", "gv"))
    gy = ("gu", "gv")
    return jax.shard_map(
        local,
        mesh=mesh,
        in_specs=(
            P("comp", None, "gx", gy),
            P("comp", None, None),
            P("comp", "gx", gy),
            P("gx", gy),
            P("comp", "gx", gy, None, None),
            P("comp", "gx", gy, None, None),
            P("comp", "gx", gy, None, None),
            P("comp", "gx", gy, None),
        ),
        out_specs=P("comp", None, "gx", gy),
        check_vma=False,
    )
```

```python
import functools
import math

import jax
import jax.numpy as jnp
import numpy as np
from jax import lax
from jax.experimental import pallas as pl
from jax.experimental.pallas import tpu as pltpu
from jax.sharding import PartitionSpec as P

FC = 4
LANES = 128
BF = jnp.bfloat16
F32 = jnp.float32
VMEM = pl.BlockSpec(memory_space=pltpu.VMEM)
SMEM = pl.BlockSpec(memory_space=pltpu.SMEM)
HBM = pl.BlockSpec(memory_space=pltpu.HBM)
LARGE = pltpu.CompilerParams(vmem_limit_bytes=60 * 2**20)
PARAMS = pltpu.CompilerParams(vmem_limit_bytes=32 * 2**20)


def one_hot(rows, index):
    spot = lax.broadcasted_iota(jnp.int16, (rows, index.shape[1]), 0)
    return jnp.where(spot == index.astype(jnp.int16), jnp.asarray(1, BF), jnp.asarray(0, BF))


def split_cell(idx, cols):
    row = (idx.astype(F32) * (1.0 / cols) + 0.5 / cols).astype(jnp.int32)
    return row, idx - row * cols


def split_lines(idx, rows, cols):
    row, col = split_cell(idx, cols)
    tile = col // LANES
    return tile * rows + row, col - tile * LANES


def encode_cell(idx, rows, cols):
    line, lane = split_lines(idx, rows, cols)
    return (lane + LANES).astype(F32) * jnp.exp2((line - 36).astype(F32))


def decode_cell(code):
    top = jnp.floor(jnp.log2(code) + 0.003)
    lane = code * jnp.exp2(-top) * LANES - LANES + 0.5
    return (top + 29.0).astype(jnp.int32), lane.astype(jnp.int32)


def tiles(block):
    return jnp.concatenate([block[:, t : t + LANES] for t in range(0, block.shape[1], LANES)], axis=0)


def untile(block, rows):
    return jnp.concatenate([block[t : t + rows] for t in range(0, block.shape[0], rows)], axis=1)


def pack_kernel(split, state_hbm, dst_hbm, early_ref, state_ref, dst_ref, sems):
    copies = [
        pltpu.make_async_copy(dst_hbm, dst_ref, sems.at[0]),
        pltpu.make_async_copy(state_hbm.at[0, FC:], state_ref, sems.at[1]),
    ]
    for copy in copies:
        copy.start()
    copies[0].wait()
    levels, rows, cols = state_ref.shape
    groups, blocks, slots = dst_ref.shape
    senders, own_rows = split * groups, rows * levels // blocks
    for h in range(blocks):
        code = encode_cell(dst_ref[:, h, :], rows, cols).astype(BF)
        u, other = h // split, h % split
        for v in range(split):
            early_ref[u * split + v, other * groups : (other + 1) * groups, :] = code
    copies[1].wait()
    for z in range(blocks):
        u, v = z // split, z % split
        early_ref[z, senders:, :] = tiles(state_ref[u, v * own_rows : (v + 1) * own_rows, :]).astype(BF)


def gather_kernel(split, blocks, surf_ref, src_ref, weight_ref, pick_ref, out_ref):
    _, _, rows, cols = surf_ref.shape
    peers, slots = src_ref.shape
    fc = split * out_ref.shape[1] // blocks
    each = fc // split * blocks
    lines = rows * cols // LANES
    half = -(-lines // 16) * 8
    shift = lines - half
    surface = [tiles(surf_ref[0, c]) for c in range(fc)]
    surface = jnp.concatenate([jnp.concatenate([x[:half], x[shift:]], axis=1) for x in surface], axis=0).astype(BF)
    spot = lax.broadcasted_iota(jnp.int32, (half, slots), 0)

    def step(g, carry):
        base = pl.multiple_of(g * blocks, blocks)
        line, col = split_lines(src_ref[pl.ds(base, blocks), :], rows, cols)
        upper = line >= half
        line = line - jnp.where(upper, shift, 0)
        col = col + jnp.where(upper, LANES, 0)
        found = []
        for i in range(0, blocks, 2):
            pick = jnp.concatenate([one_hot(2 * LANES, col[j : j + 1]) for j in (i, i + 1)], axis=1)
            values = jnp.dot(surface, pick, preferred_element_type=F32)
            for j in range(2):
                own = values[:, j * slots : (j + 1) * slots].reshape(fc, half, slots)
                own = jnp.where((spot == line[i + j : i + j + 1])[None], own, 0.0)
                found.append(jnp.sum(own.reshape(fc, half // 8, 8, slots), axis=1).reshape(fc * 8, slots))
        value = jnp.dot(pick_ref[...], jnp.concatenate(found, axis=0).astype(BF), preferred_element_type=F32)
        weight = weight_ref[pl.ds(base, blocks), :]
        value = value * jnp.concatenate([weight] * fc, axis=0)
        for v in range(split):
            out_ref[g * split + v] = value[v * each : (v + 1) * each].astype(BF)
        return carry

    lax.fori_loop(0, peers // blocks, step, 0, unroll=16)


def circle_kernel(scale, early_ref, resp_ref, ahead_ref, back_ref, twiddle_ref, x_ref, incr_ref, line_ref, lane_ref):
    blocks, frame, cols = x_ref.shape
    senders = line_ref.shape[1]
    rows = (early_ref.shape[1] - senders) * LANES // cols
    blank = jnp.zeros((frame - rows, cols), F32)
    x = []
    for h in range(blocks):
        code = early_ref[h].astype(F32)
        line_ref[h], lane_ref[h] = decode_cell(code[:senders])
        x.append(jnp.concatenate([untile(code[senders:], rows), blank], axis=0))
        x_ref[h] = x[h]
    incr = zonal_rows(x, resp_ref[0], resp_ref[1], ahead_ref, back_ref, twiddle_ref)
    for h in range(blocks):
        incr_ref[h] = incr[h] * scale


def scatter_kernel(
    split, flag_ref, arrived_ref, circle_ref, line_ref, lane_ref, state_ref, mate_ref, part_ref, x_ref, first_ref, second_ref, value_ref, acc_ref
):
    senders, each, slots = arrived_ref.shape
    blocks = circle_ref.shape[0]
    fields, _, rows, cols = part_ref.shape
    last = rows * (state_ref.shape[1] - split * fields) // blocks - 1
    groups = senders // split
    lines = rows * cols // LANES
    for s in range(senders):
        value_ref[s] = arrived_ref[s].astype(F32)
    acc_ref[...] = jnp.zeros_like(acc_ref)
    spot = lax.broadcasted_iota(jnp.int32, (lines, slots), 0)

    def step(pair, carry):
        for h in range(blocks):
            spread, pick = [], []
            for g in (2 * pair, 2 * pair + 1):
                for v in range(split):
                    at = v * groups + g
                    mask = spot == line_ref[h, pl.ds(at, 1), :]
                    vals = [
                        jnp.where(mask, value_ref[g * split + v, c * blocks + h : c * blocks + h + 1, :], 0.0)
                        for c in range(fields)
                    ]
                    spread.append(jnp.concatenate(vals, axis=0).astype(BF))
                    pick.append(one_hot(LANES, lane_ref[h, pl.ds(at, 1), :]))
            acc_ref[h] += lax.dot_general(
                jnp.concatenate(spread, axis=1),
                jnp.concatenate(pick, axis=1),
                (((1,), (1,)), ((), ())),
                preferred_element_type=F32,
            )
        return carry

    lax.fori_loop(0, groups // 2, step, 0, unroll=4)
    own = flag_ref[2]
    first_level = lax.rem(own, split) * fields
    for c in range(fields):
        for h in range(blocks):
            x = untile(acc_ref[h, c * lines : (c + 1) * lines], rows)
            part_ref[c, h] = x
            x_ref[c, h] = x
        x_ref[c, own] += state_ref[0, first_level + c]
        x_ref[c, flag_ref[3]] += mate_ref[c].astype(F32)
    tops, bottoms = [], []
    for c in range(fields):
        for h in range(blocks):
            tops.append(x_ref[c, h, :1, :])
            bottoms.append(x_ref[c, h, rows - 1 :, :])
    for h in range(blocks):
        tops.append(circle_ref[h, :1, :])
        bottoms.append(circle_ref[h, last : last + 1, :])
    top, bottom = jnp.concatenate(tops, axis=0), jnp.concatenate(bottoms, axis=0)
    odd = flag_ref[0] == 1
    first_ref[...] = jnp.where(odd, top, bottom).astype(BF)
    second_ref[...] = jnp.where(odd, bottom, top).astype(BF)


def part_kernel(scale, part_ref, x_ref, resp_ref, ahead_ref, back_ref, twiddle_ref, out_ref):
    blocks, fields, rows, cols = out_ref.shape
    for c in range(fields):
        x = [x_ref[c, h] for h in range(blocks)]
        incr = zonal_rows(x, resp_ref[c, 0], resp_ref[c, 1], ahead_ref, back_ref, twiddle_ref)
        for h in range(blocks):
            out_ref[h, c] = (incr[h] * scale + part_ref[c, h]).astype(BF)


def edge_kernel(
    scale, flag_ref, first_ref, second_ref, part_ref, circle_ref, resp_ref, ahead_ref, back_ref, twiddle_ref, out_ref
):
    blocks, fields, rows, cols = part_ref.shape
    sets = fields + 1
    odd = flag_ref[0] == 1
    first, second = first_ref[...].astype(F32), second_ref[...].astype(F32)
    low, high = jnp.where(odd, first, second), jnp.where(odd, second, first)
    x = []
    blank = jnp.zeros((8 - 2 * sets, cols), F32)
    for h in range(blocks):
        lines = [side[c * blocks + h : c * blocks + h + 1] for c in range(sets) for side in (low, high)]
        x.append(jnp.concatenate(lines + [blank], axis=0))
    zero = jnp.zeros((8 - 2 * sets, resp_ref.shape[3]), F32)
    resp = [
        [
            jnp.concatenate([resp_ref[c, k, r : r + 1, :] for c in range(sets) for _ in range(2)] + [zero], axis=0)
            for r in range(blocks)
        ]
        for k in range(2)
    ]
    incr = zonal_rows(x, resp[0], resp[1], ahead_ref, back_ref, twiddle_ref)
    more = out_ref.shape[1] - fields * rows
    for h in range(blocks):
        for c in range(fields):
            out_ref[h, c * rows : (c + 1) * rows] = part_ref[h, c]
        tail = [circle_ref[h, : more - 2 * sets], (incr[h] * scale + x[h])[: 2 * sets]]
        out_ref[h, fields * rows :] = jnp.concatenate(tail, axis=0).astype(BF)


def final_kernel(split, fields, flag_ref, state_ref, back_ref, rate_ref, land_ref, out_ref):
    _, levels, rows, cols = state_ref.shape
    blocks = back_ref.shape[0]
    coupled = split * fields
    start = fields * rows
    more = rows * (levels - coupled) // blocks
    keep = jnp.where(flag_ref[1] == 1, land_ref[...].astype(F32), 1.0)
    rate = rate_ref[0] * keep
    tail = [back_ref[z, start:].astype(F32) for z in range(blocks)]
    edge = lambda z, k: tail[z][more + k : more + k + 1]
    for c in range(levels):
        own = state_ref[0, c]
        if c < coupled:
            at = c % fields
            zs = [u * split + c // fields for u in range(blocks // split)]
            for z in zs:
                own = own + back_ref[z, at * rows : (at + 1) * rows].astype(F32)
            low = sum(edge(z, 2 * at) for z in zs)
            high = sum(edge(z, 2 * at + 1) for z in zs)
        else:
            zs = [(c - coupled) * split + v for v in range(split)]
            own = own + jnp.concatenate([tail[z][:more] for z in zs], axis=0)
            low, high = edge(zs[-1], 2 * fields), edge(zs[0], 2 * fields + 1)
        above = jnp.concatenate([low, own[: rows - 1]], axis=0)
        below = jnp.concatenate([own[1:], high], axis=0)
        out_ref[0, c] = own * keep + rate * (above + below - 2.0 * own)


def zonal_tables(blocks, cols, waves):
    total = blocks * cols
    b = np.arange(cols)
    n = np.arange(total // 2 // blocks)
    angle = 2.0 * np.pi * ((b[:, None] * n[None, :]) % cols) / cols
    pad = ((0, 0), (0, waves - len(n)))
    cos, sin = np.pad(np.cos(angle), pad), np.pad(np.sin(angle), pad)
    ahead = np.concatenate([cos, sin], axis=1)
    back = np.concatenate([cos.T, sin.T], axis=1)
    turn = 2.0 * np.pi * np.arange(blocks)[:, None] * b[None, :] / total
    twiddle = np.stack([np.cos(turn), np.sin(turn)])
    return jnp.asarray(ahead, BF), jnp.asarray(back, BF), jnp.asarray(twiddle, F32)


def response_row(resp, r):
    return resp[r] if isinstance(resp, list) else resp[r : r + 1, :]


def zonal_rows(x, resp_cos, resp_sin, ahead_ref, back_ref, twiddle_ref):
    blocks = len(x)
    rows, cols = x[0].shape
    waves = ahead_ref.shape[1] // 2
    half = math.sqrt(0.5)
    a = [x[i] + x[i + 4] for i in range(4)]
    b = [x[i] - x[i + 4] for i in range(4)]
    b13, d13 = half * (b[1] + b[3]), half * (b[1] - b[3])
    a02, a13 = a[0] + a[2], a[1] + a[3]
    z1 = (b[0] + d13, -(b[2] + b13))
    z2 = (a[0] - a[2], a[3] - a[1])
    z3 = (b[0] - d13, b[2] - b13)
    z = [(a02 + a13, None), z1, z2, z3, (a02 - a13, None)]
    z += [(re, -im) for re, im in (z3, z2, z1)]
    real, imag = [], []
    for r in range(blocks):
        re, im = z[r]
        ct, st = twiddle_ref[0, r : r + 1, :], twiddle_ref[1, r : r + 1, :]
        if r == 0:
            real.append(re)
        elif im is None:
            real.append(re * ct)
            imag.append(-re * st)
        else:
            real.append(re * ct + im * st)
            imag.append(im * ct - re * st)
    spec = jnp.dot(jnp.concatenate(real + imag, axis=0).astype(BF), ahead_ref[...], preferred_element_type=F32)
    cosine, sine = [], []
    for r in range(blocks):
        own = spec[r * rows : (r + 1) * rows]
        c, s = own[:, :waves], own[:, waves:]
        if r > 0:
            other = spec[(blocks + r - 1) * rows : (blocks + r) * rows]
            c, s = c + other[:, waves:], s - other[:, :waves]
        cosine.append(c * response_row(resp_cos, r))
        sine.append(s * response_row(resp_sin, r))
    full = jnp.dot(jnp.concatenate(cosine + sine, axis=0).astype(BF), back_ref[...], preferred_element_type=F32)
    u = []
    for r in range(blocks):
        fc = full[r * rows : (r + 1) * rows]
        fs = full[(blocks + r) * rows : (blocks + r + 1) * rows]
        re, im = fc[:, :cols] + fs[:, cols:], fc[:, cols:] - fs[:, :cols]
        ct, st = twiddle_ref[0, r : r + 1, :], twiddle_ref[1, r : r + 1, :]
        u.append((re, None) if r == 0 else (re * ct - im * st, re * st + im * ct))
    even, odd = u[0][0] + u[4][0], u[0][0] - u[4][0]
    p1, q1 = u[1][0] + u[7][0], u[1][1] - u[7][1]
    p2, q2 = u[2][0] + u[6][0], u[2][1] - u[6][1]
    p3, q3 = u[3][0] + u[5][0], u[3][1] - u[5][1]
    m1, n1 = half * (p1 - q1), half * (p1 + q1)
    m3, n3 = half * (p3 - q3), half * (p3 + q3)
    return [
        even + p1 + p2 + p3,
        odd + m1 - q2 - n3,
        even - q1 - p2 + q3,
        odd - n1 + q2 + m3,
        even - p1 + p2 - p3,
        odd - m1 - q2 + n3,
        even + q1 - p2 - q3,
        odd + n1 + q2 - m3,
    ]


def cost(micros):
    return pl.CostEstimate(flops=micros * 10**9, bytes_accessed=micros * 3 * 10**6, transcendentals=0)


def local(
    state, response, diffusion, land_mask, couple_src, couple_dst, couple_weight, couple_count
):
    levels, rows, cols = (state.shape[1], state.shape[2], state.shape[3])
    groups_x, split = lax.axis_size("gx"), lax.axis_size("gv")
    blocks = lax.axis_size("gu") * split
    peers = groups_x * blocks
    slots = couple_src.shape[4]
    cols_all = cols * blocks
    senders = groups_x * split
    each = FC // split
    cell_rows = rows * cols // LANES
    waves = 256
    gv = lax.axis_index("gv")
    own = lax.axis_index("gu") * split + gv
    src_idx = couple_src.reshape(peers, slots)
    live = jnp.arange(slots, dtype=jnp.int32)[None, :] < couple_count.reshape(peers, 1)
    weight = jnp.where(live, couple_weight.reshape(peers, slots), jnp.float32(0.0))
    more = rows * (levels - FC) // blocks
    frame = -(-more // 8) * 8

    early = pl.pallas_call(
        functools.partial(pack_kernel, split),
        out_shape=jax.ShapeDtypeStruct((blocks, senders + more * cols // LANES, LANES), BF),
        in_specs=[HBM] * 2,
        out_specs=VMEM,
        scratch_shapes=[
            pltpu.VMEM((levels - FC, rows, cols), F32),
            pltpu.VMEM((groups_x, blocks, slots), jnp.int32),
            pltpu.SemaphoreType.DMA((2,)),
        ],
        compiler_params=LARGE,
        cost_estimate=cost(1),
        name="early_pack",
    )(state, couple_dst.reshape(groups_x, blocks, slots))
    src_idx, early = lax.optimization_barrier((src_idx, early))
    early = lax.all_to_all(early, ("gu", "gv"), split_axis=0, concat_axis=0, tiled=True)

    spot = np.zeros((FC, blocks, blocks, FC, 8), np.float32)
    for c in range(FC):
        for h in range(blocks):
            spot[c, h, h, c] = 1.0
    outgoing = pl.pallas_call(
        functools.partial(gather_kernel, split, blocks),
        out_shape=jax.ShapeDtypeStruct((senders, each * blocks, slots), BF),
        in_specs=[VMEM] * 4,
        out_specs=VMEM,
        compiler_params=PARAMS,
        cost_estimate=cost(4),
        name="couple_gather",
    )(state, src_idx, weight, jnp.asarray(spot.reshape(FC * blocks, -1), BF))
    crossed = lax.ppermute(outgoing, "comp", [(0, 1), (1, 0)])
    mate = lax.dynamic_slice_in_dim(state[0], (1 - gv) * each, each, 0).astype(BF)
    crossed, early, mate, response = lax.optimization_barrier((crossed, early, mate, response))
    mate = lax.ppermute(mate, "gv", [(0, 1), (1, 0)])
    arrived = lax.all_to_all(crossed, ("gx", "gv"), split_axis=0, concat_axis=0, tiled=True)

    ahead, back, twiddle = zonal_tables(blocks, cols, waves)
    half = cols_all // 2 // blocks
    resp = jnp.concatenate(
        [lax.dynamic_slice_in_dim(response[0], gv * each, each, 0), lax.dynamic_slice_in_dim(response[0], FC + lax.axis_index("gu"), 1, 0)], axis=0
    )
    resp = resp.reshape(each + 1, 2, half, blocks).transpose(0, 1, 3, 2)
    resp = jnp.pad(resp, ((0, 0), (0, 0), (0, 0), (0, waves - half)))
    scale = 2.0 / cols_all
    mate_block = own + 1 - 2 * gv
    flag = jnp.stack([lax.axis_index("gx") % 2, lax.axis_index("comp"), own, mate_block])

    index = jax.ShapeDtypeStruct((blocks, senders, slots), jnp.int32)
    framed = jax.ShapeDtypeStruct((blocks, frame, cols), F32)
    circle, circle_incr, line, lane = pl.pallas_call(
        functools.partial(circle_kernel, scale),
        out_shape=(framed, framed, index, index),
        in_specs=[VMEM] * 5,
        out_specs=(VMEM,) * 4,
        compiler_params=PARAMS,
        cost_estimate=cost(2),
        name="circle_filter",
    )(early, resp[each], ahead, back, twiddle)
    edge = jax.ShapeDtypeStruct(((each + 1) * blocks, cols), BF)
    part_shape = jax.ShapeDtypeStruct((each, blocks, rows, cols), F32)
    part, x, first, second = pl.pallas_call(
        functools.partial(scatter_kernel, split),
        out_shape=(part_shape, part_shape, edge, edge),
        in_specs=[SMEM] + [VMEM] * 6,
        out_specs=(VMEM,) * 4,
        scratch_shapes=[
            pltpu.VMEM((senders, each * blocks, slots), F32),
            pltpu.VMEM((blocks, each * cell_rows, LANES), F32),
        ],
        compiler_params=PARAMS,
        cost_estimate=cost(4),
        name="couple_scatter",
    )(flag, arrived, circle, line, lane, state, mate)
    pairs = [(i, i ^ 1) for i in range(groups_x)]
    cross = [pair for i in range(1, groups_x - 1, 2) for pair in ((i, i + 1), (i + 1, i))]
    first = lax.ppermute(first, "gx", pairs)
    second = lax.ppermute(second, "gx", cross)
    part = pl.pallas_call(
        functools.partial(part_kernel, scale),
        out_shape=jax.ShapeDtypeStruct((blocks, each, rows, cols), BF),
        in_specs=[VMEM] * 6,
        out_specs=VMEM,
        compiler_params=PARAMS,
        cost_estimate=cost(3),
        name="part_filter",
    )(part, x, resp, ahead, back, twiddle)
    incr = pl.pallas_call(
        functools.partial(edge_kernel, scale),
        out_shape=jax.ShapeDtypeStruct((blocks, each * rows + more + 2 * (each + 1), cols), BF),
        in_specs=[SMEM] + [VMEM] * 8,
        out_specs=VMEM,
        compiler_params=PARAMS,
        cost_estimate=cost(1),
        name="edge_filter",
    )(flag, first, second, part, circle_incr, resp, ahead, back, twiddle)
    incr = lax.all_to_all(incr, ("gu", "gv"), split_axis=0, concat_axis=0, tiled=True)
    return pl.pallas_call(
        functools.partial(final_kernel, split, each),
        out_shape=jax.ShapeDtypeStruct((1, levels, rows, cols), F32),
        in_specs=[SMEM] + [VMEM] * 4,
        out_specs=VMEM,
        compiler_params=PARAMS,
        cost_estimate=cost(1),
        name="final_step",
    )(flag, state, incr, diffusion, land_mask)


def solution(mesh):
    shape = mesh.devices.shape
    mesh = jax.sharding.Mesh(mesh.devices.reshape(shape[0], shape[1], shape[2] // 2, 2), ("comp", "gx", "gu", "gv"))
    gy = ("gu", "gv")
    return jax.shard_map(
        local,
        mesh=mesh,
        in_specs=(
            P("comp", None, "gx", gy),
            P("comp", None, None),
            P("comp", "gx", gy),
            P("gx", gy),
            P("comp", "gx", gy, None, None),
            P("comp", "gx", gy, None, None),
            P("comp", "gx", gy, None, None),
            P("comp", "gx", gy, None),
        ),
        out_specs=P("comp", None, "gx", gy),
        check_vma=False,
    )
```

```python
import functools
import math

import jax
import jax.numpy as jnp
import numpy as np
from jax import lax
from jax.experimental import pallas as pl
from jax.experimental.pallas import tpu as pltpu
from jax.sharding import PartitionSpec as P

FC = 4
LANES = 128
BF = jnp.bfloat16
F32 = jnp.float32
VMEM = pl.BlockSpec(memory_space=pltpu.VMEM)
HBM = pl.BlockSpec(memory_space=pltpu.HBM)
LARGE = pltpu.CompilerParams(vmem_limit_bytes=60 * 2**20)
PARAMS = pltpu.CompilerParams(vmem_limit_bytes=32 * 2**20)


def one_hot(rows, index):
    spot = lax.broadcasted_iota(jnp.int16, (rows, index.shape[1]), 0)
    return jnp.where(spot == index.astype(jnp.int16), jnp.asarray(1, BF), jnp.asarray(0, BF))


def split_cell(idx, cols):
    row = (idx.astype(F32) * (1.0 / cols) + 0.5 / cols).astype(jnp.int32)
    return row, idx - row * cols


def split_lines(idx, rows, cols):
    row, col = split_cell(idx, cols)
    tile = col // LANES
    return tile * rows + row, col - tile * LANES


def encode_cell(idx, rows, cols):
    line, lane = split_lines(idx, rows, cols)
    return (lane + LANES).astype(F32) * jnp.exp2((line - 36).astype(F32))


def decode_cell(code):
    top = jnp.floor(jnp.log2(code) + 0.003)
    lane = code * jnp.exp2(-top) * LANES - LANES + 0.5
    return (top + 29.0).astype(jnp.int32), lane.astype(jnp.int32)


def tiles(block):
    return jnp.concatenate([block[:, t : t + LANES] for t in range(0, block.shape[1], LANES)], axis=0)


def untile(block, rows):
    return jnp.concatenate([block[t : t + rows] for t in range(0, block.shape[0], rows)], axis=1)


def pack_kernel(split, state_hbm, dst_hbm, early_ref, state_ref, dst_ref, sems):
    copies = [
        pltpu.make_async_copy(dst_hbm, dst_ref, sems.at[0]),
        pltpu.make_async_copy(state_hbm.at[0, FC:], state_ref, sems.at[1]),
    ]
    for copy in copies:
        copy.start()
    copies[0].wait()
    levels, rows, cols = state_ref.shape
    groups, blocks, slots = dst_ref.shape
    senders, own_rows = split * groups, rows * levels // blocks
    for h in range(blocks):
        code = encode_cell(dst_ref[:, h, :], rows, cols).astype(BF)
        u, other = h // split, h % split
        for v in range(split):
            early_ref[u * split + v, other * groups : (other + 1) * groups, :] = code
    copies[1].wait()
    for z in range(blocks):
        u, v = z // split, z % split
        early_ref[z, senders:, :] = tiles(state_ref[u, v * own_rows : (v + 1) * own_rows, :]).astype(BF)


def gather_kernel(split, blocks, surf_ref, src_ref, weight_ref, pick_ref, out_ref):
    _, _, rows, cols = surf_ref.shape
    peers, slots = src_ref.shape
    fc = split * out_ref.shape[1] // blocks
    each = fc // split * blocks
    lines = rows * cols // LANES
    half = -(-lines // 16) * 8
    shift = lines - half
    surface = [tiles(surf_ref[0, c]) for c in range(fc)]
    surface = jnp.concatenate([jnp.concatenate([x[:half], x[shift:]], axis=1) for x in surface], axis=0).astype(BF)
    spot = lax.broadcasted_iota(jnp.int32, (half, slots), 0)

    def step(g, carry):
        base = pl.multiple_of(g * blocks, blocks)
        line, col = split_lines(src_ref[pl.ds(base, blocks), :], rows, cols)
        upper = line >= half
        line = line - jnp.where(upper, shift, 0)
        col = col + jnp.where(upper, LANES, 0)
        found = []
        for i in range(0, blocks, 2):
            pick = jnp.concatenate([one_hot(2 * LANES, col[j : j + 1]) for j in (i, i + 1)], axis=1)
            values = jnp.dot(surface, pick, preferred_element_type=F32)
            for j in range(2):
                own = values[:, j * slots : (j + 1) * slots].reshape(fc, half, slots)
                own = jnp.where((spot == line[i + j : i + j + 1])[None], own, 0.0)
                found.append(jnp.sum(own.reshape(fc, half // 8, 8, slots), axis=1).reshape(fc * 8, slots))
        value = jnp.dot(pick_ref[...], jnp.concatenate(found, axis=0).astype(BF), preferred_element_type=F32)
        weight = weight_ref[pl.ds(base, blocks), :]
        value = value * jnp.concatenate([weight] * fc, axis=0)
        for v in range(split):
            out_ref[g * split + v] = value[v * each : (v + 1) * each].astype(BF)
        return carry

    lax.fori_loop(0, peers // blocks, step, 0, unroll=16)


def circle_kernel(scale, early_ref, resp_ref, ahead_ref, back_ref, twiddle_ref, x_ref, incr_ref, line_ref, lane_ref):
    blocks, frame, cols = x_ref.shape
    senders = line_ref.shape[1]
    rows = (early_ref.shape[1] - senders) * LANES // cols
    blank = jnp.zeros((frame - rows, cols), F32)
    x = []
    for h in range(blocks):
        code = early_ref[h].astype(F32)
        line_ref[h], lane_ref[h] = decode_cell(code[:senders])
        x.append(jnp.concatenate([untile(code[senders:], rows), blank], axis=0))
        x_ref[h] = x[h]
    incr = zonal_rows(x, resp_ref[0], resp_ref[1], ahead_ref, back_ref, twiddle_ref)
    for h in range(blocks):
        incr_ref[h] = incr[h] * scale


def scatter_kernel(
    split, arrived_ref, circle_ref, line_ref, lane_ref, state_ref, mate_ref, part_ref, x_ref, first_ref, second_ref, value_ref, acc_ref
):
    senders, each, slots = arrived_ref.shape
    blocks = circle_ref.shape[0]
    fields, _, rows, cols = part_ref.shape
    last = rows * (state_ref.shape[1] - split * fields) // blocks - 1
    groups = senders // split
    lines = rows * cols // LANES
    for s in range(senders):
        value_ref[s] = arrived_ref[s].astype(F32)
    acc_ref[...] = jnp.zeros_like(acc_ref)
    spot = lax.broadcasted_iota(jnp.int32, (lines, slots), 0)

    def step(pair, carry):
        for h in range(blocks):
            spread, pick = [], []
            for g in (2 * pair, 2 * pair + 1):
                for v in range(split):
                    at = v * groups + g
                    mask = spot == line_ref[h, pl.ds(at, 1), :]
                    vals = [
                        jnp.where(mask, value_ref[g * split + v, c * blocks + h : c * blocks + h + 1, :], 0.0)
                        for c in range(fields)
                    ]
                    spread.append(jnp.concatenate(vals, axis=0).astype(BF))
                    pick.append(one_hot(LANES, lane_ref[h, pl.ds(at, 1), :]))
            acc_ref[h] += lax.dot_general(
                jnp.concatenate(spread, axis=1),
                jnp.concatenate(pick, axis=1),
                (((1,), (1,)), ((), ())),
                preferred_element_type=F32,
            )
        return carry

    lax.fori_loop(0, groups // 2, step, 0, unroll=4)
    gv = lax.axis_index("gv")
    own = lax.axis_index("gu") * split + gv
    first_level = gv * fields
    for c in range(fields):
        for h in range(blocks):
            x = untile(acc_ref[h, c * lines : (c + 1) * lines], rows)
            part_ref[c, h] = x
            x_ref[c, h] = x
        x_ref[c, own] += state_ref[0, first_level + c]
        x_ref[c, own + 1 - 2 * gv] += mate_ref[c].astype(F32)
    tops, bottoms = [], []
    for c in range(fields):
        for h in range(blocks):
            tops.append(x_ref[c, h, :1, :])
            bottoms.append(x_ref[c, h, rows - 1 :, :])
    for h in range(blocks):
        tops.append(circle_ref[h, :1, :])
        bottoms.append(circle_ref[h, last : last + 1, :])
    top, bottom = jnp.concatenate(tops, axis=0), jnp.concatenate(bottoms, axis=0)
    odd = lax.axis_index("gx") % 2 == 1
    first_ref[...] = jnp.where(odd, top, bottom).astype(BF)
    second_ref[...] = jnp.where(odd, bottom, top).astype(BF)


def part_kernel(scale, part_ref, x_ref, resp_ref, ahead_ref, back_ref, twiddle_ref, out_ref):
    blocks, fields, rows, cols = out_ref.shape
    for c in range(fields):
        x = [x_ref[c, h] for h in range(blocks)]
        incr = zonal_rows(x, resp_ref[c, 0], resp_ref[c, 1], ahead_ref, back_ref, twiddle_ref)
        for h in range(blocks):
            out_ref[h, c] = (incr[h] * scale + part_ref[c, h]).astype(BF)


def edge_kernel(
    scale, second_ref, first_ref, part_ref, circle_ref, resp_ref, ahead_ref, back_ref, twiddle_ref, out_ref
):
    blocks, fields, rows, cols = part_ref.shape
    sets = fields + 1
    odd = lax.axis_index("gx") % 2 == 1
    first, second = first_ref[...].astype(F32), second_ref[...].astype(F32)
    low, high = jnp.where(odd, first, second), jnp.where(odd, second, first)
    x = []
    blank = jnp.zeros((8 - 2 * sets, cols), F32)
    for h in range(blocks):
        lines = [side[c * blocks + h : c * blocks + h + 1] for c in range(sets) for side in (low, high)]
        x.append(jnp.concatenate(lines + [blank], axis=0))
    zero = jnp.zeros((8 - 2 * sets, resp_ref.shape[3]), F32)
    resp = [
        [
            jnp.concatenate([resp_ref[c, k, r : r + 1, :] for c in range(sets) for _ in range(2)] + [zero], axis=0)
            for r in range(blocks)
        ]
        for k in range(2)
    ]
    incr = zonal_rows(x, resp[0], resp[1], ahead_ref, back_ref, twiddle_ref)
    more = out_ref.shape[1] - fields * rows
    for h in range(blocks):
        for c in range(fields):
            out_ref[h, c * rows : (c + 1) * rows] = part_ref[h, c]
        tail = [circle_ref[h, : more - 2 * sets], (incr[h] * scale + x[h])[: 2 * sets]]
        out_ref[h, fields * rows :] = jnp.concatenate(tail, axis=0).astype(BF)


def final_kernel(split, fields, state_ref, back_ref, rate_ref, land_ref, out_hbm, out_ref, sems):
    _, levels, rows, cols = state_ref.shape
    blocks = back_ref.shape[0]
    coupled = split * fields
    start = fields * rows
    more = rows * (levels - coupled) // blocks
    keep = jnp.where(lax.axis_index("comp") == 1, land_ref[...].astype(F32), 1.0)
    rate = rate_ref[0] * keep
    tail = [back_ref[z, start:].astype(F32) for z in range(blocks)]
    edge = lambda z, k: tail[z][more + k : more + k + 1]
    copies = []
    for c in range(levels):
        own = state_ref[0, c]
        if c < coupled:
            at = c % fields
            zs = [u * split + c // fields for u in range(blocks // split)]
            for z in zs:
                own = own + back_ref[z, at * rows : (at + 1) * rows].astype(F32)
            low = sum(edge(z, 2 * at) for z in zs)
            high = sum(edge(z, 2 * at + 1) for z in zs)
        else:
            zs = [(c - coupled) * split + v for v in range(split)]
            own = own + jnp.concatenate([tail[z][:more] for z in zs], axis=0)
            low, high = edge(zs[-1], 2 * fields), edge(zs[0], 2 * fields + 1)
        above = jnp.concatenate([low, own[: rows - 1]], axis=0)
        below = jnp.concatenate([own[1:], high], axis=0)
        out_ref[c] = own * keep + rate * (above + below - 2.0 * own)
        copies.append(pltpu.make_async_copy(out_ref.at[c], out_hbm.at[0, c], sems.at[c]))
        copies[c].start()
    for copy in copies:
        copy.wait()


def zonal_tables(blocks, cols, waves):
    total = blocks * cols
    b = np.arange(cols)
    n = np.arange(total // 2 // blocks)
    angle = 2.0 * np.pi * ((b[:, None] * n[None, :]) % cols) / cols
    pad = ((0, 0), (0, waves - len(n)))
    cos, sin = np.pad(np.cos(angle), pad), np.pad(np.sin(angle), pad)
    ahead = np.concatenate([cos, sin], axis=1)
    back = np.concatenate([cos.T, sin.T], axis=1)
    turn = 2.0 * np.pi * np.arange(blocks)[:, None] * b[None, :] / total
    twiddle = np.stack([np.cos(turn), np.sin(turn)])
    return jnp.asarray(ahead, BF), jnp.asarray(back, BF), jnp.asarray(twiddle, F32)


def response_row(resp, r):
    return resp[r] if isinstance(resp, list) else resp[r : r + 1, :]


def zonal_rows(x, resp_cos, resp_sin, ahead_ref, back_ref, twiddle_ref):
    blocks = len(x)
    rows, cols = x[0].shape
    waves = ahead_ref.shape[1] // 2
    half = math.sqrt(0.5)
    a = [x[i] + x[i + 4] for i in range(4)]
    b = [x[i] - x[i + 4] for i in range(4)]
    b13, d13 = half * (b[1] + b[3]), half * (b[1] - b[3])
    a02, a13 = a[0] + a[2], a[1] + a[3]
    z1 = (b[0] + d13, -(b[2] + b13))
    z2 = (a[0] - a[2], a[3] - a[1])
    z3 = (b[0] - d13, b[2] - b13)
    z = [(a02 + a13, None), z1, z2, z3, (a02 - a13, None)]
    z += [(re, -im) for re, im in (z3, z2, z1)]
    real, imag = [], []
    for r in range(blocks):
        re, im = z[r]
        ct, st = twiddle_ref[0, r : r + 1, :], twiddle_ref[1, r : r + 1, :]
        if r == 0:
            real.append(re)
        elif im is None:
            real.append(re * ct)
            imag.append(-re * st)
        else:
            real.append(re * ct + im * st)
            imag.append(im * ct - re * st)
    spec = jnp.dot(jnp.concatenate(real + imag, axis=0).astype(BF), ahead_ref[...], preferred_element_type=F32)
    cosine, sine = [], []
    for r in range(blocks):
        own = spec[r * rows : (r + 1) * rows]
        c, s = own[:, :waves], own[:, waves:]
        if r > 0:
            other = spec[(blocks + r - 1) * rows : (blocks + r) * rows]
            c, s = c + other[:, waves:], s - other[:, :waves]
        cosine.append(c * response_row(resp_cos, r))
        sine.append(s * response_row(resp_sin, r))
    full = jnp.dot(jnp.concatenate(cosine + sine, axis=0).astype(BF), back_ref[...], preferred_element_type=F32)
    u = []
    for r in range(blocks):
        fc = full[r * rows : (r + 1) * rows]
        fs = full[(blocks + r) * rows : (blocks + r + 1) * rows]
        re, im = fc[:, :cols] + fs[:, cols:], fc[:, cols:] - fs[:, :cols]
        ct, st = twiddle_ref[0, r : r + 1, :], twiddle_ref[1, r : r + 1, :]
        u.append((re, None) if r == 0 else (re * ct - im * st, re * st + im * ct))
    even, odd = u[0][0] + u[4][0], u[0][0] - u[4][0]
    p1, q1 = u[1][0] + u[7][0], u[1][1] - u[7][1]
    p2, q2 = u[2][0] + u[6][0], u[2][1] - u[6][1]
    p3, q3 = u[3][0] + u[5][0], u[3][1] - u[5][1]
    m1, n1 = half * (p1 - q1), half * (p1 + q1)
    m3, n3 = half * (p3 - q3), half * (p3 + q3)
    return [
        even + p1 + p2 + p3,
        odd + m1 - q2 - n3,
        even - q1 - p2 + q3,
        odd - n1 + q2 + m3,
        even - p1 + p2 - p3,
        odd - m1 - q2 + n3,
        even + q1 - p2 - q3,
        odd + n1 + q2 - m3,
    ]


def cost(micros):
    return pl.CostEstimate(flops=micros * 10**9, bytes_accessed=micros * 3 * 10**6, transcendentals=0)


def local(
    state, response, diffusion, land_mask, couple_src, couple_dst, couple_weight, couple_count
):
    levels, rows, cols = (state.shape[1], state.shape[2], state.shape[3])
    groups_x, split = lax.axis_size("gx"), lax.axis_size("gv")
    blocks = lax.axis_size("gu") * split
    peers = groups_x * blocks
    slots = couple_src.shape[4]
    cols_all = cols * blocks
    senders = groups_x * split
    each = FC // split
    cell_rows = rows * cols // LANES
    waves = 256
    gv = lax.axis_index("gv")
    src_idx = couple_src.reshape(peers, slots)
    more = rows * (levels - FC) // blocks
    frame = -(-more // 8) * 8

    early = pl.pallas_call(
        functools.partial(pack_kernel, split),
        out_shape=jax.ShapeDtypeStruct((blocks, senders + more * cols // LANES, LANES), BF),
        in_specs=[HBM] * 2,
        out_specs=VMEM,
        scratch_shapes=[
            pltpu.VMEM((levels - FC, rows, cols), F32),
            pltpu.VMEM((groups_x, blocks, slots), jnp.int32),
            pltpu.SemaphoreType.DMA((2,)),
        ],
        compiler_params=LARGE,
        cost_estimate=cost(1),
        name="early_pack",
    )(state, couple_dst.reshape(groups_x, blocks, slots))
    after_pack, early = lax.optimization_barrier((lax.axis_index("gx"), early))
    live = jnp.arange(slots, dtype=jnp.int32)[None, :] + jnp.minimum(after_pack, 0) < couple_count.reshape(peers, 1)
    weight = jnp.where(live, couple_weight.reshape(peers, slots), jnp.float32(0.0))
    early = lax.all_to_all(early, ("gu", "gv"), split_axis=0, concat_axis=0, tiled=True)

    spot = np.zeros((FC, blocks, blocks, FC, 8), np.float32)
    for c in range(FC):
        for h in range(blocks):
            spot[c, h, h, c] = 1.0
    outgoing = pl.pallas_call(
        functools.partial(gather_kernel, split, blocks),
        out_shape=jax.ShapeDtypeStruct((senders, each * blocks, slots), BF),
        in_specs=[VMEM] * 4,
        out_specs=VMEM,
        compiler_params=PARAMS,
        cost_estimate=cost(4),
        name="couple_gather",
    )(state, src_idx, weight, jnp.asarray(spot.reshape(FC * blocks, -1), BF))
    crossed = lax.ppermute(outgoing, "comp", [(0, 1), (1, 0)])
    mate = lax.dynamic_slice_in_dim(state[0], (1 - gv) * each, each, 0).astype(BF)
    crossed, early, mate, response = lax.optimization_barrier((crossed, early, mate, response))
    mate = lax.ppermute(mate, "gv", [(0, 1), (1, 0)])
    arrived = lax.all_to_all(crossed, ("gx", "gv"), split_axis=0, concat_axis=0, tiled=True)

    ahead, back, twiddle = zonal_tables(blocks, cols, waves)
    half = cols_all // 2 // blocks
    resp = jnp.concatenate(
        [lax.dynamic_slice_in_dim(response[0], gv * each, each, 0), lax.dynamic_slice_in_dim(response[0], FC + lax.axis_index("gu"), 1, 0)], axis=0
    )
    resp = resp.reshape(each + 1, 2, half, blocks).transpose(0, 1, 3, 2)
    resp = jnp.pad(resp, ((0, 0), (0, 0), (0, 0), (0, waves - half)))
    scale = 2.0 / cols_all

    index = jax.ShapeDtypeStruct((blocks, senders, slots), jnp.int32)
    framed = jax.ShapeDtypeStruct((blocks, frame, cols), F32)
    circle, circle_incr, line, lane = pl.pallas_call(
        functools.partial(circle_kernel, scale),
        out_shape=(framed, framed, index, index),
        in_specs=[VMEM] * 5,
        out_specs=(VMEM,) * 4,
        compiler_params=PARAMS,
        cost_estimate=cost(2),
        name="circle_filter",
    )(early, resp[each], ahead, back, twiddle)
    edge = jax.ShapeDtypeStruct(((each + 1) * blocks, cols), BF)
    part_shape = jax.ShapeDtypeStruct((each, blocks, rows, cols), F32)
    part, x, first, second = pl.pallas_call(
        functools.partial(scatter_kernel, split),
        out_shape=(part_shape, part_shape, edge, edge),
        in_specs=[VMEM] * 6,
        out_specs=(VMEM,) * 4,
        scratch_shapes=[
            pltpu.VMEM((senders, each * blocks, slots), F32),
            pltpu.VMEM((blocks, each * cell_rows, LANES), F32),
        ],
        compiler_params=PARAMS,
        cost_estimate=cost(4),
        name="couple_scatter",
    )(arrived, circle, line, lane, state, mate)
    pairs = [(i, i ^ 1) for i in range(groups_x)]
    cross = [pair for i in range(1, groups_x - 1, 2) for pair in ((i, i + 1), (i + 1, i))]
    second = lax.ppermute(second, "gx", cross)
    first = lax.ppermute(first, "gx", pairs)
    part = pl.pallas_call(
        functools.partial(part_kernel, scale),
        out_shape=jax.ShapeDtypeStruct((blocks, each, rows, cols), BF),
        in_specs=[VMEM] * 6,
        out_specs=VMEM,
        compiler_params=PARAMS,
        cost_estimate=cost(3),
        name="part_filter",
    )(part, x, resp, ahead, back, twiddle)
    incr = pl.pallas_call(
        functools.partial(edge_kernel, scale),
        out_shape=jax.ShapeDtypeStruct((blocks, each * rows + more + 2 * (each + 1), cols), BF),
        in_specs=[VMEM] * 8,
        out_specs=VMEM,
        compiler_params=PARAMS,
        cost_estimate=cost(1),
        name="edge_filter",
    )(second, first, part, circle_incr, resp, ahead, back, twiddle)
    incr = lax.all_to_all(incr, ("gu", "gv"), split_axis=0, concat_axis=0, tiled=True)
    return pl.pallas_call(
        functools.partial(final_kernel, split, each),
        out_shape=jax.ShapeDtypeStruct((1, levels, rows, cols), F32),
        in_specs=[VMEM] * 4,
        out_specs=HBM,
        scratch_shapes=[pltpu.VMEM((levels, rows, cols), F32), pltpu.SemaphoreType.DMA((levels,))],
        compiler_params=PARAMS,
        cost_estimate=cost(1),
        name="final_step",
    )(state, incr, diffusion, land_mask)


def solution(mesh):
    shape = mesh.devices.shape
    mesh = jax.sharding.Mesh(mesh.devices.reshape(shape[0], shape[1], shape[2] // 2, 2), ("comp", "gx", "gu", "gv"))
    gy = ("gu", "gv")
    return jax.shard_map(
        local,
        mesh=mesh,
        in_specs=(
            P("comp", None, "gx", gy),
            P("comp", None, None),
            P("comp", "gx", gy),
            P("gx", gy),
            P("comp", "gx", gy, None, None),
            P("comp", "gx", gy, None, None),
            P("comp", "gx", gy, None, None),
            P("comp", "gx", gy, None),
        ),
        out_specs=P("comp", None, "gx", gy),
        check_vma=False,
    )
```

```python
import functools
import math

import jax
import jax.numpy as jnp
import numpy as np
from jax import lax
from jax.experimental import pallas as pl
from jax.experimental.pallas import tpu as pltpu
from jax.sharding import PartitionSpec as P

FC = 4
LANES = 128
BF = jnp.bfloat16
F32 = jnp.float32
VMEM = pl.BlockSpec(memory_space=pltpu.VMEM)
HBM = pl.BlockSpec(memory_space=pltpu.HBM)
LARGE = pltpu.CompilerParams(vmem_limit_bytes=60 * 2**20)
PARAMS = pltpu.CompilerParams(vmem_limit_bytes=32 * 2**20)


def one_hot(rows, index):
    spot = lax.broadcasted_iota(jnp.int16, (rows, index.shape[1]), 0)
    return jnp.where(spot == index.astype(jnp.int16), jnp.asarray(1, BF), jnp.asarray(0, BF))


def split_cell(idx, cols):
    row = (idx.astype(F32) * (1.0 / cols) + 0.5 / cols).astype(jnp.int32)
    return row, idx - row * cols


def split_lines(idx, rows, cols):
    row, col = split_cell(idx, cols)
    tile = col // LANES
    return tile * rows + row, col - tile * LANES


def encode_cell(idx, rows, cols):
    line, lane = split_lines(idx, rows, cols)
    return (lane + LANES).astype(F32) * jnp.exp2((line - 36).astype(F32))


def decode_cell(code):
    top = jnp.floor(jnp.log2(code) + 0.003)
    lane = code * jnp.exp2(-top) * LANES - LANES + 0.5
    return (top + 29.0).astype(jnp.int32), lane.astype(jnp.int32)


def tiles(block):
    return jnp.concatenate([block[:, t : t + LANES] for t in range(0, block.shape[1], LANES)], axis=0)


def untile(block, rows):
    return jnp.concatenate([block[t : t + rows] for t in range(0, block.shape[0], rows)], axis=1)


def pack_kernel(split, state_hbm, dst_hbm, early_ref, state_ref, dst_ref, sems):
    copies = [
        pltpu.make_async_copy(dst_hbm, dst_ref, sems.at[0]),
        pltpu.make_async_copy(state_hbm.at[0, FC:], state_ref, sems.at[1]),
    ]
    for copy in copies:
        copy.start()
    copies[0].wait()
    levels, rows, cols = state_ref.shape
    groups, blocks, slots = dst_ref.shape
    senders, own_rows = split * groups, rows * levels // blocks
    for h in range(blocks):
        code = encode_cell(dst_ref[:, h, :], rows, cols).astype(BF)
        u, other = h // split, h % split
        for v in range(split):
            early_ref[u * split + v, other * groups : (other + 1) * groups, :] = code
    copies[1].wait()
    for z in range(blocks):
        u, v = z // split, z % split
        early_ref[z, senders:, :] = tiles(state_ref[u, v * own_rows : (v + 1) * own_rows, :]).astype(BF)


def gather_kernel(split, blocks, surf_ref, src_ref, all_ref, pick_ref, count_ref, out_ref, weight_ref):
    _, _, rows, cols = surf_ref.shape
    peers, slots = src_ref.shape
    fc = split * out_ref.shape[1] // blocks
    each = fc // split * blocks
    lines = rows * cols // LANES
    half = -(-lines // 16) * 8
    shift = lines - half
    surface = [tiles(surf_ref[0, c]) for c in range(fc)]
    surface = jnp.concatenate([jnp.concatenate([x[:half], x[shift:]], axis=1) for x in surface], axis=0).astype(BF)
    spot = lax.broadcasted_iota(jnp.int32, (half, slots), 0)
    slot = lax.broadcasted_iota(jnp.int32, (peers, slots), 1)
    same = slot == lax.broadcasted_iota(jnp.int32, (peers, slots), 0)
    limit = jnp.sum(jnp.where(same, count_ref[...].astype(F32), 0.0), axis=1, keepdims=True)
    weight_ref[...] = jnp.where(slot.astype(F32) < limit, all_ref[...], 0.0)

    def step(g, carry):
        base = pl.multiple_of(g * blocks, blocks)
        line, col = split_lines(src_ref[pl.ds(base, blocks), :], rows, cols)
        upper = line >= half
        line = line - jnp.where(upper, shift, 0)
        col = col + jnp.where(upper, LANES, 0)
        found = []
        for i in range(0, blocks, 2):
            pick = jnp.concatenate([one_hot(2 * LANES, col[j : j + 1]) for j in (i, i + 1)], axis=1)
            values = jnp.dot(surface, pick, preferred_element_type=F32)
            for j in range(2):
                own = values[:, j * slots : (j + 1) * slots].reshape(fc, half, slots)
                own = jnp.where((spot == line[i + j : i + j + 1])[None], own, 0.0)
                found.append(jnp.sum(own.reshape(fc, half // 8, 8, slots), axis=1).reshape(fc * 8, slots))
        value = jnp.dot(pick_ref[...], jnp.concatenate(found, axis=0).astype(BF), preferred_element_type=F32)
        weight = weight_ref[pl.ds(base, blocks), :]
        value = value * jnp.concatenate([weight] * fc, axis=0)
        for v in range(split):
            out_ref[g * split + v] = value[v * each : (v + 1) * each].astype(BF)
        return carry

    lax.fori_loop(0, peers // blocks, step, 0, unroll=16)


def circle_kernel(scale, early_ref, resp_ref, ahead_ref, back_ref, twiddle_ref, x_ref, incr_ref, line_ref, lane_ref):
    blocks, frame, cols = x_ref.shape
    senders = line_ref.shape[1]
    rows = (early_ref.shape[1] - senders) * LANES // cols
    blank = jnp.zeros((frame - rows, cols), F32)
    x = []
    for h in range(blocks):
        code = early_ref[h].astype(F32)
        line_ref[h], lane_ref[h] = decode_cell(code[:senders])
        x.append(jnp.concatenate([untile(code[senders:], rows), blank], axis=0))
        x_ref[h] = x[h]
    incr = zonal_rows(x, resp_ref[0], resp_ref[1], ahead_ref, back_ref, twiddle_ref)
    for h in range(blocks):
        incr_ref[h] = incr[h] * scale


def scatter_kernel(
    split, arrived_ref, circle_ref, line_ref, lane_ref, state_ref, mate_ref, part_ref, x_ref, first_ref, second_ref, value_ref, acc_ref
):
    senders, each, slots = arrived_ref.shape
    blocks = circle_ref.shape[0]
    fields, _, rows, cols = part_ref.shape
    last = rows * (state_ref.shape[1] - split * fields) // blocks - 1
    groups = senders // split
    lines = rows * cols // LANES
    for s in range(senders):
        value_ref[s] = arrived_ref[s].astype(F32)
    acc_ref[...] = jnp.zeros_like(acc_ref)
    spot = lax.broadcasted_iota(jnp.int32, (lines, slots), 0)

    def step(pair, carry):
        for h in range(blocks):
            spread, pick = [], []
            for g in (2 * pair, 2 * pair + 1):
                for v in range(split):
                    at = v * groups + g
                    mask = spot == line_ref[h, pl.ds(at, 1), :]
                    vals = [
                        jnp.where(mask, value_ref[g * split + v, c * blocks + h : c * blocks + h + 1, :], 0.0)
                        for c in range(fields)
                    ]
                    spread.append(jnp.concatenate(vals, axis=0).astype(BF))
                    pick.append(one_hot(LANES, lane_ref[h, pl.ds(at, 1), :]))
            acc_ref[h] += lax.dot_general(
                jnp.concatenate(spread, axis=1),
                jnp.concatenate(pick, axis=1),
                (((1,), (1,)), ((), ())),
                preferred_element_type=F32,
            )
        return carry

    lax.fori_loop(0, groups // 2, step, 0, unroll=4)
    gv = lax.axis_index("gv")
    own = lax.axis_index("gu") * split + gv
    first_level = gv * fields
    for c in range(fields):
        for h in range(blocks):
            x = untile(acc_ref[h, c * lines : (c + 1) * lines], rows)
            part_ref[c, h] = x
            x_ref[c, h] = x
        x_ref[c, own] += state_ref[0, first_level + c]
        x_ref[c, own + 1 - 2 * gv] += mate_ref[c].astype(F32)
    tops, bottoms = [], []
    for c in range(fields):
        for h in range(blocks):
            tops.append(x_ref[c, h, :1, :])
            bottoms.append(x_ref[c, h, rows - 1 :, :])
    for h in range(blocks):
        tops.append(circle_ref[h, :1, :])
        bottoms.append(circle_ref[h, last : last + 1, :])
    top, bottom = jnp.concatenate(tops, axis=0), jnp.concatenate(bottoms, axis=0)
    odd = lax.axis_index("gx") % 2 == 1
    first_ref[...] = jnp.where(odd, top, bottom).astype(BF)
    second_ref[...] = jnp.where(odd, bottom, top).astype(BF)


def part_kernel(scale, part_ref, x_ref, resp_ref, ahead_ref, back_ref, twiddle_ref, out_ref):
    blocks, fields, rows, cols = out_ref.shape
    xs = [[x_ref[c, h] for h in range(blocks)] for c in range(fields)]
    resps = [(resp_ref[c, 0], resp_ref[c, 1]) for c in range(fields)]
    incrs = zonal_sets(xs, resps, ahead_ref, back_ref, twiddle_ref)
    for c in range(fields):
        for h in range(blocks):
            out_ref[h, c] = (incrs[c][h] * scale + part_ref[c, h]).astype(BF)


def edge_kernel(
    scale, second_ref, first_ref, part_ref, circle_ref, resp_ref, ahead_ref, back_ref, twiddle_ref, out_ref
):
    blocks, fields, rows, cols = part_ref.shape
    sets = fields + 1
    odd = lax.axis_index("gx") % 2 == 1
    first, second = first_ref[...].astype(F32), second_ref[...].astype(F32)
    low, high = jnp.where(odd, first, second), jnp.where(odd, second, first)
    x = []
    blank = jnp.zeros((8 - 2 * sets, cols), F32)
    for h in range(blocks):
        lines = [side[c * blocks + h : c * blocks + h + 1] for c in range(sets) for side in (low, high)]
        x.append(jnp.concatenate(lines + [blank], axis=0))
    zero = jnp.zeros((8 - 2 * sets, resp_ref.shape[3]), F32)
    resp = [
        [
            jnp.concatenate([resp_ref[c, k, r : r + 1, :] for c in range(sets) for _ in range(2)] + [zero], axis=0)
            for r in range(blocks)
        ]
        for k in range(2)
    ]
    incr = zonal_rows(x, resp[0], resp[1], ahead_ref, back_ref, twiddle_ref)
    more = out_ref.shape[1] - fields * rows
    for h in range(blocks):
        for c in range(fields):
            out_ref[h, c * rows : (c + 1) * rows] = part_ref[h, c]
        tail = [circle_ref[h, : more - 2 * sets], (incr[h] * scale + x[h])[: 2 * sets]]
        out_ref[h, fields * rows :] = jnp.concatenate(tail, axis=0).astype(BF)


def final_kernel(split, fields, state_ref, back_ref, rate_ref, land_ref, out_hbm, out_ref, sems):
    _, levels, rows, cols = state_ref.shape
    blocks = back_ref.shape[0]
    coupled = split * fields
    start = fields * rows
    more = rows * (levels - coupled) // blocks
    keep = jnp.where(lax.axis_index("comp") == 1, land_ref[...].astype(F32), 1.0)
    rate = rate_ref[0] * keep
    tail = [back_ref[z, start:].astype(F32) for z in range(blocks)]
    edge = lambda z, k: tail[z][more + k : more + k + 1]
    copies = []
    for c in range(levels):
        own = state_ref[0, c]
        if c < coupled:
            at = c % fields
            zs = [u * split + c // fields for u in range(blocks // split)]
            for z in zs:
                own = own + back_ref[z, at * rows : (at + 1) * rows].astype(F32)
            low = sum(edge(z, 2 * at) for z in zs)
            high = sum(edge(z, 2 * at + 1) for z in zs)
        else:
            zs = [(c - coupled) * split + v for v in range(split)]
            own = own + jnp.concatenate([tail[z][:more] for z in zs], axis=0)
            low, high = edge(zs[-1], 2 * fields), edge(zs[0], 2 * fields + 1)
        above = jnp.concatenate([low, own[: rows - 1]], axis=0)
        below = jnp.concatenate([own[1:], high], axis=0)
        out_ref[c] = own * keep + rate * (above + below - 2.0 * own)
        copies.append(pltpu.make_async_copy(out_ref.at[c], out_hbm.at[0, c], sems.at[c]))
        copies[c].start()
    for copy in copies:
        copy.wait()


def zonal_tables(blocks, cols, waves):
    total = blocks * cols
    b = np.arange(cols)
    n = np.arange(total // 2 // blocks)
    angle = 2.0 * np.pi * ((b[:, None] * n[None, :]) % cols) / cols
    pad = ((0, 0), (0, waves - len(n)))
    cos, sin = np.pad(np.cos(angle), pad), np.pad(np.sin(angle), pad)
    ahead = np.concatenate([cos, sin], axis=1)
    back = np.concatenate([cos.T, sin.T], axis=1)
    turn = 2.0 * np.pi * np.arange(blocks)[:, None] * b[None, :] / total
    twiddle = np.stack([np.cos(turn), np.sin(turn)])
    return jnp.asarray(ahead, BF), jnp.asarray(back, BF), jnp.asarray(twiddle, F32)


def response_row(resp, r):
    return resp[r] if isinstance(resp, list) else resp[r : r + 1, :]


def zonal_ahead(x, twiddle_ref):
    blocks = len(x)
    rows, cols = x[0].shape
    half = math.sqrt(0.5)
    a = [x[i] + x[i + 4] for i in range(4)]
    b = [x[i] - x[i + 4] for i in range(4)]
    b13, d13 = half * (b[1] + b[3]), half * (b[1] - b[3])
    a02, a13 = a[0] + a[2], a[1] + a[3]
    z1 = (b[0] + d13, -(b[2] + b13))
    z2 = (a[0] - a[2], a[3] - a[1])
    z3 = (b[0] - d13, b[2] - b13)
    z = [(a02 + a13, None), z1, z2, z3, (a02 - a13, None)]
    z += [(re, -im) for re, im in (z3, z2, z1)]
    real, imag = [], []
    for r in range(blocks):
        re, im = z[r]
        ct, st = twiddle_ref[0, r : r + 1, :], twiddle_ref[1, r : r + 1, :]
        if r == 0:
            real.append(re)
        elif im is None:
            real.append(re * ct)
            imag.append(-re * st)
        else:
            real.append(re * ct + im * st)
            imag.append(im * ct - re * st)
    return real + imag


def zonal_middle(spec, blocks, rows, resp_cos, resp_sin):
    waves = spec.shape[1] // 2
    cosine, sine = [], []
    for r in range(blocks):
        own = spec[r * rows : (r + 1) * rows]
        c, s = own[:, :waves], own[:, waves:]
        if r > 0:
            other = spec[(blocks + r - 1) * rows : (blocks + r) * rows]
            c, s = c + other[:, waves:], s - other[:, :waves]
        cosine.append(c * response_row(resp_cos, r))
        sine.append(s * response_row(resp_sin, r))
    return cosine + sine


def zonal_back(full, blocks, rows, twiddle_ref):
    cols = full.shape[1] // 2
    half = math.sqrt(0.5)
    u = []
    for r in range(blocks):
        fc = full[r * rows : (r + 1) * rows]
        fs = full[(blocks + r) * rows : (blocks + r + 1) * rows]
        re, im = fc[:, :cols] + fs[:, cols:], fc[:, cols:] - fs[:, :cols]
        ct, st = twiddle_ref[0, r : r + 1, :], twiddle_ref[1, r : r + 1, :]
        u.append((re, None) if r == 0 else (re * ct - im * st, re * st + im * ct))
    even, odd = u[0][0] + u[4][0], u[0][0] - u[4][0]
    p1, q1 = u[1][0] + u[7][0], u[1][1] - u[7][1]
    p2, q2 = u[2][0] + u[6][0], u[2][1] - u[6][1]
    p3, q3 = u[3][0] + u[5][0], u[3][1] - u[5][1]
    m1, n1 = half * (p1 - q1), half * (p1 + q1)
    m3, n3 = half * (p3 - q3), half * (p3 + q3)
    return [
        even + p1 + p2 + p3,
        odd + m1 - q2 - n3,
        even - q1 - p2 + q3,
        odd - n1 + q2 + m3,
        even - p1 + p2 - p3,
        odd - m1 - q2 + n3,
        even + q1 - p2 - q3,
        odd + n1 + q2 - m3,
    ]


def cost(micros):
    return pl.CostEstimate(flops=micros * 10**9, bytes_accessed=micros * 3 * 10**6, transcendentals=0)


def zonal_sets(xs, resps, ahead_ref, back_ref, twiddle_ref):
    blocks = len(xs[0])
    rows = xs[0][0].shape[0]
    lines = [line for x in xs for line in zonal_ahead(x, twiddle_ref)]
    spec = jnp.dot(jnp.concatenate(lines, axis=0).astype(BF), ahead_ref[...], preferred_element_type=F32)
    each = spec.shape[0] // len(xs)
    lines = []
    for at, (resp_cos, resp_sin) in enumerate(resps):
        lines += zonal_middle(spec[at * each : (at + 1) * each], blocks, rows, resp_cos, resp_sin)
    full = jnp.dot(jnp.concatenate(lines, axis=0).astype(BF), back_ref[...], preferred_element_type=F32)
    each = full.shape[0] // len(xs)
    return [zonal_back(full[at * each : (at + 1) * each], blocks, rows, twiddle_ref) for at in range(len(xs))]


def zonal_rows(x, resp_cos, resp_sin, ahead_ref, back_ref, twiddle_ref):
    return zonal_sets([x], [(resp_cos, resp_sin)], ahead_ref, back_ref, twiddle_ref)[0]


def local(
    state, response, diffusion, land_mask, couple_src, couple_dst, couple_weight, couple_count
):
    levels, rows, cols = (state.shape[1], state.shape[2], state.shape[3])
    groups_x, split = lax.axis_size("gx"), lax.axis_size("gv")
    blocks = lax.axis_size("gu") * split
    peers = groups_x * blocks
    slots = couple_src.shape[4]
    cols_all = cols * blocks
    senders = groups_x * split
    each = FC // split
    cell_rows = rows * cols // LANES
    waves = 256
    gv = lax.axis_index("gv")
    src_idx = couple_src.reshape(peers, slots)
    more = rows * (levels - FC) // blocks
    frame = -(-more // 8) * 8

    early = pl.pallas_call(
        functools.partial(pack_kernel, split),
        out_shape=jax.ShapeDtypeStruct((blocks, senders + more * cols // LANES, LANES), BF),
        in_specs=[HBM] * 2,
        out_specs=VMEM,
        scratch_shapes=[
            pltpu.VMEM((levels - FC, rows, cols), F32),
            pltpu.VMEM((groups_x, blocks, slots), jnp.int32),
            pltpu.SemaphoreType.DMA((2,)),
        ],
        compiler_params=LARGE,
        cost_estimate=cost(1),
        name="early_pack",
    )(state, couple_dst.reshape(groups_x, blocks, slots))
    count, early = lax.optimization_barrier((couple_count.reshape(1, peers), early))
    early = lax.all_to_all(early, ("gu", "gv"), split_axis=0, concat_axis=0, tiled=True)

    spot = np.zeros((FC, blocks, blocks, FC, 8), np.float32)
    for c in range(FC):
        for h in range(blocks):
            spot[c, h, h, c] = 1.0
    outgoing = pl.pallas_call(
        functools.partial(gather_kernel, split, blocks),
        out_shape=jax.ShapeDtypeStruct((senders, each * blocks, slots), BF),
        in_specs=[VMEM] * 5,
        out_specs=VMEM,
        scratch_shapes=[pltpu.VMEM((peers, slots), F32)],
        compiler_params=PARAMS,
        cost_estimate=cost(4),
        name="couple_gather",
    )(state, src_idx, couple_weight.reshape(peers, slots), jnp.asarray(spot.reshape(FC * blocks, -1), BF), count)
    crossed = lax.ppermute(outgoing, "comp", [(0, 1), (1, 0)])
    mate = lax.dynamic_slice_in_dim(state[0], (1 - gv) * each, each, 0).astype(BF)
    crossed, early, mate, response = lax.optimization_barrier((crossed, early, mate, response))
    mate = lax.ppermute(mate, "gv", [(0, 1), (1, 0)])
    arrived = lax.all_to_all(crossed, ("gx", "gv"), split_axis=0, concat_axis=0, tiled=True)

    ahead, back, twiddle = zonal_tables(blocks, cols, waves)
    half = cols_all // 2 // blocks
    resp = jnp.concatenate(
        [lax.dynamic_slice_in_dim(response[0], gv * each, each, 0), lax.dynamic_slice_in_dim(response[0], FC + lax.axis_index("gu"), 1, 0)], axis=0
    )
    resp = resp.reshape(each + 1, 2, half, blocks).transpose(0, 1, 3, 2)
    resp = jnp.pad(resp, ((0, 0), (0, 0), (0, 0), (0, waves - half)))
    scale = 2.0 / cols_all

    index = jax.ShapeDtypeStruct((blocks, senders, slots), jnp.int32)
    framed = jax.ShapeDtypeStruct((blocks, frame, cols), F32)
    circle, circle_incr, line, lane = pl.pallas_call(
        functools.partial(circle_kernel, scale),
        out_shape=(framed, framed, index, index),
        in_specs=[VMEM] * 5,
        out_specs=(VMEM,) * 4,
        compiler_params=PARAMS,
        cost_estimate=cost(2),
        name="circle_filter",
    )(early, resp[each], ahead, back, twiddle)
    edge = jax.ShapeDtypeStruct(((each + 1) * blocks, cols), BF)
    part_shape = jax.ShapeDtypeStruct((each, blocks, rows, cols), F32)
    part, x, first, second = pl.pallas_call(
        functools.partial(scatter_kernel, split),
        out_shape=(part_shape, part_shape, edge, edge),
        in_specs=[VMEM] * 6,
        out_specs=(VMEM,) * 4,
        scratch_shapes=[
            pltpu.VMEM((senders, each * blocks, slots), F32),
            pltpu.VMEM((blocks, each * cell_rows, LANES), F32),
        ],
        compiler_params=PARAMS,
        cost_estimate=cost(4),
        name="couple_scatter",
    )(arrived, circle, line, lane, state, mate)
    pairs = [(i, i ^ 1) for i in range(groups_x)]
    cross = [pair for i in range(1, groups_x - 1, 2) for pair in ((i, i + 1), (i + 1, i))]
    second = lax.ppermute(second, "gx", cross)
    first = lax.ppermute(first, "gx", pairs)
    part = pl.pallas_call(
        functools.partial(part_kernel, scale),
        out_shape=jax.ShapeDtypeStruct((blocks, each, rows, cols), BF),
        in_specs=[VMEM] * 6,
        out_specs=VMEM,
        compiler_params=PARAMS,
        cost_estimate=cost(3),
        name="part_filter",
    )(part, x, resp, ahead, back, twiddle)
    incr = pl.pallas_call(
        functools.partial(edge_kernel, scale),
        out_shape=jax.ShapeDtypeStruct((blocks, each * rows + more + 2 * (each + 1), cols), BF),
        in_specs=[VMEM] * 8,
        out_specs=VMEM,
        compiler_params=PARAMS,
        cost_estimate=cost(1),
        name="edge_filter",
    )(second, first, part, circle_incr, resp, ahead, back, twiddle)
    incr = lax.all_to_all(incr, ("gu", "gv"), split_axis=0, concat_axis=0, tiled=True)
    return pl.pallas_call(
        functools.partial(final_kernel, split, each),
        out_shape=jax.ShapeDtypeStruct((1, levels, rows, cols), F32),
        in_specs=[VMEM] * 4,
        out_specs=HBM,
        scratch_shapes=[pltpu.VMEM((levels, rows, cols), F32), pltpu.SemaphoreType.DMA((levels,))],
        compiler_params=PARAMS,
        cost_estimate=cost(1),
        name="final_step",
    )(state, incr, diffusion, land_mask)


def solution(mesh):
    shape = mesh.devices.shape
    mesh = jax.sharding.Mesh(mesh.devices.reshape(shape[0], shape[1], shape[2] // 2, 2), ("comp", "gx", "gu", "gv"))
    gy = ("gu", "gv")
    return jax.shard_map(
        local,
        mesh=mesh,
        in_specs=(
            P("comp", None, "gx", gy),
            P("comp", None, None),
            P("comp", "gx", gy),
            P("gx", gy),
            P("comp", "gx", gy, None, None),
            P("comp", "gx", gy, None, None),
            P("comp", "gx", gy, None, None),
            P("comp", "gx", gy, None),
        ),
        out_specs=P("comp", None, "gx", gy),
        check_vma=False,
    )
```

```python
import functools
import math

import jax
import jax.numpy as jnp
import numpy as np
from jax import lax
from jax.experimental import pallas as pl
from jax.experimental.pallas import tpu as pltpu
from jax.sharding import PartitionSpec as P

FC = 4
LANES = 128
BF = jnp.bfloat16
F32 = jnp.float32
VMEM = pl.BlockSpec(memory_space=pltpu.VMEM)
HBM = pl.BlockSpec(memory_space=pltpu.HBM)
LARGE = pltpu.CompilerParams(vmem_limit_bytes=60 * 2**20)
PARAMS = pltpu.CompilerParams(vmem_limit_bytes=32 * 2**20)


def one_hot(rows, index):
    spot = lax.broadcasted_iota(jnp.int16, (rows, index.shape[1]), 0)
    return jnp.where(spot == index.astype(jnp.int16), jnp.asarray(1, BF), jnp.asarray(0, BF))


def split_cell(idx, cols):
    row = (idx.astype(F32) * (1.0 / cols) + 0.5 / cols).astype(jnp.int32)
    return row, idx - row * cols


def split_lines(idx, rows, cols):
    row, col = split_cell(idx, cols)
    tile = col // LANES
    return tile * rows + row, col - tile * LANES


def encode_cell(idx, rows, cols):
    line, lane = split_lines(idx, rows, cols)
    return (lane + LANES).astype(F32) * jnp.exp2((line - 36).astype(F32))


def decode_cell(code):
    top = jnp.floor(jnp.log2(code) + 0.003)
    lane = code * jnp.exp2(-top) * LANES - LANES + 0.5
    return (top + 29.0).astype(jnp.int32), lane.astype(jnp.int32)


def tiles(block):
    return jnp.concatenate([block[:, t : t + LANES] for t in range(0, block.shape[1], LANES)], axis=0)


def untile(block, rows):
    return jnp.concatenate([block[t : t + rows] for t in range(0, block.shape[0], rows)], axis=1)


def pack_kernel(split, state_hbm, dst_hbm, early_ref, state_ref, dst_ref, sems):
    copies = [
        pltpu.make_async_copy(dst_hbm, dst_ref, sems.at[0]),
        pltpu.make_async_copy(state_hbm.at[0, FC:], state_ref, sems.at[1]),
    ]
    for copy in copies:
        copy.start()
    copies[0].wait()
    levels, rows, cols = state_ref.shape
    groups, blocks, slots = dst_ref.shape
    senders, own_rows = split * groups, rows * levels // blocks
    for h in range(blocks):
        code = encode_cell(dst_ref[:, h, :], rows, cols).astype(BF)
        u, other = h // split, h % split
        for v in range(split):
            early_ref[u * split + v, other * groups : (other + 1) * groups, :] = code
    copies[1].wait()
    for z in range(blocks):
        u, v = z // split, z % split
        early_ref[z, senders:, :] = tiles(state_ref[u, v * own_rows : (v + 1) * own_rows, :]).astype(BF)


def gather_kernel(split, blocks, surf_ref, src_ref, all_ref, pick_ref, count_ref, out_ref, weight_ref):
    _, _, rows, cols = surf_ref.shape
    peers, slots = src_ref.shape
    fc = split * out_ref.shape[1] // blocks
    each = fc // split * blocks
    lines = rows * cols // LANES
    half = -(-lines // 16) * 8
    shift = lines - half
    surface = [tiles(surf_ref[0, c]) for c in range(fc)]
    surface = jnp.concatenate([jnp.concatenate([x[:half], x[shift:]], axis=1) for x in surface], axis=0).astype(BF)
    spot = lax.broadcasted_iota(jnp.int32, (half, slots), 0)
    slot = lax.broadcasted_iota(jnp.int32, (peers, slots), 1)
    same = slot == lax.broadcasted_iota(jnp.int32, (peers, slots), 0)
    limit = jnp.sum(jnp.where(same, count_ref[...].astype(F32), 0.0), axis=1, keepdims=True)
    weight_ref[...] = jnp.where(slot.astype(F32) < limit, all_ref[...], 0.0)

    def step(g, carry):
        base = pl.multiple_of(g * blocks, blocks)
        line, col = split_lines(src_ref[pl.ds(base, blocks), :], rows, cols)
        upper = line >= half
        line = line - jnp.where(upper, shift, 0)
        col = col + jnp.where(upper, LANES, 0)
        found = []
        for i in range(0, blocks, 2):
            pick = jnp.concatenate([one_hot(2 * LANES, col[j : j + 1]) for j in (i, i + 1)], axis=1)
            values = jnp.dot(surface, pick, preferred_element_type=F32)
            for j in range(2):
                own = values[:, j * slots : (j + 1) * slots].reshape(fc, half, slots)
                own = jnp.where((spot == line[i + j : i + j + 1])[None], own, 0.0)
                found.append(jnp.sum(own.reshape(fc, half // 8, 8, slots), axis=1).reshape(fc * 8, slots))
        value = jnp.dot(pick_ref[...], jnp.concatenate(found, axis=0).astype(BF), preferred_element_type=F32)
        weight = weight_ref[pl.ds(base, blocks), :]
        value = value * jnp.concatenate([weight] * fc, axis=0)
        for v in range(split):
            out_ref[g * split + v] = value[v * each : (v + 1) * each].astype(BF)
        return carry

    lax.fori_loop(0, peers // blocks, step, 0, unroll=16)


def circle_kernel(scale, early_ref, resp_ref, ahead_ref, back_ref, twiddle_ref, x_ref, incr_ref, line_ref, lane_ref):
    blocks, frame, cols = x_ref.shape
    senders = line_ref.shape[1]
    rows = (early_ref.shape[1] - senders) * LANES // cols
    blank = jnp.zeros((frame - rows, cols), F32)
    x = []
    for h in range(blocks):
        code = early_ref[h].astype(F32)
        line_ref[h], lane_ref[h] = decode_cell(code[:senders])
        x.append(jnp.concatenate([untile(code[senders:], rows), blank], axis=0))
        x_ref[h] = x[h]
    incr = zonal_rows(x, resp_ref[0], resp_ref[1], ahead_ref, back_ref, twiddle_ref)
    for h in range(blocks):
        incr_ref[h] = incr[h] * scale


def scatter_kernel(
    split, arrived_ref, circle_ref, line_ref, lane_ref, state_ref, mate_ref, part_ref, x_ref, first_ref, second_ref, value_ref
):
    senders, each, slots = arrived_ref.shape
    blocks = circle_ref.shape[0]
    fields, _, rows, cols = part_ref.shape
    last = rows * (state_ref.shape[1] - split * fields) // blocks - 1
    groups = senders // split
    lines = rows * cols // LANES
    for s in range(senders):
        value_ref[s] = arrived_ref[s].astype(F32)
    spot = lax.broadcasted_iota(jnp.int32, (lines, slots), 0)
    for h in range(blocks):
        total = None
        for pair in range(0, groups, 2):
            spread, pick = [], []
            for g in (pair, pair + 1):
                for v in range(split):
                    at = v * groups + g
                    mask = spot == line_ref[h, at : at + 1, :]
                    vals = [
                        jnp.where(mask, value_ref[g * split + v, c * blocks + h : c * blocks + h + 1, :], 0.0)
                        for c in range(fields)
                    ]
                    spread.append(jnp.concatenate(vals, axis=0).astype(BF))
                    pick.append(one_hot(LANES, lane_ref[h, at : at + 1, :]))
            part = lax.dot_general(
                jnp.concatenate(spread, axis=1),
                jnp.concatenate(pick, axis=1),
                (((1,), (1,)), ((), ())),
                preferred_element_type=F32,
            )
            total = part if total is None else total + part
        for c in range(fields):
            x = untile(total[c * lines : (c + 1) * lines], rows)
            part_ref[c, h] = x
            x_ref[c, h] = x
    gv = lax.axis_index("gv")
    own = lax.axis_index("gu") * split + gv
    first_level = gv * fields
    for c in range(fields):
        x_ref[c, own] += state_ref[0, first_level + c]
        x_ref[c, own + 1 - 2 * gv] += mate_ref[c].astype(F32)
    tops, bottoms = [], []
    for c in range(fields):
        for h in range(blocks):
            tops.append(x_ref[c, h, :1, :])
            bottoms.append(x_ref[c, h, rows - 1 :, :])
    for h in range(blocks):
        tops.append(circle_ref[h, :1, :])
        bottoms.append(circle_ref[h, last : last + 1, :])
    top, bottom = jnp.concatenate(tops, axis=0), jnp.concatenate(bottoms, axis=0)
    odd = lax.axis_index("gx") % 2 == 1
    first_ref[...] = jnp.where(odd, top, bottom).astype(BF)
    second_ref[...] = jnp.where(odd, bottom, top).astype(BF)


def part_kernel(scale, part_ref, x_ref, resp_ref, ahead_ref, back_ref, twiddle_ref, out_ref):
    blocks, fields, rows, cols = out_ref.shape
    xs = [[x_ref[c, h] for h in range(blocks)] for c in range(fields)]
    resps = [(resp_ref[c, 0], resp_ref[c, 1]) for c in range(fields)]
    incrs = zonal_sets(xs, resps, ahead_ref, back_ref, twiddle_ref)
    for c in range(fields):
        for h in range(blocks):
            out_ref[h, c] = (incrs[c][h] * scale + part_ref[c, h]).astype(BF)


def edge_kernel(
    scale, second_ref, first_ref, part_ref, circle_ref, resp_ref, ahead_ref, back_ref, twiddle_ref, out_ref
):
    blocks, fields, rows, cols = part_ref.shape
    sets = fields + 1
    odd = lax.axis_index("gx") % 2 == 1
    first, second = first_ref[...].astype(F32), second_ref[...].astype(F32)
    low, high = jnp.where(odd, first, second), jnp.where(odd, second, first)
    x = []
    blank = jnp.zeros((8 - 2 * sets, cols), F32)
    for h in range(blocks):
        lines = [side[c * blocks + h : c * blocks + h + 1] for c in range(sets) for side in (low, high)]
        x.append(jnp.concatenate(lines + [blank], axis=0))
    zero = jnp.zeros((8 - 2 * sets, resp_ref.shape[3]), F32)
    resp = [
        [
            jnp.concatenate([resp_ref[c, k, r : r + 1, :] for c in range(sets) for _ in range(2)] + [zero], axis=0)
            for r in range(blocks)
        ]
        for k in range(2)
    ]
    incr = zonal_rows(x, resp[0], resp[1], ahead_ref, back_ref, twiddle_ref)
    more = out_ref.shape[1] - fields * rows
    for h in range(blocks):
        for c in range(fields):
            out_ref[h, c * rows : (c + 1) * rows] = part_ref[h, c]
        tail = [circle_ref[h, : more - 2 * sets], (incr[h] * scale + x[h])[: 2 * sets]]
        out_ref[h, fields * rows :] = jnp.concatenate(tail, axis=0).astype(BF)


def final_kernel(split, fields, state_ref, back_ref, rate_ref, land_ref, out_hbm, out_ref, sems):
    _, levels, rows, cols = state_ref.shape
    blocks = back_ref.shape[0]
    coupled = split * fields
    start = fields * rows
    more = rows * (levels - coupled) // blocks
    keep = jnp.where(lax.axis_index("comp") == 1, land_ref[...].astype(F32), 1.0)
    rate = rate_ref[0] * keep
    tail = [back_ref[z, start:].astype(F32) for z in range(blocks)]
    edge = lambda z, k: tail[z][more + k : more + k + 1]
    copies = []
    for c in range(levels):
        own = state_ref[0, c]
        if c < coupled:
            at = c % fields
            zs = [u * split + c // fields for u in range(blocks // split)]
            for z in zs:
                own = own + back_ref[z, at * rows : (at + 1) * rows].astype(F32)
            low = sum(edge(z, 2 * at) for z in zs)
            high = sum(edge(z, 2 * at + 1) for z in zs)
        else:
            zs = [(c - coupled) * split + v for v in range(split)]
            own = own + jnp.concatenate([tail[z][:more] for z in zs], axis=0)
            low, high = edge(zs[-1], 2 * fields), edge(zs[0], 2 * fields + 1)
        above = jnp.concatenate([low, own[: rows - 1]], axis=0)
        below = jnp.concatenate([own[1:], high], axis=0)
        out_ref[c] = own * keep + rate * (above + below - 2.0 * own)
        copies.append(pltpu.make_async_copy(out_ref.at[c], out_hbm.at[0, c], sems.at[c]))
        copies[c].start()
    for copy in copies:
        copy.wait()


def zonal_tables(blocks, cols, waves):
    total = blocks * cols
    b = np.arange(cols)
    n = np.arange(total // 2 // blocks)
    angle = 2.0 * np.pi * ((b[:, None] * n[None, :]) % cols) / cols
    pad = ((0, 0), (0, waves - len(n)))
    cos, sin = np.pad(np.cos(angle), pad), np.pad(np.sin(angle), pad)
    ahead = np.concatenate([cos, sin], axis=1)
    back = np.concatenate([cos.T, sin.T], axis=1)
    turn = 2.0 * np.pi * np.arange(blocks)[:, None] * b[None, :] / total
    twiddle = np.stack([np.cos(turn), np.sin(turn)])
    return jnp.asarray(ahead, BF), jnp.asarray(back, BF), jnp.asarray(twiddle, F32)


def response_row(resp, r):
    return resp[r] if isinstance(resp, list) else resp[r : r + 1, :]


def zonal_ahead(x, twiddle_ref):
    blocks = len(x)
    rows, cols = x[0].shape
    half = math.sqrt(0.5)
    a = [x[i] + x[i + 4] for i in range(4)]
    b = [x[i] - x[i + 4] for i in range(4)]
    b13, d13 = half * (b[1] + b[3]), half * (b[1] - b[3])
    a02, a13 = a[0] + a[2], a[1] + a[3]
    z1 = (b[0] + d13, -(b[2] + b13))
    z2 = (a[0] - a[2], a[3] - a[1])
    z3 = (b[0] - d13, b[2] - b13)
    z = [(a02 + a13, None), z1, z2, z3, (a02 - a13, None)]
    z += [(re, -im) for re, im in (z3, z2, z1)]
    real, imag = [], []
    for r in range(blocks):
        re, im = z[r]
        ct, st = twiddle_ref[0, r : r + 1, :], twiddle_ref[1, r : r + 1, :]
        if r == 0:
            real.append(re)
        elif im is None:
            real.append(re * ct)
            imag.append(-re * st)
        else:
            real.append(re * ct + im * st)
            imag.append(im * ct - re * st)
    return real + imag


def zonal_middle(spec, blocks, rows, resp_cos, resp_sin):
    waves = spec.shape[1] // 2
    cosine, sine = [], []
    for r in range(blocks):
        own = spec[r * rows : (r + 1) * rows]
        c, s = own[:, :waves], own[:, waves:]
        if r > 0:
            other = spec[(blocks + r - 1) * rows : (blocks + r) * rows]
            c, s = c + other[:, waves:], s - other[:, :waves]
        cosine.append(c * response_row(resp_cos, r))
        sine.append(s * response_row(resp_sin, r))
    return cosine + sine


def zonal_back(full, blocks, rows, twiddle_ref):
    cols = full.shape[1] // 2
    half = math.sqrt(0.5)
    u = []
    for r in range(blocks):
        fc = full[r * rows : (r + 1) * rows]
        fs = full[(blocks + r) * rows : (blocks + r + 1) * rows]
        re, im = fc[:, :cols] + fs[:, cols:], fc[:, cols:] - fs[:, :cols]
        ct, st = twiddle_ref[0, r : r + 1, :], twiddle_ref[1, r : r + 1, :]
        u.append((re, None) if r == 0 else (re * ct - im * st, re * st + im * ct))
    even, odd = u[0][0] + u[4][0], u[0][0] - u[4][0]
    p1, q1 = u[1][0] + u[7][0], u[1][1] - u[7][1]
    p2, q2 = u[2][0] + u[6][0], u[2][1] - u[6][1]
    p3, q3 = u[3][0] + u[5][0], u[3][1] - u[5][1]
    m1, n1 = half * (p1 - q1), half * (p1 + q1)
    m3, n3 = half * (p3 - q3), half * (p3 + q3)
    return [
        even + p1 + p2 + p3,
        odd + m1 - q2 - n3,
        even - q1 - p2 + q3,
        odd - n1 + q2 + m3,
        even - p1 + p2 - p3,
        odd - m1 - q2 + n3,
        even + q1 - p2 - q3,
        odd + n1 + q2 - m3,
    ]


def cost(micros):
    return pl.CostEstimate(flops=micros * 10**9, bytes_accessed=micros * 3 * 10**6, transcendentals=0)


def zonal_sets(xs, resps, ahead_ref, back_ref, twiddle_ref):
    blocks = len(xs[0])
    rows = xs[0][0].shape[0]
    lines = [line for x in xs for line in zonal_ahead(x, twiddle_ref)]
    spec = jnp.dot(jnp.concatenate(lines, axis=0).astype(BF), ahead_ref[...], preferred_element_type=F32)
    each = spec.shape[0] // len(xs)
    lines = []
    for at, (resp_cos, resp_sin) in enumerate(resps):
        lines += zonal_middle(spec[at * each : (at + 1) * each], blocks, rows, resp_cos, resp_sin)
    full = jnp.dot(jnp.concatenate(lines, axis=0).astype(BF), back_ref[...], preferred_element_type=F32)
    each = full.shape[0] // len(xs)
    return [zonal_back(full[at * each : (at + 1) * each], blocks, rows, twiddle_ref) for at in range(len(xs))]


def zonal_rows(x, resp_cos, resp_sin, ahead_ref, back_ref, twiddle_ref):
    return zonal_sets([x], [(resp_cos, resp_sin)], ahead_ref, back_ref, twiddle_ref)[0]


def local(
    state, response, diffusion, land_mask, couple_src, couple_dst, couple_weight, couple_count
):
    levels, rows, cols = (state.shape[1], state.shape[2], state.shape[3])
    groups_x, split = lax.axis_size("gx"), lax.axis_size("gv")
    blocks = lax.axis_size("gu") * split
    peers = groups_x * blocks
    slots = couple_src.shape[4]
    cols_all = cols * blocks
    senders = groups_x * split
    each = FC // split
    cell_rows = rows * cols // LANES
    waves = 256
    gv = lax.axis_index("gv")
    src_idx = couple_src.reshape(peers, slots)
    more = rows * (levels - FC) // blocks
    frame = -(-more // 8) * 8

    early = pl.pallas_call(
        functools.partial(pack_kernel, split),
        out_shape=jax.ShapeDtypeStruct((blocks, senders + more * cols // LANES, LANES), BF),
        in_specs=[HBM] * 2,
        out_specs=VMEM,
        scratch_shapes=[
            pltpu.VMEM((levels - FC, rows, cols), F32),
            pltpu.VMEM((groups_x, blocks, slots), jnp.int32),
            pltpu.SemaphoreType.DMA((2,)),
        ],
        compiler_params=LARGE,
        cost_estimate=cost(1),
        name="early_pack",
    )(state, couple_dst.reshape(groups_x, blocks, slots))
    count, early = lax.optimization_barrier((couple_count.reshape(1, peers), early))
    early = lax.all_to_all(early, ("gu", "gv"), split_axis=0, concat_axis=0, tiled=True)

    spot = np.zeros((FC, blocks, blocks, FC, 8), np.float32)
    for c in range(FC):
        for h in range(blocks):
            spot[c, h, h, c] = 1.0
    outgoing = pl.pallas_call(
        functools.partial(gather_kernel, split, blocks),
        out_shape=jax.ShapeDtypeStruct((senders, each * blocks, slots), BF),
        in_specs=[VMEM] * 5,
        out_specs=VMEM,
        scratch_shapes=[pltpu.VMEM((peers, slots), F32)],
        compiler_params=PARAMS,
        cost_estimate=cost(4),
        name="couple_gather",
    )(state, src_idx, couple_weight.reshape(peers, slots), jnp.asarray(spot.reshape(FC * blocks, -1), BF), count)
    crossed = lax.ppermute(outgoing, "comp", [(0, 1), (1, 0)])
    mate = lax.dynamic_slice_in_dim(state[0], (1 - gv) * each, each, 0).astype(BF)
    crossed, early, mate, response = lax.optimization_barrier((crossed, early, mate, response))
    mate = lax.ppermute(mate, "gv", [(0, 1), (1, 0)])
    arrived = lax.all_to_all(crossed, ("gx", "gv"), split_axis=0, concat_axis=0, tiled=True)

    ahead, back, twiddle = zonal_tables(blocks, cols, waves)
    half = cols_all // 2 // blocks
    resp = jnp.concatenate(
        [lax.dynamic_slice_in_dim(response[0], gv * each, each, 0), lax.dynamic_slice_in_dim(response[0], FC + lax.axis_index("gu"), 1, 0)], axis=0
    )
    resp = resp.reshape(each + 1, 2, half, blocks).transpose(0, 1, 3, 2)
    resp = jnp.pad(resp, ((0, 0), (0, 0), (0, 0), (0, waves - half)))
    scale = 2.0 / cols_all

    index = jax.ShapeDtypeStruct((blocks, senders, slots), jnp.int32)
    framed = jax.ShapeDtypeStruct((blocks, frame, cols), F32)
    circle, circle_incr, line, lane = pl.pallas_call(
        functools.partial(circle_kernel, scale),
        out_shape=(framed, framed, index, index),
        in_specs=[VMEM] * 5,
        out_specs=(VMEM,) * 4,
        compiler_params=PARAMS,
        cost_estimate=cost(2),
        name="circle_filter",
    )(early, resp[each], ahead, back, twiddle)
    edge = jax.ShapeDtypeStruct(((each + 1) * blocks, cols), BF)
    part_shape = jax.ShapeDtypeStruct((each, blocks, rows, cols), F32)
    part, x, first, second = pl.pallas_call(
        functools.partial(scatter_kernel, split),
        out_shape=(part_shape, part_shape, edge, edge),
        in_specs=[VMEM] * 6,
        out_specs=(VMEM,) * 4,
        scratch_shapes=[
            pltpu.VMEM((senders, each * blocks, slots), F32),
        ],
        compiler_params=PARAMS,
        cost_estimate=cost(4),
        name="couple_scatter",
    )(arrived, circle, line, lane, state, mate)
    pairs = [(i, i ^ 1) for i in range(groups_x)]
    cross = [pair for i in range(1, groups_x - 1, 2) for pair in ((i, i + 1), (i + 1, i))]
    second = lax.ppermute(second, "gx", cross)
    first = lax.ppermute(first, "gx", pairs)
    part = pl.pallas_call(
        functools.partial(part_kernel, scale),
        out_shape=jax.ShapeDtypeStruct((blocks, each, rows, cols), BF),
        in_specs=[VMEM] * 6,
        out_specs=VMEM,
        compiler_params=PARAMS,
        cost_estimate=cost(3),
        name="part_filter",
    )(part, x, resp, ahead, back, twiddle)
    incr = pl.pallas_call(
        functools.partial(edge_kernel, scale),
        out_shape=jax.ShapeDtypeStruct((blocks, each * rows + more + 2 * (each + 1), cols), BF),
        in_specs=[VMEM] * 8,
        out_specs=VMEM,
        compiler_params=PARAMS,
        cost_estimate=cost(1),
        name="edge_filter",
    )(second, first, part, circle_incr, resp, ahead, back, twiddle)
    incr = lax.all_to_all(incr, ("gu", "gv"), split_axis=0, concat_axis=0, tiled=True)
    return pl.pallas_call(
        functools.partial(final_kernel, split, each),
        out_shape=jax.ShapeDtypeStruct((1, levels, rows, cols), F32),
        in_specs=[VMEM] * 4,
        out_specs=HBM,
        scratch_shapes=[pltpu.VMEM((levels, rows, cols), F32), pltpu.SemaphoreType.DMA((levels,))],
        compiler_params=PARAMS,
        cost_estimate=cost(1),
        name="final_step",
    )(state, incr, diffusion, land_mask)


def solution(mesh):
    shape = mesh.devices.shape
    mesh = jax.sharding.Mesh(mesh.devices.reshape(shape[0], shape[1], shape[2] // 2, 2), ("comp", "gx", "gu", "gv"))
    gy = ("gu", "gv")
    return jax.shard_map(
        local,
        mesh=mesh,
        in_specs=(
            P("comp", None, "gx", gy),
            P("comp", None, None),
            P("comp", "gx", gy),
            P("gx", gy),
            P("comp", "gx", gy, None, None),
            P("comp", "gx", gy, None, None),
            P("comp", "gx", gy, None, None),
            P("comp", "gx", gy, None),
        ),
        out_specs=P("comp", None, "gx", gy),
        check_vma=False,
    )
```

```python
import functools
import math

import jax
import jax.numpy as jnp
import numpy as np
from jax import lax
from jax.experimental import pallas as pl
from jax.experimental.pallas import tpu as pltpu
from jax.sharding import PartitionSpec as P

FC = 4
LANES = 128
BF = jnp.bfloat16
F32 = jnp.float32
VMEM = pl.BlockSpec(memory_space=pltpu.VMEM)
HBM = pl.BlockSpec(memory_space=pltpu.HBM)
LARGE = pltpu.CompilerParams(vmem_limit_bytes=60 * 2**20)
PARAMS = pltpu.CompilerParams(vmem_limit_bytes=32 * 2**20)


def one_hot(rows, index):
    spot = lax.broadcasted_iota(jnp.int16, (rows, index.shape[1]), 0)
    return jnp.where(spot == index.astype(jnp.int16), jnp.asarray(1, BF), jnp.asarray(0, BF))


def split_cell(idx, cols):
    row = (idx.astype(F32) * (1.0 / cols) + 0.5 / cols).astype(jnp.int32)
    return row, idx - row * cols


def split_lines(idx, rows, cols):
    row, col = split_cell(idx, cols)
    tile = col // LANES
    return tile * rows + row, col - tile * LANES


def encode_cell(idx, rows, cols):
    line, lane = split_lines(idx, rows, cols)
    return (lane + LANES).astype(F32) * jnp.exp2((line - 36).astype(F32))


def decode_cell(code):
    top = jnp.floor(jnp.log2(code) + 0.003)
    lane = code * jnp.exp2(-top) * LANES - LANES + 0.5
    return (top + 29.0).astype(jnp.int32), lane.astype(jnp.int32)


def tiles(block):
    return jnp.concatenate([block[:, t : t + LANES] for t in range(0, block.shape[1], LANES)], axis=0)


def untile(block, rows):
    return jnp.concatenate([block[t : t + rows] for t in range(0, block.shape[0], rows)], axis=1)


def pack_kernel(split, state_hbm, dst_hbm, early_ref, state_ref, dst_ref, sems):
    copies = [
        pltpu.make_async_copy(dst_hbm, dst_ref, sems.at[0]),
        pltpu.make_async_copy(state_hbm.at[0, FC:], state_ref, sems.at[1]),
    ]
    for copy in copies:
        copy.start()
    copies[0].wait()
    levels, rows, cols = state_ref.shape
    groups, blocks, slots = dst_ref.shape
    senders, own_rows = split * groups, rows * levels // blocks
    for h in range(blocks):
        code = encode_cell(dst_ref[:, h, :], rows, cols).astype(BF)
        u, other = h // split, h % split
        for v in range(split):
            early_ref[u * split + v, other * groups : (other + 1) * groups, :] = code
    copies[1].wait()
    for z in range(blocks):
        u, v = z // split, z % split
        early_ref[z, senders:, :] = tiles(state_ref[u, v * own_rows : (v + 1) * own_rows, :]).astype(BF)


def gather_kernel(split, blocks, surf_ref, src_ref, all_ref, pick_ref, count_ref, out_ref, weight_ref):
    _, _, rows, cols = surf_ref.shape
    peers, slots = src_ref.shape
    fc = split * out_ref.shape[1] // blocks
    each = fc // split * blocks
    lines = rows * cols // LANES
    half = -(-lines // 16) * 8
    shift = lines - half
    surface = [tiles(surf_ref[0, c]) for c in range(fc)]
    surface = jnp.concatenate([jnp.concatenate([x[:half], x[shift:]], axis=1) for x in surface], axis=0).astype(BF)
    spot = lax.broadcasted_iota(jnp.int32, (half, slots), 0)
    slot = lax.broadcasted_iota(jnp.int32, (peers, slots), 1)
    same = slot == lax.broadcasted_iota(jnp.int32, (peers, slots), 0)
    limit = jnp.sum(jnp.where(same, count_ref[...].astype(F32), 0.0), axis=1, keepdims=True)
    weight_ref[...] = jnp.where(slot.astype(F32) < limit, all_ref[...], 0.0)

    lines_all, cols_all = split_lines(src_ref[...], rows, cols)
    upper = lines_all >= half
    lines_all = lines_all - jnp.where(upper, shift, 0)
    cols_all = cols_all + jnp.where(upper, LANES, 0)
    for g in range(peers // blocks):
        base = g * blocks
        line, col = lines_all[base : base + blocks], cols_all[base : base + blocks]
        found = []
        for i in range(0, blocks, 2):
            pick = jnp.concatenate([one_hot(2 * LANES, col[j : j + 1]) for j in (i, i + 1)], axis=1)
            values = jnp.dot(surface, pick, preferred_element_type=F32)
            for j in range(2):
                own = values[:, j * slots : (j + 1) * slots].reshape(fc, half, slots)
                own = jnp.where((spot == line[i + j : i + j + 1])[None], own, 0.0)
                found.append(jnp.sum(own.reshape(fc, half // 8, 8, slots), axis=1).reshape(fc * 8, slots))
        value = jnp.dot(pick_ref[...], jnp.concatenate(found, axis=0).astype(BF), preferred_element_type=F32)
        weight = weight_ref[base : base + blocks, :]
        value = value * jnp.concatenate([weight] * fc, axis=0)
        for v in range(split):
            out_ref[g * split + v] = value[v * each : (v + 1) * each].astype(BF)


def circle_kernel(scale, early_ref, resp_ref, ahead_ref, back_ref, twiddle_ref, x_ref, incr_ref, line_ref, lane_ref):
    blocks, frame, cols = x_ref.shape
    senders = line_ref.shape[1]
    rows = (early_ref.shape[1] - senders) * LANES // cols
    blank = jnp.zeros((frame - rows, cols), F32)
    x = []
    for h in range(blocks):
        code = early_ref[h].astype(F32)
        line_ref[h], lane_ref[h] = decode_cell(code[:senders])
        x.append(jnp.concatenate([untile(code[senders:], rows), blank], axis=0))
        x_ref[h] = x[h]
    incr = zonal_rows(x, resp_ref[0], resp_ref[1], ahead_ref, back_ref, twiddle_ref)
    for h in range(blocks):
        incr_ref[h] = incr[h] * scale


def scatter_kernel(
    split, arrived_ref, circle_ref, line_ref, lane_ref, state_ref, mate_ref, part_ref, x_ref, first_ref, second_ref, value_ref
):
    senders, each, slots = arrived_ref.shape
    blocks = circle_ref.shape[0]
    fields, _, rows, cols = part_ref.shape
    last = rows * (state_ref.shape[1] - split * fields) // blocks - 1
    groups = senders // split
    lines = rows * cols // LANES
    for s in range(senders):
        value_ref[s] = arrived_ref[s].astype(F32)
    spot = lax.broadcasted_iota(jnp.int32, (lines, slots), 0)
    for h in range(blocks):
        total = None
        for four in range(0, groups, 4):
            spread, pick = [], []
            for g in range(four, four + 4):
                for v in range(split):
                    at = v * groups + g
                    mask = spot == line_ref[h, at : at + 1, :]
                    vals = [
                        jnp.where(mask, value_ref[g * split + v, c * blocks + h : c * blocks + h + 1, :], 0.0)
                        for c in range(fields)
                    ]
                    spread.append(jnp.concatenate(vals, axis=0).astype(BF))
                    pick.append(one_hot(LANES, lane_ref[h, at : at + 1, :]))
            part = lax.dot_general(
                jnp.concatenate(spread, axis=1),
                jnp.concatenate(pick, axis=1),
                (((1,), (1,)), ((), ())),
                preferred_element_type=F32,
            )
            total = part if total is None else total + part
        for c in range(fields):
            x = untile(total[c * lines : (c + 1) * lines], rows)
            part_ref[c, h] = x
            x_ref[c, h] = x
    gv = lax.axis_index("gv")
    own = lax.axis_index("gu") * split + gv
    first_level = gv * fields
    for c in range(fields):
        x_ref[c, own] += state_ref[0, first_level + c]
        x_ref[c, own + 1 - 2 * gv] += mate_ref[c].astype(F32)
    tops, bottoms = [], []
    for c in range(fields):
        for h in range(blocks):
            tops.append(x_ref[c, h, :1, :])
            bottoms.append(x_ref[c, h, rows - 1 :, :])
    for h in range(blocks):
        tops.append(circle_ref[h, :1, :])
        bottoms.append(circle_ref[h, last : last + 1, :])
    top, bottom = jnp.concatenate(tops, axis=0), jnp.concatenate(bottoms, axis=0)
    odd = lax.axis_index("gx") % 2 == 1
    first_ref[...] = jnp.where(odd, top, bottom).astype(BF)
    second_ref[...] = jnp.where(odd, bottom, top).astype(BF)


def part_kernel(scale, part_ref, x_ref, resp_ref, ahead_ref, back_ref, twiddle_ref, out_ref):
    blocks, fields, rows, cols = out_ref.shape
    xs = [[x_ref[c, h] for h in range(blocks)] for c in range(fields)]
    resps = [(resp_ref[c, 0], resp_ref[c, 1]) for c in range(fields)]
    incrs = zonal_sets(xs, resps, ahead_ref, back_ref, twiddle_ref)
    for c in range(fields):
        for h in range(blocks):
            out_ref[h, c] = (incrs[c][h] * scale + part_ref[c, h]).astype(BF)


def edge_kernel(
    scale, second_ref, first_ref, part_ref, circle_ref, resp_ref, ahead_ref, back_ref, twiddle_ref, out_ref
):
    blocks, fields, rows, cols = part_ref.shape
    sets = fields + 1
    odd = lax.axis_index("gx") % 2 == 1
    first, second = first_ref[...].astype(F32), second_ref[...].astype(F32)
    low, high = jnp.where(odd, first, second), jnp.where(odd, second, first)
    x = []
    blank = jnp.zeros((8 - 2 * sets, cols), F32)
    for h in range(blocks):
        lines = [side[c * blocks + h : c * blocks + h + 1] for c in range(sets) for side in (low, high)]
        x.append(jnp.concatenate(lines + [blank], axis=0))
    zero = jnp.zeros((8 - 2 * sets, resp_ref.shape[3]), F32)
    resp = [
        [
            jnp.concatenate([resp_ref[c, k, r : r + 1, :] for c in range(sets) for _ in range(2)] + [zero], axis=0)
            for r in range(blocks)
        ]
        for k in range(2)
    ]
    incr = zonal_rows(x, resp[0], resp[1], ahead_ref, back_ref, twiddle_ref)
    more = out_ref.shape[1] - fields * rows
    for h in range(blocks):
        for c in range(fields):
            out_ref[h, c * rows : (c + 1) * rows] = part_ref[h, c]
        tail = [circle_ref[h, : more - 2 * sets], (incr[h] * scale + x[h])[: 2 * sets]]
        out_ref[h, fields * rows :] = jnp.concatenate(tail, axis=0).astype(BF)


def final_kernel(split, fields, state_ref, back_ref, rate_ref, land_ref, out_hbm, out_ref, sems):
    _, levels, rows, cols = state_ref.shape
    blocks = back_ref.shape[0]
    coupled = split * fields
    start = fields * rows
    more = rows * (levels - coupled) // blocks
    keep = jnp.where(lax.axis_index("comp") == 1, land_ref[...].astype(F32), 1.0)
    rate = rate_ref[0] * keep
    tail = [back_ref[z, start:].astype(F32) for z in range(blocks)]
    edge = lambda z, k: tail[z][more + k : more + k + 1]
    copies = []
    for c in range(levels):
        own = state_ref[0, c]
        if c < coupled:
            at = c % fields
            zs = [u * split + c // fields for u in range(blocks // split)]
            for z in zs:
                own = own + back_ref[z, at * rows : (at + 1) * rows].astype(F32)
            low = sum(edge(z, 2 * at) for z in zs)
            high = sum(edge(z, 2 * at + 1) for z in zs)
        else:
            zs = [(c - coupled) * split + v for v in range(split)]
            own = own + jnp.concatenate([tail[z][:more] for z in zs], axis=0)
            low, high = edge(zs[-1], 2 * fields), edge(zs[0], 2 * fields + 1)
        above = jnp.concatenate([low, own[: rows - 1]], axis=0)
        below = jnp.concatenate([own[1:], high], axis=0)
        out_ref[c] = own * keep + rate * (above + below - 2.0 * own)
        copies.append(pltpu.make_async_copy(out_ref.at[c], out_hbm.at[0, c], sems.at[c]))
        copies[c].start()
    for copy in copies:
        copy.wait()


def zonal_tables(blocks, cols, waves):
    total = blocks * cols
    b = np.arange(cols)
    n = np.arange(total // 2 // blocks)
    angle = 2.0 * np.pi * ((b[:, None] * n[None, :]) % cols) / cols
    pad = ((0, 0), (0, waves - len(n)))
    cos, sin = np.pad(np.cos(angle), pad), np.pad(np.sin(angle), pad)
    ahead = np.concatenate([cos, sin], axis=1)
    back = np.concatenate([cos.T, sin.T], axis=1)
    turn = 2.0 * np.pi * np.arange(blocks)[:, None] * b[None, :] / total
    twiddle = np.stack([np.cos(turn), np.sin(turn)])
    return jnp.asarray(ahead, BF), jnp.asarray(back, BF), jnp.asarray(twiddle, F32)


def response_row(resp, r):
    return resp[r] if isinstance(resp, list) else resp[r : r + 1, :]


def zonal_ahead(x, twiddle_ref):
    blocks = len(x)
    rows, cols = x[0].shape
    half = math.sqrt(0.5)
    a = [x[i] + x[i + 4] for i in range(4)]
    b = [x[i] - x[i + 4] for i in range(4)]
    b13, d13 = half * (b[1] + b[3]), half * (b[1] - b[3])
    a02, a13 = a[0] + a[2], a[1] + a[3]
    z1 = (b[0] + d13, -(b[2] + b13))
    z2 = (a[0] - a[2], a[3] - a[1])
    z3 = (b[0] - d13, b[2] - b13)
    z = [(a02 + a13, None), z1, z2, z3, (a02 - a13, None)]
    z += [(re, -im) for re, im in (z3, z2, z1)]
    real, imag = [], []
    for r in range(blocks):
        re, im = z[r]
        ct, st = twiddle_ref[0, r : r + 1, :], twiddle_ref[1, r : r + 1, :]
        if r == 0:
            real.append(re)
        elif im is None:
            real.append(re * ct)
            imag.append(-re * st)
        else:
            real.append(re * ct + im * st)
            imag.append(im * ct - re * st)
    return real + imag


def zonal_middle(spec, blocks, rows, resp_cos, resp_sin):
    waves = spec.shape[1] // 2
    cosine, sine = [], []
    for r in range(blocks):
        own = spec[r * rows : (r + 1) * rows]
        c, s = own[:, :waves], own[:, waves:]
        if r > 0:
            other = spec[(blocks + r - 1) * rows : (blocks + r) * rows]
            c, s = c + other[:, waves:], s - other[:, :waves]
        cosine.append(c * response_row(resp_cos, r))
        sine.append(s * response_row(resp_sin, r))
    return cosine + sine


def zonal_back(full, blocks, rows, twiddle_ref):
    cols = full.shape[1] // 2
    half = math.sqrt(0.5)
    u = []
    for r in range(blocks):
        fc = full[r * rows : (r + 1) * rows]
        fs = full[(blocks + r) * rows : (blocks + r + 1) * rows]
        re, im = fc[:, :cols] + fs[:, cols:], fc[:, cols:] - fs[:, :cols]
        ct, st = twiddle_ref[0, r : r + 1, :], twiddle_ref[1, r : r + 1, :]
        u.append((re, None) if r == 0 else (re * ct - im * st, re * st + im * ct))
    even, odd = u[0][0] + u[4][0], u[0][0] - u[4][0]
    p1, q1 = u[1][0] + u[7][0], u[1][1] - u[7][1]
    p2, q2 = u[2][0] + u[6][0], u[2][1] - u[6][1]
    p3, q3 = u[3][0] + u[5][0], u[3][1] - u[5][1]
    m1, n1 = half * (p1 - q1), half * (p1 + q1)
    m3, n3 = half * (p3 - q3), half * (p3 + q3)
    return [
        even + p1 + p2 + p3,
        odd + m1 - q2 - n3,
        even - q1 - p2 + q3,
        odd - n1 + q2 + m3,
        even - p1 + p2 - p3,
        odd - m1 - q2 + n3,
        even + q1 - p2 - q3,
        odd + n1 + q2 - m3,
    ]


def cost(micros):
    return pl.CostEstimate(flops=micros * 10**9, bytes_accessed=micros * 3 * 10**6, transcendentals=0)


def zonal_sets(xs, resps, ahead_ref, back_ref, twiddle_ref):
    blocks = len(xs[0])
    rows = xs[0][0].shape[0]
    lines = [line for x in xs for line in zonal_ahead(x, twiddle_ref)]
    spec = jnp.dot(jnp.concatenate(lines, axis=0).astype(BF), ahead_ref[...], preferred_element_type=F32)
    each = spec.shape[0] // len(xs)
    lines = []
    for at, (resp_cos, resp_sin) in enumerate(resps):
        lines += zonal_middle(spec[at * each : (at + 1) * each], blocks, rows, resp_cos, resp_sin)
    full = jnp.dot(jnp.concatenate(lines, axis=0).astype(BF), back_ref[...], preferred_element_type=F32)
    each = full.shape[0] // len(xs)
    return [zonal_back(full[at * each : (at + 1) * each], blocks, rows, twiddle_ref) for at in range(len(xs))]


def zonal_rows(x, resp_cos, resp_sin, ahead_ref, back_ref, twiddle_ref):
    return zonal_sets([x], [(resp_cos, resp_sin)], ahead_ref, back_ref, twiddle_ref)[0]


def local(
    state, response, diffusion, land_mask, couple_src, couple_dst, couple_weight, couple_count
):
    levels, rows, cols = (state.shape[1], state.shape[2], state.shape[3])
    groups_x, split = lax.axis_size("gx"), lax.axis_size("gv")
    blocks = lax.axis_size("gu") * split
    peers = groups_x * blocks
    slots = couple_src.shape[4]
    cols_all = cols * blocks
    senders = groups_x * split
    each = FC // split
    cell_rows = rows * cols // LANES
    waves = 256
    gv = lax.axis_index("gv")
    src_idx = couple_src.reshape(peers, slots)
    more = rows * (levels - FC) // blocks
    frame = -(-more // 8) * 8

    early = pl.pallas_call(
        functools.partial(pack_kernel, split),
        out_shape=jax.ShapeDtypeStruct((blocks, senders + more * cols // LANES, LANES), BF),
        in_specs=[HBM] * 2,
        out_specs=VMEM,
        scratch_shapes=[
            pltpu.VMEM((levels - FC, rows, cols), F32),
            pltpu.VMEM((groups_x, blocks, slots), jnp.int32),
            pltpu.SemaphoreType.DMA((2,)),
        ],
        compiler_params=LARGE,
        cost_estimate=cost(1),
        name="early_pack",
    )(state, couple_dst.reshape(groups_x, blocks, slots))
    count, early = lax.optimization_barrier((couple_count.reshape(1, peers), early))
    early = lax.all_to_all(early, ("gu", "gv"), split_axis=0, concat_axis=0, tiled=True)

    spot = np.zeros((FC, blocks, blocks, FC, 8), np.float32)
    for c in range(FC):
        for h in range(blocks):
            spot[c, h, h, c] = 1.0
    outgoing = pl.pallas_call(
        functools.partial(gather_kernel, split, blocks),
        out_shape=jax.ShapeDtypeStruct((senders, each * blocks, slots), BF),
        in_specs=[VMEM] * 5,
        out_specs=VMEM,
        scratch_shapes=[pltpu.VMEM((peers, slots), F32)],
        compiler_params=PARAMS,
        cost_estimate=cost(4),
        name="couple_gather",
    )(state, src_idx, couple_weight.reshape(peers, slots), jnp.asarray(spot.reshape(FC * blocks, -1), BF), count)
    crossed = lax.ppermute(outgoing, "comp", [(0, 1), (1, 0)])
    mate = lax.dynamic_slice_in_dim(state[0], (1 - gv) * each, each, 0).astype(BF)
    crossed, early, mate, response = lax.optimization_barrier((crossed, early, mate, response))
    mate = lax.ppermute(mate, "gv", [(0, 1), (1, 0)])
    arrived = lax.all_to_all(crossed, ("gx", "gv"), split_axis=0, concat_axis=0, tiled=True)

    ahead, back, twiddle = zonal_tables(blocks, cols, waves)
    half = cols_all // 2 // blocks
    resp = jnp.concatenate(
        [lax.dynamic_slice_in_dim(response[0], gv * each, each, 0), lax.dynamic_slice_in_dim(response[0], FC + lax.axis_index("gu"), 1, 0)], axis=0
    )
    resp = resp.reshape(each + 1, 2, half, blocks).transpose(0, 1, 3, 2)
    resp = jnp.pad(resp, ((0, 0), (0, 0), (0, 0), (0, waves - half)))
    scale = 2.0 / cols_all

    index = jax.ShapeDtypeStruct((blocks, senders, slots), jnp.int32)
    framed = jax.ShapeDtypeStruct((blocks, frame, cols), F32)
    circle, circle_incr, line, lane = pl.pallas_call(
        functools.partial(circle_kernel, scale),
        out_shape=(framed, framed, index, index),
        in_specs=[VMEM] * 5,
        out_specs=(VMEM,) * 4,
        compiler_params=PARAMS,
        cost_estimate=cost(2),
        name="circle_filter",
    )(early, resp[each], ahead, back, twiddle)
    edge = jax.ShapeDtypeStruct(((each + 1) * blocks, cols), BF)
    part_shape = jax.ShapeDtypeStruct((each, blocks, rows, cols), F32)
    part, x, first, second = pl.pallas_call(
        functools.partial(scatter_kernel, split),
        out_shape=(part_shape, part_shape, edge, edge),
        in_specs=[VMEM] * 6,
        out_specs=(VMEM,) * 4,
        scratch_shapes=[
            pltpu.VMEM((senders, each * blocks, slots), F32),
        ],
        compiler_params=PARAMS,
        cost_estimate=cost(4),
        name="couple_scatter",
    )(arrived, circle, line, lane, state, mate)
    pairs = [(i, i ^ 1) for i in range(groups_x)]
    cross = [pair for i in range(1, groups_x - 1, 2) for pair in ((i, i + 1), (i + 1, i))]
    second = lax.ppermute(second, "gx", cross)
    first = lax.ppermute(first, "gx", pairs)
    part = pl.pallas_call(
        functools.partial(part_kernel, scale),
        out_shape=jax.ShapeDtypeStruct((blocks, each, rows, cols), BF),
        in_specs=[VMEM] * 6,
        out_specs=VMEM,
        compiler_params=PARAMS,
        cost_estimate=cost(3),
        name="part_filter",
    )(part, x, resp, ahead, back, twiddle)
    incr = pl.pallas_call(
        functools.partial(edge_kernel, scale),
        out_shape=jax.ShapeDtypeStruct((blocks, each * rows + more + 2 * (each + 1), cols), BF),
        in_specs=[VMEM] * 8,
        out_specs=VMEM,
        compiler_params=PARAMS,
        cost_estimate=cost(1),
        name="edge_filter",
    )(second, first, part, circle_incr, resp, ahead, back, twiddle)
    incr = lax.all_to_all(incr, ("gu", "gv"), split_axis=0, concat_axis=0, tiled=True)
    return pl.pallas_call(
        functools.partial(final_kernel, split, each),
        out_shape=jax.ShapeDtypeStruct((1, levels, rows, cols), F32),
        in_specs=[VMEM] * 4,
        out_specs=HBM,
        scratch_shapes=[pltpu.VMEM((levels, rows, cols), F32), pltpu.SemaphoreType.DMA((levels,))],
        compiler_params=PARAMS,
        cost_estimate=cost(1),
        name="final_step",
    )(state, incr, diffusion, land_mask)


def solution(mesh):
    shape = mesh.devices.shape
    mesh = jax.sharding.Mesh(mesh.devices.reshape(shape[0], shape[1], shape[2] // 2, 2), ("comp", "gx", "gu", "gv"))
    gy = ("gu", "gv")
    return jax.shard_map(
        local,
        mesh=mesh,
        in_specs=(
            P("comp", None, "gx", gy),
            P("comp", None, None),
            P("comp", "gx", gy),
            P("gx", gy),
            P("comp", "gx", gy, None, None),
            P("comp", "gx", gy, None, None),
            P("comp", "gx", gy, None, None),
            P("comp", "gx", gy, None),
        ),
        out_specs=P("comp", None, "gx", gy),
        check_vma=False,
    )
```
